256 devices in a mesh: dp: 32 (over y, x, z_hi), ctx: 8 (over z_lo, core).
Axes of the slice: x: 4, y: 4, z: 8 (z_hi: 2, z_lo: 4; z = z_hi * 4 + z_lo), core: 2. Of those that a mesh axis runs over, the one named last changes fastest.
Arguments:
- queries: bfloat16 [32, 1024, 2048], P('dp', 'ctx'), may hold values from -9 to 9
- keys: bfloat16 [32, 1024, 256], P('dp', 'ctx'), may hold values from -9 to 9
- values: bfloat16 [32, 1024, 256], P('dp', 'ctx'), may hold values from -6 to 6
- out_grad: bfloat16 [32, 1024, 2048], P('dp', 'ctx'), may hold values from -6 to 6
- layer_input: bfloat16 [32, 1024, 8192], P('dp', 'ctx'), may hold values from -6 to 6
- segment_ids: int32 [32, 1024], P('dp'), may hold values from 0 to 7, never falling along the last dimension, each value on 1 to 512 neighbouring positions
Outputs:
- query_grad: bfloat16 [32, 1024, 2048], P('dp', 'ctx')
- kv_weight_grad: float32 [8192, 512], P(('dp', 'ctx'))
The draws below stay inside these ranges and needn't reach their ends.
Inputs may be any that keep to these rules, and one draw needn't show every extreme that they name: `segment_ids`: never falls along a sequence; each document holds 1 to 512 positions and one holds exactly 512.
All inputs are finite; a program needn't handle non-finite values.
Results may differ from the reference program's by a relative error of at most 0.01.
The reference program's roundings to bfloat16 on the way (of `pb`, `ds` and `kv_grad`) count: a program that leaves them out, or rounds other values in their place, can miss the bound.
Values may be sent and summed in bfloat16 or wider, within the bound.
No kernel may reach another device: no remote copies, remote signals or barrier semaphores. Data moves between devices by JAX's collectives and lax.ppermute only.
A program may use at most 128 MiB of HBM per device.

```python
import math
import jax
import jax.numpy as jnp
import numpy as np
from jax import lax

D = 8192
H = 16
KV = 2
DH = 128
DOCS = 8
L = 1024
SEQS = 32


def aligned_runs(key, top, gap):
    span = min(64, L)
    spans = L // span
    offsets = jax.random.randint(jax.random.fold_in(key, 41), (SEQS, spans), 0, span - 3)
    flips = jax.random.bernoulli(jax.random.fold_in(key, 42), 0.5, (SEQS, spans, KV, DH))
    signs = jnp.where(flips, 1.0, -1.0).astype(jnp.float32)
    which_span = jnp.arange(L) // span
    inside = jnp.arange(L) % span
    place = inside[None, :] - jnp.take(offsets, which_span, axis=1)
    levels = jnp.array([0.4, 0.6667, 1.0], jnp.float32)
    strength = top * jnp.take(levels, which_span % 3)
    amplitude = jnp.sqrt(strength / math.sqrt(DH))
    sign_rows = jnp.take(signs, which_span, axis=1)
    factor = amplitude[None, :] * (1.0 - (gap / strength)[None, :] * (3 - place).astype(jnp.float32))
    in_run = (place >= 0) & (place <= 3)
    at_end = place == 3
    key_rows = factor[:, :, None, None] * sign_rows
    query_rows = amplitude[None, :, None, None] * sign_rows
    return (in_run, at_end, key_rows, query_rows)


def draw_queries(key, part):
    own_key = jax.random.fold_in(key, 1)
    in_run, at_end, key_rows, query_rows = aligned_runs(key, 4.0, 0.3)
    base = jax.random.truncated_normal(own_key, -6.0, 6.0, (SEQS, L, KV, H // KV, DH), jnp.float32)
    mixed = jnp.where(at_end[:, :, None, None, None], query_rows[:, :, :, None, :], base)
    return mixed.reshape(SEQS, L, H * DH).astype(jnp.bfloat16)


def draw_keys(key, part):
    own_key = jax.random.fold_in(key, 2)
    in_run, at_end, key_rows, query_rows = aligned_runs(key, 4.0, 0.3)
    base = jax.random.truncated_normal(own_key, -6.0, 6.0, (SEQS, L, KV, DH), jnp.float32)
    mixed = jnp.where(in_run[:, :, None, None], key_rows, base)
    return mixed.reshape(SEQS, L, KV * DH).astype(jnp.bfloat16)


def level_of(rng, shape, shards, low, largest):
    gain, own = 1.0, jax.random.fold_in(rng, 6)
    for position, shards_of in shards:
        draws = jnp.exp(jax.random.uniform(jax.random.fold_in(own, position), (shards_of,), jnp.float32, low / len(shards), largest / len(shards)))
        gain = gain * jnp.repeat(draws, shape[position] // shards_of).reshape([-1 if axis == position else 1 for axis in range(len(shape))])
    return gain


def profile(count, total, bound, skew):
    loads = [(1 << 20) // math.isqrt(standing ** skew) + 1 for standing in range(2, count + 1)]
    spare, holding = total - bound - (count - 1), [1] * (count - 1)
    while spare > 0:
        free = [i for i in range(count - 1) if holding[i] < bound]
        mass, remaining = sum([loads[i] for i in free]), spare
        for i in free:
            addition = min(bound - holding[i], max(1, remaining * loads[i] // mass), spare)
            holding[i] = holding[i] + addition
            spare = spare - addition
    return np.array([bound] + holding)


def ragged(rng, number_of, total, most, lean):
    if number_of == 2:
        one = jax.random.randint(rng, (), max(1, total - most), min(most, total - 1) + 1)
        return jnp.stack([one, total - one])
    tallies = jnp.asarray(profile(number_of, total, most, lean), jnp.int32)
    twos = (number_of - 1) // 2
    source_of, taker = tallies[1:1 + 2 * twos:2], tallies[2:2 + 2 * twos:2]
    margin = jnp.minimum(source_of - 1, most - taker)
    moved = jax.random.randint(jax.random.fold_in(rng, 1), (twos,), 0, 1 << 20) % (margin + 1)
    tallies = tallies.at[1:1 + 2 * twos:2].set(source_of - moved).at[2:2 + 2 * twos:2].set(taker + moved)
    return tallies[jax.random.permutation(jax.random.fold_in(rng, 2), number_of)]


def scatter_about(key, shape, deviation, most, cuts=(), kind=jnp.bfloat16):
    result = deviation * jax.random.normal(key, shape, jnp.float32)
    if cuts:
        result = result * level_of(key, shape, cuts, -0.22, 0.18)
    return jnp.clip(result, -most, most).astype(kind)


def setup_inputs(seed: int = 0) -> dict:
    arg_keys = jax.random.split(jax.random.key(seed), 7)
    queries = draw_queries(jax.random.fold_in(arg_keys[6], 71), 0)
    keys = draw_keys(jax.random.fold_in(arg_keys[6], 71), 0)
    values = scatter_about(arg_keys[2], (SEQS, L, KV * DH), 1.0, 6.0, ((0, 32), (1, 8)))
    out_grad = scatter_about(arg_keys[3], (SEQS, L, H * DH), 1.0, 6.0, ((0, 32), (1, 8)))
    layer_input = scatter_about(arg_keys[4], (SEQS, L, D), 1.0, 6.0, ((0, 32), (1, 8)))
    segment_ids = jax.vmap(lambda own: jnp.searchsorted(jnp.cumsum(ragged(own, DOCS, L, L // 2, 2)), jnp.arange(L), side="right"))(jax.random.split(arg_keys[5], SEQS)).reshape((SEQS, L)).astype(jnp.int32)
    return {"queries": queries, "keys": keys, "values": values, "out_grad": out_grad, "layer_input": layer_input, "segment_ids": segment_ids}


def head_terms(q_h, k_g, v_g, do_h, allowed, scale):
    s = jnp.dot(q_h, k_g.T, preferred_element_type=jnp.float32) * scale
    s = jnp.where(allowed, s, -jnp.inf)
    top = jnp.max(s, axis=1, keepdims=True)
    e = jnp.exp(s - top)
    p = e / jnp.sum(e, axis=1, keepdims=True)
    pb = p.astype(jnp.bfloat16)
    o = jnp.dot(pb, v_g, preferred_element_type=jnp.float32)
    delta = jnp.sum(do_h.astype(jnp.float32) * o, axis=1, keepdims=True)
    dpr = jnp.dot(do_h, v_g.T, preferred_element_type=jnp.float32)
    ds = (p * (dpr - delta) * scale).astype(jnp.bfloat16)
    dq = jnp.dot(ds, k_g, preferred_element_type=jnp.float32)
    dk = jnp.dot(ds.T, q_h, preferred_element_type=jnp.float32)
    dv = jnp.dot(pb.T, do_h, preferred_element_type=jnp.float32)
    return dq, dk, dv


def sequence_grads(q_s, k_s, v_s, do_s, seg_s):
    rows = q_s.shape[0]
    scale = 1.0 / (DH ** 0.5)
    qpos = jnp.arange(rows, dtype=jnp.int32)
    allowed = (qpos[None, :] <= qpos[:, None]) & (seg_s[:, None] == seg_s[None, :])
    per_group = H // KV
    q_heads = q_s.reshape(rows, H, DH).transpose(1, 0, 2)
    do_heads = do_s.reshape(rows, H, DH).transpose(1, 0, 2)
    dq_list, dk_list, dv_list = [], [], []
    for group in range(KV):
        k_g = k_s[:, group * DH:(group + 1) * DH]
        v_g = v_s[:, group * DH:(group + 1) * DH]

        def one_head(carry, pair):
            dq, dk, dv = head_terms(pair[0], k_g, v_g, pair[1], allowed, scale)
            return (carry[0] + dk, carry[1] + dv), dq.astype(jnp.bfloat16)

        zeros = jnp.zeros((rows, DH), jnp.float32)
        sl = slice(group * per_group, (group + 1) * per_group)
        (dk, dv), dqs = lax.scan(one_head, (zeros, zeros), (q_heads[sl], do_heads[sl]))
        dq_list.append(dqs)
        dk_list.append(dk)
        dv_list.append(dv)
    dq_all = jnp.concatenate(dq_list, axis=0).transpose(1, 0, 2).reshape(rows, H * DH)
    kv_grad = jnp.concatenate(dk_list + dv_list, axis=1).astype(jnp.bfloat16)
    return dq_all, kv_grad


def reference(queries, keys, values, out_grad, layer_input, segment_ids):
    def per_sequence(total, items):
        q_s, k_s, v_s, do_s, x_s, seg_s = items
        dq, kv_grad = sequence_grads(q_s, k_s, v_s, do_s, seg_s)
        total = total + jnp.dot(x_s.T, kv_grad, preferred_element_type=jnp.float32)
        return total, dq

    start = jnp.zeros((D, 2 * KV * DH), jnp.float32)
    weight_grad, query_grad = lax.scan(per_sequence, start, (queries, keys, values, out_grad, layer_input, segment_ids))
    return query_grad, weight_grad
```

```python
import jax
import jax.numpy as jnp
from jax import lax
from jax.experimental import pallas as pl
from jax.experimental.pallas import tpu as pltpu
from jax.sharding import Mesh, PartitionSpec as P

H = 16
KV = 2
DH = 128
GROUP = H // KV
SCALE = 1.0 / DH**0.5
LOG2E = 1.4426950408889634
REACH = 2
MASKED = -1e30


def dot_nt(left, right):
    return lax.dot_general(
        left, right, (((1,), (1,)), ((), ())), preferred_element_type=jnp.float32
    )


def dot_nn(left, right):
    return jnp.dot(left, right, preferred_element_type=jnp.float32)


def attention_kernel(
    q_mine, do_mine, qdo_other, k0, k1, k2, k3, k4, k5, bias,
    dq_mine, dq_other, own_grad, near_grad, far_grad, dk_acc, dv_acc,
):
    pairs = jnp.concatenate([ref[...] for ref in (k0, k1, k2, k3, k4, k5)], axis=0)
    key, value = pairs[:, :DH], pairs[:, DH:]
    key_t = key.T
    rows = q_mine.shape[0]
    for head in range(GROUP):
        cols = slice(head * DH, (head + 1) * DH)
        grad_cols = slice((GROUP + head) * DH, (GROUP + head + 1) * DH)
        query = jnp.concatenate([q_mine[:, cols], qdo_other[:, cols]], axis=0)
        grad = jnp.concatenate([do_mine[:, cols], qdo_other[:, grad_cols]], axis=0)
        score = dot_nt(key, query) * (SCALE * LOG2E) + bias[...]
        top = jnp.max(score, axis=0, keepdims=True)
        weight = jnp.exp2(score - top)
        inverse = 1.0 / jnp.sum(weight, axis=0, keepdims=True)
        prob = weight * inverse
        prob_half = prob.astype(jnp.bfloat16)
        prob_grad = dot_nt(value, grad)
        delta = jnp.sum(prob_half.astype(jnp.float32) * prob_grad, axis=0, keepdims=True)
        score_grad = (prob * (prob_grad - delta) * SCALE).astype(jnp.bfloat16)
        dq = dot_nn(key_t, score_grad).T.astype(jnp.bfloat16)
        dq_mine[:, cols] = dq[:rows]
        dq_other[:, cols] = dq[rows:]
        dk = dot_nn(score_grad, query)
        dv = dot_nn(prob_half, grad)
        if head == 0:
            dk_acc[...] = dk
            dv_acc[...] = dv
        else:
            dk_acc[...] += dk
            dv_acc[...] += dv
    chip = 2 * rows
    own_grad[:, :DH] = dk_acc[:chip]
    own_grad[:, DH:] = dv_acc[:chip]
    near_grad[:, :DH] = dk_acc[chip : 2 * chip].astype(jnp.bfloat16)
    near_grad[:, DH:] = dv_acc[chip : 2 * chip].astype(jnp.bfloat16)
    far_grad[:, :DH] = dk_acc[2 * chip :].astype(jnp.bfloat16)
    far_grad[:, DH:] = dv_acc[2 * chip :].astype(jnp.bfloat16)


def attention(q_mine, do_mine, qdo_other, blocks, bias):
    rows = q_mine.shape[0]
    chip = 2 * rows
    keys = chip * (REACH + 1)
    half = jnp.bfloat16
    return pl.pallas_call(
        attention_kernel,
        out_shape=(
            jax.ShapeDtypeStruct((rows, GROUP * DH), half),
            jax.ShapeDtypeStruct((rows, GROUP * DH), half),
            jax.ShapeDtypeStruct((chip, 2 * DH), jnp.float32),
            jax.ShapeDtypeStruct((chip, 2 * DH), half),
            jax.ShapeDtypeStruct((chip, 2 * DH), half),
        ),
        scratch_shapes=[
            pltpu.VMEM((keys, DH), jnp.float32),
            pltpu.VMEM((keys, DH), jnp.float32),
        ],
        compiler_params=pltpu.CompilerParams(vmem_limit_bytes=32 * 1024 * 1024),
        cost_estimate=pl.CostEstimate(
            flops=10 * keys * chip * DH * GROUP,
            bytes_accessed=4 * 1024 * 1024,
            transcendentals=keys * chip * GROUP,
        ),
    )(q_mine, do_mine, qdo_other, *blocks, bias)


def per_device(queries, keys, values, out_grad, layer_input, segment_ids):
    rows = queries.shape[1]
    chip = 2 * rows
    z_lo = lax.axis_index("z_lo")
    core = lax.axis_index("core")
    n_chips = lax.axis_size("z_lo")
    n_plane = lax.axis_size("y") * lax.axis_size("x")

    def half_of(array, which):
        width = array.shape[-1] // 2
        return lax.dynamic_slice_in_dim(array[0], which * width, width, 1)

    swap = [(0, 1), (1, 0)]

    pair_mine = jnp.concatenate([half_of(keys, core), half_of(values, core)], axis=1)
    pair_other = jnp.concatenate([half_of(keys, 1 - core), half_of(values, 1 - core)], axis=1)

    def behind(distance, flip):
        return [
            (chip_at * 2 + c, (chip_at + distance) * 2 + (c ^ flip))
            for chip_at in range(n_chips - distance)
            for c in range(2)
        ]

    blocks = [pair_mine, lax.ppermute(pair_other, "core", swap)]
    for distance in range(1, REACH + 1):
        blocks.append(lax.ppermute(pair_mine, ("z_lo", "core"), behind(distance, 0)))
        blocks.append(lax.ppermute(pair_other, ("z_lo", "core"), behind(distance, 1)))
    q_mine, do_mine = half_of(queries, core), half_of(out_grad, core)
    qdo_other = lax.ppermute(
        jnp.concatenate([half_of(queries, 1 - core), half_of(out_grad, 1 - core)], axis=1),
        "core",
        swap,
    )

    n_z = lax.axis_size("z_hi") * n_chips
    depth = layer_input.shape[2] // n_plane
    columns = layer_input[0].reshape(rows, n_plane, depth).transpose(1, 0, 2)
    columns_mine = lax.all_to_all(columns, ("y", "x"), 0, 0, tiled=True)
    columns_other = lax.ppermute(columns_mine, "core", swap)
    columns_all = jnp.concatenate([columns_mine, columns_other], axis=1).reshape(
        n_plane * chip, depth
    )

    seg_row = segment_ids[0]
    lane = jnp.arange(rows, dtype=jnp.int32)

    def places(chip_at, which):
        start = chip_at * chip + which * rows
        return (start + lane, lax.dynamic_slice_in_dim(seg_row, jnp.maximum(start, 0), rows, 0))

    key_places = [
        places(z_lo - distance, which)
        for distance in range(REACH + 1)
        for which in (core, 1 - core)
    ]
    key_pos = jnp.concatenate([place[0] for place in key_places])[:, None]
    key_doc = jnp.concatenate([place[1] for place in key_places])[:, None]
    query_pos = jnp.concatenate([place[0] for place in key_places[:2]])[None, :]
    query_doc = jnp.concatenate([place[1] for place in key_places[:2]])[None, :]
    allowed = (key_pos >= 0) & (key_pos <= query_pos) & (key_doc == query_doc)
    bias = jnp.where(allowed, 0.0, MASKED).astype(jnp.float32)

    dq_mine, dq_other, pair_grad, near_grad, far_grad = attention(
        q_mine, do_mine, qdo_other, blocks, bias
    )
    dq_back = lax.ppermute(dq_other, "core", swap)
    query_grad = jnp.where(
        core == 0,
        jnp.concatenate([dq_mine, dq_back], axis=1),
        jnp.concatenate([dq_back, dq_mine], axis=1),
    )[None]

    for distance, part in ((1, near_grad), (2, far_grad)):
        back = [(b, a) for a, b in behind(distance, 0)]
        pair_grad = pair_grad + lax.ppermute(part, ("z_lo", "core"), back).astype(jnp.float32)
    pair_grad = pair_grad.astype(jnp.bfloat16)

    gathered = lax.all_to_all(
        jnp.broadcast_to(pair_grad, (n_plane, chip, 2 * DH)), ("y", "x"), 0, 0, tiled=True
    ).reshape(n_plane * chip, 2 * DH)
    term = lax.dot_general(
        columns_all, gathered, (((0,), (0,)), ((), ())), preferred_element_type=jnp.float32
    ).astype(jnp.bfloat16)
    spread = lax.all_to_all(
        term.reshape(n_z * 2, depth // (n_z * 2), 2 * DH), ("z_hi", "z_lo", "core"), 0, 0, tiled=True
    )
    by_head = jnp.sum(spread.reshape(n_z, 2, depth // (n_z * 2), 2 * DH).astype(jnp.float32), axis=0)
    weight_grad = jnp.concatenate(
        [by_head[0, :, :DH], by_head[1, :, :DH], by_head[0, :, DH:], by_head[1, :, DH:]], axis=1
    )
    return (query_grad, weight_grad)


def solution(mesh):
    axes = ("y", "x", "z_hi", "z_lo", "core")
    fine = Mesh(mesh.devices.reshape(4, 4, 2, 4, 2), axes)
    dp, ctx = axes[:3], axes[3:]
    return jax.shard_map(
        per_device,
        mesh=fine,
        in_specs=(P(dp, ctx, None),) * 5 + (P(dp, None),),
        out_specs=(P(dp, ctx, None), P(axes, None)),
        check_vma=False,
    )
```

```python
import jax
import jax.numpy as jnp
from jax import lax
from jax.experimental import pallas as pl
from jax.experimental.pallas import tpu as pltpu
from jax.sharding import Mesh, PartitionSpec as P

H = 16
KV = 2
DH = 128
GROUP = H // KV
SCALE = 1.0 / DH**0.5
LOG2E = 1.4426950408889634
REACH = 2
MASKED = -1e30


def dot_nt(left, right):
    return lax.dot_general(
        left, right, (((1,), (1,)), ((), ())), preferred_element_type=jnp.float32
    )


def dot_nn(left, right):
    return jnp.dot(left, right, preferred_element_type=jnp.float32)


def attention_kernel(
    q_mine, do_mine, qdo_other, k0, k1, k2, k3, k4, k5, bias,
    dq_mine, dq_other, own_grad, near_grad, far_grad, dk_acc, dv_acc,
):
    pairs = jnp.concatenate([ref[...] for ref in (k0, k1, k2, k3, k4, k5)], axis=0)
    key, value = pairs[:, :DH], pairs[:, DH:]
    key_t = key.T
    rows = q_mine.shape[0]
    for head in range(GROUP):
        cols = slice(head * DH, (head + 1) * DH)
        grad_cols = slice((GROUP + head) * DH, (GROUP + head + 1) * DH)
        query = jnp.concatenate([q_mine[:, cols], qdo_other[:, cols]], axis=0)
        grad = jnp.concatenate([do_mine[:, cols], qdo_other[:, grad_cols]], axis=0)
        score = dot_nt(key, query) * (SCALE * LOG2E) + bias[...]
        top = jnp.max(score, axis=0, keepdims=True)
        weight = jnp.exp2(score - top)
        inverse = 1.0 / jnp.sum(weight, axis=0, keepdims=True)
        prob = weight * inverse
        prob_half = prob.astype(jnp.bfloat16)
        prob_grad = dot_nt(value, grad)
        delta = jnp.sum(prob_half.astype(jnp.float32) * prob_grad, axis=0, keepdims=True)
        score_grad = (prob * (prob_grad - delta) * SCALE).astype(jnp.bfloat16)
        dq = dot_nn(key_t, score_grad).T.astype(jnp.bfloat16)
        dq_mine[:, cols] = dq[:rows]
        dq_other[:, cols] = dq[rows:]
        dk = dot_nn(score_grad, query)
        dv = dot_nn(prob_half, grad)
        if head == 0:
            dk_acc[...] = dk
            dv_acc[...] = dv
        else:
            dk_acc[...] += dk
            dv_acc[...] += dv
    chip = 2 * rows
    own_grad[:, :DH] = dk_acc[:chip]
    own_grad[:, DH:] = dv_acc[:chip]
    near_grad[:, :DH] = dk_acc[chip : 2 * chip].astype(jnp.bfloat16)
    near_grad[:, DH:] = dv_acc[chip : 2 * chip].astype(jnp.bfloat16)
    far_grad[:, :DH] = dk_acc[2 * chip :].astype(jnp.bfloat16)
    far_grad[:, DH:] = dv_acc[2 * chip :].astype(jnp.bfloat16)


def attention(q_mine, do_mine, qdo_other, blocks, bias):
    rows = q_mine.shape[0]
    chip = 2 * rows
    keys = chip * (REACH + 1)
    half = jnp.bfloat16
    return pl.pallas_call(
        attention_kernel,
        out_shape=(
            jax.ShapeDtypeStruct((rows, GROUP * DH), half),
            jax.ShapeDtypeStruct((rows, GROUP * DH), half),
            jax.ShapeDtypeStruct((chip, 2 * DH), jnp.float32),
            jax.ShapeDtypeStruct((chip, 2 * DH), half),
            jax.ShapeDtypeStruct((chip, 2 * DH), half),
        ),
        scratch_shapes=[
            pltpu.VMEM((keys, DH), jnp.float32),
            pltpu.VMEM((keys, DH), jnp.float32),
        ],
        compiler_params=pltpu.CompilerParams(vmem_limit_bytes=32 * 1024 * 1024),
        cost_estimate=pl.CostEstimate(
            flops=10 * keys * chip * DH * GROUP,
            bytes_accessed=4 * 1024 * 1024,
            transcendentals=keys * chip * GROUP,
        ),
    )(q_mine, do_mine, qdo_other, *blocks, bias)


def project_kernel(mine, other, grads, out):
    total = None
    for place in range(mine.shape[0]):
        block = jnp.concatenate([mine[place], other[place]], axis=1)
        part = dot_nn(block, grads[place])
        total = part if total is None else total + part
    out[...] = total.astype(jnp.bfloat16)


def project(mine, other, grads, blocks):
    places, columns, rows = mine.shape
    width = grads.shape[2]
    step = columns // blocks
    return pl.pallas_call(
        project_kernel,
        out_shape=jax.ShapeDtypeStruct((columns, width), jnp.bfloat16),
        grid=(blocks,),
        in_specs=[
            pl.BlockSpec((places, step, rows), lambda i: (0, i, 0)),
            pl.BlockSpec((places, step, rows), lambda i: (0, i, 0)),
            pl.BlockSpec(grads.shape, lambda i: (0, 0, 0)),
        ],
        out_specs=pl.BlockSpec((step, width), lambda i: (i, 0)),
        compiler_params=pltpu.CompilerParams(vmem_limit_bytes=32 * 1024 * 1024),
        cost_estimate=pl.CostEstimate(
            flops=4 * places * rows * columns * width, bytes_accessed=6 * 1024 * 1024, transcendentals=0
        ),
    )(mine, other, grads)


def final_kernel(parts, out):
    n_z = parts.shape[0] // 2
    for head in range(KV):
        total = parts[head].astype(jnp.float32)
        for z in range(1, n_z):
            total = total + parts[2 * z + head].astype(jnp.float32)
        out[:, head * DH : (head + 1) * DH] = total[:, :DH]
        out[:, (KV + head) * DH : (KV + head + 1) * DH] = total[:, DH:]


def final_sum(parts):
    return pl.pallas_call(
        final_kernel,
        out_shape=jax.ShapeDtypeStruct((parts.shape[1], 2 * KV * DH), jnp.float32),
        cost_estimate=pl.CostEstimate(flops=0, bytes_accessed=512 * 1024, transcendentals=0),
    )(parts)


def per_device(queries, keys, values, out_grad, layer_input, segment_ids):
    rows = queries.shape[1]
    chip = 2 * rows
    z_lo = lax.axis_index("z_lo")
    core = lax.axis_index("core")
    n_chips = lax.axis_size("z_lo")

    def half_of(array, which):
        width = array.shape[-1] // 2
        return lax.dynamic_slice_in_dim(array[0], which * width, width, 1)

    swap = [(0, 1), (1, 0)]

    pair_mine = jnp.concatenate([half_of(keys, core), half_of(values, core)], axis=1)
    pair_other = jnp.concatenate([half_of(keys, 1 - core), half_of(values, 1 - core)], axis=1)

    def behind(distance, flip):
        return [
            (chip_at * 2 + c, (chip_at + distance) * 2 + (c ^ flip))
            for chip_at in range(n_chips - distance)
            for c in range(2)
        ]

    blocks = [pair_mine, lax.ppermute(pair_other, "core", swap)]
    for distance in range(1, REACH + 1):
        blocks.append(lax.ppermute(pair_mine, ("z_lo", "core"), behind(distance, 0)))
        blocks.append(lax.ppermute(pair_other, ("z_lo", "core"), behind(distance, 1)))
    q_mine, do_mine = half_of(queries, core), half_of(out_grad, core)
    qdo_other = lax.ppermute(
        jnp.concatenate([half_of(queries, 1 - core), half_of(out_grad, 1 - core)], axis=1),
        "core",
        swap,
    )

    n_y, n_x = lax.axis_size("y"), lax.axis_size("x")
    n_z = lax.axis_size("z_hi") * n_chips
    depth = layer_input.shape[2] // (n_y * n_x)
    columns = (
        layer_input[0].reshape(rows, n_y, n_x, depth).transpose(2, 1, 3, 0).reshape(n_x, n_y * depth, rows)
    )
    columns_mine = lax.all_to_all(columns, "x", 0, 0, tiled=True)
    columns_other = lax.ppermute(columns_mine, "core", swap)

    seg_row = segment_ids[0]
    lane = jnp.arange(rows, dtype=jnp.int32)

    def places(chip_at, which):
        start = chip_at * chip + which * rows
        return (start + lane, lax.dynamic_slice_in_dim(seg_row, jnp.maximum(start, 0), rows, 0))

    key_places = [
        places(z_lo - distance, which)
        for distance in range(REACH + 1)
        for which in (core, 1 - core)
    ]
    key_pos = jnp.concatenate([place[0] for place in key_places])[:, None]
    key_doc = jnp.concatenate([place[1] for place in key_places])[:, None]
    query_pos = jnp.concatenate([place[0] for place in key_places[:2]])[None, :]
    query_doc = jnp.concatenate([place[1] for place in key_places[:2]])[None, :]
    allowed = (key_pos >= 0) & (key_pos <= query_pos) & (key_doc == query_doc)
    bias = jnp.where(allowed, 0.0, MASKED).astype(jnp.float32)

    dq_mine, dq_other, pair_grad, near_grad, far_grad = attention(
        q_mine, do_mine, qdo_other, blocks, bias
    )
    dq_back = lax.ppermute(dq_other, "core", swap)
    query_grad = jnp.where(
        core == 0,
        jnp.concatenate([dq_mine, dq_back], axis=1),
        jnp.concatenate([dq_back, dq_mine], axis=1),
    )[None]

    for distance, part in ((1, near_grad), (2, far_grad)):
        back = [(b, a) for a, b in behind(distance, 0)]
        pair_grad = pair_grad + lax.ppermute(part, ("z_lo", "core"), back).astype(jnp.float32)
    pair_grad = pair_grad.astype(jnp.bfloat16)

    gathered = lax.all_to_all(
        jnp.broadcast_to(pair_grad, (n_x, chip, 2 * DH)), "x", 0, 0, tiled=True
    )
    term = project(columns_mine, columns_other, gathered, n_y)
    over_y = lax.all_to_all(term.reshape(n_y, depth, 2 * DH), "y", 0, 0, tiled=True)
    term = jnp.sum(over_y.astype(jnp.float32), axis=0).astype(jnp.bfloat16)
    spread = lax.all_to_all(
        term.reshape(n_z * 2, depth // (n_z * 2), 2 * DH), ("z_hi", "z_lo", "core"), 0, 0, tiled=True
    )
    weight_grad = final_sum(spread)
    return (query_grad, weight_grad)


def solution(mesh):
    axes = ("y", "x", "z_hi", "z_lo", "core")
    fine = Mesh(mesh.devices.reshape(4, 4, 2, 4, 2), axes)
    dp, ctx = axes[:3], axes[3:]
    return jax.shard_map(
        per_device,
        mesh=fine,
        in_specs=(P(dp, ctx, None),) * 5 + (P(dp, None),),
        out_specs=(P(dp, ctx, None), P(axes, None)),
        check_vma=False,
    )
```

```python
import jax
import jax.numpy as jnp
from jax import lax
from jax.experimental import pallas as pl
from jax.experimental.pallas import tpu as pltpu
from jax.sharding import Mesh, PartitionSpec as P

H = 16
KV = 2
DH = 128
GROUP = H // KV
SCALE = 1.0 / DH**0.5
LOG2E = 1.4426950408889634
REACH = 2
MASKED = -1e30
MIB = 1024 * 1024
SMALL = pltpu.CompilerParams(vmem_limit_bytes=4 * MIB)


def dot_nt(left, right):
    return lax.dot_general(
        left, right, (((1,), (1,)), ((), ())), preferred_element_type=jnp.float32
    )


def dot_nn(left, right):
    return jnp.dot(left, right, preferred_element_type=jnp.float32)


def whole(shape, dtype=jnp.bfloat16):
    return jax.ShapeDtypeStruct(shape, dtype)


HBM = pl.BlockSpec(memory_space=pltpu.HBM)
SCALAR = pl.BlockSpec(memory_space=pltpu.SMEM)
VMEM = pl.BlockSpec(memory_space=pltpu.VMEM)


def half(which, width):
    return pl.ds(pl.multiple_of(which * width, width), width)


def pair_kernel(core_ref, keys, values, mine, other):
    core = core_ref[0]
    for out, which in ((mine, core), (other, 1 - core)):
        out[:, :DH] = keys[:, half(which, DH)]
        out[:, DH:] = values[:, half(which, DH)]


def split_pairs(core, keys, values):
    return pl.pallas_call(
        pair_kernel,
        out_shape=(whole(keys.shape), whole(keys.shape)),
        in_specs=[SCALAR, VMEM, VMEM],
        compiler_params=SMALL,
        cost_estimate=pl.CostEstimate(flops=0, bytes_accessed=256 * 1024, transcendentals=0),
    )(core, keys, values)


def run_copies(copies, sems):
    started = [pltpu.make_async_copy(src, dst, sems.at[i]) for i, (src, dst) in enumerate(copies)]
    for copy in started:
        copy.start()
    for copy in started:
        copy.wait()


def other_kernel(core_ref, queries, out_grad, keys, values, out, sems):
    other = 1 - core_ref[0]
    wide = GROUP * DH
    run_copies(
        [
            (queries.at[:, half(other, wide)], out.at[:, :wide]),
            (out_grad.at[:, half(other, wide)], out.at[:, wide : 2 * wide]),
            (keys.at[:, half(other, DH)], out.at[:, 2 * wide : 2 * wide + DH]),
            (values.at[:, half(other, DH)], out.at[:, 2 * wide + DH :]),
        ],
        sems,
    )


def split_other(core, queries, out_grad, keys, values):
    rows = queries.shape[0]
    return pl.pallas_call(
        other_kernel,
        out_shape=whole((rows, 2 * GROUP * DH + 2 * DH)),
        in_specs=[SCALAR, HBM, HBM, HBM, HBM],
        out_specs=HBM,
        scratch_shapes=[pltpu.SemaphoreType.DMA((4,))],
        compiler_params=SMALL,
        cost_estimate=pl.CostEstimate(flops=0, bytes_accessed=1200 * 1024, transcendentals=0),
    )(core, queries, out_grad, keys, values)


def chunk_kernel(columns, out, sems):
    width = out.shape[2]
    run_copies(
        [(columns.at[:, i * width : (i + 1) * width], out.at[i]) for i in range(out.shape[0])], sems
    )


def split_columns(columns, chunks):
    rows, width = columns.shape
    return pl.pallas_call(
        chunk_kernel,
        out_shape=whole((chunks, rows, width // chunks)),
        in_specs=[HBM],
        out_specs=HBM,
        scratch_shapes=[pltpu.SemaphoreType.DMA((chunks,))],
        compiler_params=SMALL,
        cost_estimate=pl.CostEstimate(flops=0, bytes_accessed=4 * 1024 * 1024, transcendentals=0),
    )(columns)


def attention_kernel(
    core_ref, queries, out_grad, swapped, k0, k2, k3, k4, k5, bias,
    dq_mine, dq_other, own_grad, near_grad, far_grad, dk_acc, dv_acc,
):
    wide = GROUP * DH
    core = core_ref[0]
    k1 = swapped[:, 2 * wide :]
    pairs = jnp.concatenate([k0[...], k1, k2[...], k3[...], k4[...], k5[...]], axis=0)
    key, value = pairs[:, :DH], pairs[:, DH:]
    key_t = key.T
    rows = queries.shape[0]
    for head in range(GROUP):
        cols = slice(head * DH, (head + 1) * DH)
        grad_cols = slice(wide + head * DH, wide + (head + 1) * DH)
        mine = pl.ds(pl.multiple_of(core * wide + head * DH, DH), DH)
        query = jnp.concatenate([queries[:, mine], swapped[:, cols]], axis=0)
        grad = jnp.concatenate([out_grad[:, mine], swapped[:, grad_cols]], axis=0)
        score = dot_nt(key, query) * (SCALE * LOG2E) + bias[...]
        top = jnp.max(score, axis=0, keepdims=True)
        weight = jnp.exp2(score - top)
        inverse = 1.0 / jnp.sum(weight, axis=0, keepdims=True)
        prob = weight * inverse
        prob_half = prob.astype(jnp.bfloat16)
        prob_grad = dot_nt(value, grad)
        delta = jnp.sum(prob_half.astype(jnp.float32) * prob_grad, axis=0, keepdims=True)
        score_grad = (prob * (prob_grad - delta) * SCALE).astype(jnp.bfloat16)
        dq = dot_nn(key_t, score_grad).T.astype(jnp.bfloat16)
        dq_mine[:, cols] = dq[:rows]
        dq_other[:, cols] = dq[rows:]
        dk = dot_nn(score_grad, query)
        dv = dot_nn(prob_half, grad)
        if head == 0:
            dk_acc[...] = dk
            dv_acc[...] = dv
        else:
            dk_acc[...] += dk
            dv_acc[...] += dv
    chip = 2 * rows
    own_grad[:, :DH] = dk_acc[:chip]
    own_grad[:, DH:] = dv_acc[:chip]
    near_grad[:, :DH] = dk_acc[chip : 2 * chip].astype(jnp.bfloat16)
    near_grad[:, DH:] = dv_acc[chip : 2 * chip].astype(jnp.bfloat16)
    far_grad[:, :DH] = dk_acc[2 * chip :].astype(jnp.bfloat16)
    far_grad[:, DH:] = dv_acc[2 * chip :].astype(jnp.bfloat16)


def attention(core, queries, out_grad, swapped, blocks, bias):
    rows = queries.shape[0]
    chip = 2 * rows
    keys = chip * (REACH + 1)
    return pl.pallas_call(
        attention_kernel,
        out_shape=(
            whole((rows, GROUP * DH)),
            whole((rows, GROUP * DH)),
            whole((chip, 2 * DH), jnp.float32),
            whole((chip, 2 * DH)),
            whole((chip, 2 * DH)),
        ),
        in_specs=[SCALAR] + [VMEM] * (4 + len(blocks)),
        scratch_shapes=[
            pltpu.VMEM((keys, DH), jnp.float32),
            pltpu.VMEM((keys, DH), jnp.float32),
        ],
        compiler_params=pltpu.CompilerParams(vmem_limit_bytes=16 * MIB),
        cost_estimate=pl.CostEstimate(
            flops=10 * keys * chip * DH * GROUP,
            bytes_accessed=4 * 1024 * 1024,
            transcendentals=keys * chip * GROUP,
        ),
    )(core, queries, out_grad, swapped, *blocks, bias)


def combine_kernel(own, near, far, out):
    total = own[...] + near[...].astype(jnp.float32) + far[...].astype(jnp.float32)
    turned = total.T.astype(jnp.bfloat16)
    for i in range(out.shape[0]):
        out[i] = turned


def combine(own, near, far, copies):
    return pl.pallas_call(
        combine_kernel,
        out_shape=whole((copies, own.shape[1], own.shape[0])),
        compiler_params=SMALL,
        cost_estimate=pl.CostEstimate(flops=0, bytes_accessed=2 * 1024 * 1024, transcendentals=0),
    )(own, near, far)


def project_kernel(mine, other, grads, out):
    places = range(mine.shape[0])
    left = jnp.concatenate([grads[i] for i in places], axis=1)
    right = jnp.concatenate([part[i] for i in places for part in (mine, other)], axis=0)
    out[...] = dot_nn(left, right).T.astype(jnp.bfloat16)


def project(mine, other, grads, blocks):
    places, rows, columns = mine.shape
    width = grads.shape[1]
    step = columns // blocks
    return pl.pallas_call(
        project_kernel,
        out_shape=whole((columns, width)),
        grid=(blocks,),
        in_specs=[
            pl.BlockSpec((places, rows, step), lambda i: (0, 0, i)),
            pl.BlockSpec((places, rows, step), lambda i: (0, 0, i)),
            pl.BlockSpec(grads.shape, lambda i: (0, 0, 0)),
        ],
        out_specs=pl.BlockSpec((step, width), lambda i: (i, 0)),
        compiler_params=pltpu.CompilerParams(vmem_limit_bytes=8 * MIB),
        cost_estimate=pl.CostEstimate(
            flops=4 * places * rows * columns * width, bytes_accessed=6 * 1024 * 1024, transcendentals=0
        ),
    )(mine, other, grads)


def final_kernel(parts, out):
    for head in range(KV):
        total = parts[head].astype(jnp.float32)
        for i in range(1, parts.shape[0] // KV):
            total = total + parts[KV * i + head].astype(jnp.float32)
        out[:, head * DH : (head + 1) * DH] = total[:, :DH]
        out[:, (KV + head) * DH : (KV + head + 1) * DH] = total[:, DH:]


def final_sum(parts):
    return pl.pallas_call(
        final_kernel,
        out_shape=whole((parts.shape[1], 2 * KV * DH), jnp.float32),
        compiler_params=SMALL,
        cost_estimate=pl.CostEstimate(flops=0, bytes_accessed=512 * 1024, transcendentals=0),
    )(parts)


def per_device(queries, keys, values, out_grad, layer_input, segment_ids):
    rows = queries.shape[1]
    chip = 2 * rows
    z_lo = lax.axis_index("z_lo")
    core = lax.axis_index("core")
    core_ref = core.astype(jnp.int32).reshape(1)
    n_chips = lax.axis_size("z_lo")
    swap = [(0, 1), (1, 0)]

    group = ("y", "x_hi")
    n_group = lax.axis_size("y") * lax.axis_size("x_hi")
    columns = split_columns(layer_input[0], n_group)
    core_ref, columns = lax.optimization_barrier((core_ref, columns))

    pair_mine, pair_other = split_pairs(core_ref, keys[0], values[0])

    def behind(distance, flip):
        return [
            (chip_at * 2 + c, (chip_at + distance) * 2 + (c ^ flip))
            for chip_at in range(n_chips - distance)
            for c in range(2)
        ]

    blocks = [pair_mine]
    for distance in range(1, REACH + 1):
        blocks.append(lax.ppermute(pair_mine, ("z_lo", "core"), behind(distance, 0)))
        blocks.append(lax.ppermute(pair_other, ("z_lo", "core"), behind(distance, 1)))
    swapped = lax.ppermute(
        split_other(core_ref, queries[0], out_grad[0], keys[0], values[0]), "core", swap
    )

    columns_mine = lax.all_to_all(columns, group, 0, 0, tiled=True)

    seg_row = segment_ids[0]
    lane = jnp.arange(rows, dtype=jnp.int32)

    def places(chip_at, which):
        start = chip_at * chip + which * rows
        return (start + lane, lax.dynamic_slice_in_dim(seg_row, jnp.maximum(start, 0), rows, 0))

    key_places = [
        places(z_lo - distance, which)
        for distance in range(REACH + 1)
        for which in (core, 1 - core)
    ]
    key_pos = jnp.concatenate([place[0] for place in key_places])[:, None]
    key_doc = jnp.concatenate([place[1] for place in key_places])[:, None]
    query_pos = jnp.concatenate([place[0] for place in key_places[:2]])[None, :]
    query_doc = jnp.concatenate([place[1] for place in key_places[:2]])[None, :]
    allowed = (key_pos >= 0) & (key_pos <= query_pos) & (key_doc == query_doc)
    bias = jnp.where(allowed, 0.0, MASKED).astype(jnp.float32)

    dq_mine, dq_other, own_grad, near_grad, far_grad = attention(
        core_ref, queries[0], out_grad[0], swapped, blocks, bias
    )
    dq_back = lax.ppermute(dq_other, "core", swap)
    query_grad = jnp.where(
        core == 0,
        jnp.concatenate([dq_mine, dq_back], axis=1),
        jnp.concatenate([dq_back, dq_mine], axis=1),
    )[None]

    near_back, far_back = (
        lax.ppermute(part, ("z_lo", "core"), [(b, a) for a, b in behind(distance, 0)])
        for distance, part in ((1, near_grad), (2, far_grad))
    )

    copies = combine(own_grad, near_back, far_back, n_group)
    gathered = lax.all_to_all(copies, group, 0, 0, tiled=True)
    columns_mine, _ = lax.optimization_barrier((columns_mine, copies))
    columns_other = lax.ppermute(columns_mine, "core", swap)
    term = project(columns_mine, columns_other, gathered, 4)
    rest = ("x_lo", "z_hi", "z_lo", "core")
    n_rest = lax.axis_size(rest)
    spread = lax.all_to_all(
        term.reshape(n_rest, term.shape[0] // n_rest, term.shape[1]), rest, 0, 0, tiled=True
    )
    return (query_grad, final_sum(spread))


def solution(mesh):
    axes = ("y", "x_hi", "x_lo", "z_hi", "z_lo", "core")
    fine = Mesh(mesh.devices.reshape(4, 2, 2, 2, 4, 2), axes)
    dp, ctx = axes[:4], axes[4:]
    return jax.shard_map(
        per_device,
        mesh=fine,
        in_specs=(P(dp, ctx, None),) * 5 + (P(dp, None),),
        out_specs=(P(dp, ctx, None), P(axes, None)),
        check_vma=False,
    )
```

```python
import jax
import jax.numpy as jnp
from jax import lax
from jax.experimental import pallas as pl
from jax.experimental.pallas import tpu as pltpu
from jax.sharding import Mesh, PartitionSpec as P

H = 16
KV = 2
DH = 128
GROUP = H // KV
SCALE = 1.0 / DH**0.5
LOG2E = 1.4426950408889634
REACH = 2
MASKED = -1e30
MIB = 1024 * 1024
SMALL = pltpu.CompilerParams(vmem_limit_bytes=4 * MIB)


def dot_nt(left, right):
    return lax.dot_general(
        left, right, (((1,), (1,)), ((), ())), preferred_element_type=jnp.float32
    )


def dot_nn(left, right):
    return jnp.dot(left, right, preferred_element_type=jnp.float32)


def whole(shape, dtype=jnp.bfloat16):
    return jax.ShapeDtypeStruct(shape, dtype)


HBM = pl.BlockSpec(memory_space=pltpu.HBM)


def run_copies(copies, sems):
    started = [pltpu.make_async_copy(src, dst, sems.at[i]) for i, (src, dst) in enumerate(copies)]
    for copy in started:
        copy.start()
    for copy in started:
        copy.wait()


def pair_kernel(keys, values, swapped, out):
    rows = keys.shape[0]
    out[:rows, :DH] = keys[...]
    out[:rows, DH:] = values[...]
    out[rows:] = swapped[:, 2 * GROUP * DH :]


def chip_pairs(keys, values, swapped):
    return pl.pallas_call(
        pair_kernel,
        out_shape=whole((2 * keys.shape[0], 2 * DH)),
        compiler_params=SMALL,
        cost_estimate=pl.CostEstimate(flops=0, bytes_accessed=256 * 1024, transcendentals=0),
    )(keys, values, swapped)


def chunk_kernel(columns, out, sems):
    width = out.shape[2]
    run_copies(
        [(columns.at[:, i * width : (i + 1) * width], out.at[i]) for i in range(out.shape[0])], sems
    )


def split_columns(columns, chunks):
    rows, width = columns.shape
    return pl.pallas_call(
        chunk_kernel,
        out_shape=whole((chunks, rows, width // chunks)),
        in_specs=[HBM],
        out_specs=HBM,
        scratch_shapes=[pltpu.SemaphoreType.DMA((chunks,))],
        compiler_params=SMALL,
        cost_estimate=pl.CostEstimate(flops=0, bytes_accessed=4 * 1024 * 1024, transcendentals=0),
    )(columns)


def attention_kernel(
    queries, out_grad, swapped, chip_pair, near_pair, far_pair, bias,
    dq_mine, dq_other, own_grad, near_grad, far_grad, dk_acc, dv_acc,
):
    wide = GROUP * DH
    pairs = jnp.concatenate([chip_pair[...], near_pair[...], far_pair[...]], axis=0)
    key, value = pairs[:, :DH], pairs[:, DH:]
    key_t = key.T
    rows = queries.shape[0]
    for head in range(GROUP):
        cols = slice(head * DH, (head + 1) * DH)
        grad_cols = slice(wide + head * DH, wide + (head + 1) * DH)
        query = jnp.concatenate([queries[:, cols], swapped[:, cols]], axis=0)
        grad = jnp.concatenate([out_grad[:, cols], swapped[:, grad_cols]], axis=0)
        score = dot_nt(key, query) * (SCALE * LOG2E) + bias[...]
        top = jnp.max(score, axis=0, keepdims=True)
        weight = jnp.exp2(score - top)
        inverse = 1.0 / jnp.sum(weight, axis=0, keepdims=True)
        prob = weight * inverse
        prob_half = prob.astype(jnp.bfloat16)
        prob_grad = dot_nt(value, grad)
        delta = jnp.sum(prob_half.astype(jnp.float32) * prob_grad, axis=0, keepdims=True)
        score_grad = (prob * (prob_grad - delta) * SCALE).astype(jnp.bfloat16)
        dq = dot_nn(key_t, score_grad).T.astype(jnp.bfloat16)
        dq_mine[:, cols] = dq[:rows]
        dq_other[:, cols] = dq[rows:]
        dk = dot_nn(score_grad, query)
        dv = dot_nn(prob_half, grad)
        if head == 0:
            dk_acc[...] = dk
            dv_acc[...] = dv
        else:
            dk_acc[...] += dk
            dv_acc[...] += dv
    chip = 2 * rows
    own_grad[:, :DH] = dk_acc[:chip]
    own_grad[:, DH:] = dv_acc[:chip]
    near_grad[:, :DH] = dk_acc[chip : 2 * chip].astype(jnp.bfloat16)
    near_grad[:, DH:] = dv_acc[chip : 2 * chip].astype(jnp.bfloat16)
    far_grad[:, :DH] = dk_acc[2 * chip :].astype(jnp.bfloat16)
    far_grad[:, DH:] = dv_acc[2 * chip :].astype(jnp.bfloat16)


def attention(queries, out_grad, swapped, blocks, bias):
    rows = queries.shape[0]
    chip = 2 * rows
    keys = chip * (REACH + 1)
    return pl.pallas_call(
        attention_kernel,
        out_shape=(
            whole((rows, GROUP * DH)),
            whole((rows, GROUP * DH)),
            whole((chip, 2 * DH), jnp.float32),
            whole((chip, 2 * DH)),
            whole((chip, 2 * DH)),
        ),
        scratch_shapes=[
            pltpu.VMEM((keys, DH), jnp.float32),
            pltpu.VMEM((keys, DH), jnp.float32),
        ],
        compiler_params=pltpu.CompilerParams(vmem_limit_bytes=16 * MIB),
        cost_estimate=pl.CostEstimate(
            flops=160 * keys * chip * DH * GROUP,
            bytes_accessed=4 * 1024 * 1024,
            transcendentals=keys * chip * GROUP,
        ),
    )(queries, out_grad, swapped, *blocks, bias)


def combine_kernel(own, near, far, out):
    total = own[...] + near[...].astype(jnp.float32) + far[...].astype(jnp.float32)
    turned = total.T.astype(jnp.bfloat16)
    for i in range(out.shape[0]):
        out[i] = turned


def combine(own, near, far, copies):
    return pl.pallas_call(
        combine_kernel,
        out_shape=whole((copies, own.shape[1], own.shape[0])),
        compiler_params=SMALL,
        cost_estimate=pl.CostEstimate(flops=0, bytes_accessed=2 * 1024 * 1024, transcendentals=0),
    )(own, near, far)


def project_kernel(mine, other, grads, out):
    places = range(mine.shape[0])
    left = jnp.concatenate([grads[i] for i in places], axis=1)
    right = jnp.concatenate([part[i] for i in places for part in (mine, other)], axis=0)
    out[...] = dot_nn(left, right).T.astype(jnp.bfloat16)


def project(mine, other, grads, blocks):
    places, rows, columns = mine.shape
    width = grads.shape[1]
    step = columns // blocks
    return pl.pallas_call(
        project_kernel,
        out_shape=whole((columns, width)),
        grid=(blocks,),
        in_specs=[
            pl.BlockSpec((places, rows, step), lambda i: (0, 0, i)),
            pl.BlockSpec((places, rows, step), lambda i: (0, 0, i)),
            pl.BlockSpec(grads.shape, lambda i: (0, 0, 0)),
        ],
        out_specs=pl.BlockSpec((step, width), lambda i: (i, 0)),
        compiler_params=pltpu.CompilerParams(vmem_limit_bytes=8 * MIB),
        cost_estimate=pl.CostEstimate(
            flops=4 * places * rows * columns * width, bytes_accessed=6 * 1024 * 1024, transcendentals=0
        ),
    )(mine, other, grads)


def final_kernel(parts, out):
    for head in range(KV):
        total = parts[head].astype(jnp.float32)
        for i in range(1, parts.shape[0] // KV):
            total = total + parts[KV * i + head].astype(jnp.float32)
        out[:, head * DH : (head + 1) * DH] = total[:, :DH]
        out[:, (KV + head) * DH : (KV + head + 1) * DH] = total[:, DH:]


def final_sum(parts):
    return pl.pallas_call(
        final_kernel,
        out_shape=whole((parts.shape[1], 2 * KV * DH), jnp.float32),
        compiler_params=SMALL,
        cost_estimate=pl.CostEstimate(flops=0, bytes_accessed=512 * 1024, transcendentals=0),
    )(parts)


def per_device(queries, keys, values, out_grad, layer_input, segment_ids):
    rows = queries.shape[1]
    chip = 2 * rows
    z_lo = lax.axis_index("z_lo")
    core = lax.axis_index("core")
    n_chips = lax.axis_size("z_lo")
    swap = [(0, 1), (1, 0)]

    def half_of(array, which):
        width = array.shape[-1] // 2
        return lax.dynamic_slice_in_dim(array[0], which * width, width, 1)

    sources = (queries, out_grad, keys, values)
    q_mine, do_mine, k_mine, v_mine = (half_of(array, core) for array in sources)
    swapped = lax.ppermute(
        jnp.concatenate([half_of(array, 1 - core) for array in sources], axis=1), "core", swap
    )
    chip_pair = chip_pairs(k_mine, v_mine, swapped)

    def behind(distance):
        return [
            (chip_at * 2 + c, (chip_at + distance) * 2 + c)
            for chip_at in range(n_chips - distance)
            for c in range(2)
        ]

    blocks = [chip_pair] + [
        lax.ppermute(chip_pair, ("z_lo", "core"), behind(distance)) for distance in (2, 1)
    ][::-1]

    group = ("y", "x_hi")
    n_group = lax.axis_size("y") * lax.axis_size("x_hi")
    columns = split_columns(layer_input[0], n_group)
    columns, _ = lax.optimization_barrier((columns, chip_pair))

    columns_mine = lax.all_to_all(columns, group, 0, 0, tiled=True)

    seg_row = segment_ids[0]
    lane = jnp.arange(rows, dtype=jnp.int32)

    def places(chip_at, which):
        start = chip_at * chip + which * rows
        return (start + lane, lax.dynamic_slice_in_dim(seg_row, jnp.maximum(start, 0), rows, 0))

    key_places = [
        places(z_lo - distance, which)
        for distance in range(REACH + 1)
        for which in (core, 1 - core)
    ]
    key_pos = jnp.concatenate([place[0] for place in key_places])[:, None]
    key_doc = jnp.concatenate([place[1] for place in key_places])[:, None]
    query_pos = jnp.concatenate([place[0] for place in key_places[:2]])[None, :]
    query_doc = jnp.concatenate([place[1] for place in key_places[:2]])[None, :]
    allowed = (key_pos >= 0) & (key_pos <= query_pos) & (key_doc == query_doc)
    bias = jnp.where(allowed, 0.0, MASKED).astype(jnp.float32)

    dq_mine, dq_other, own_grad, near_grad, far_grad = attention(
        q_mine, do_mine, swapped, blocks, bias
    )
    dq_back = lax.ppermute(dq_other, "core", swap)
    query_grad = jnp.where(
        core == 0,
        jnp.concatenate([dq_mine, dq_back], axis=1),
        jnp.concatenate([dq_back, dq_mine], axis=1),
    )[None]

    near_back, far_back = (
        lax.ppermute(part, ("z_lo", "core"), [(b, a) for a, b in behind(distance)])
        for distance, part in ((1, near_grad), (2, far_grad))
    )

    near_back, query_grad = lax.optimization_barrier((near_back, query_grad))

    copies = combine(own_grad, near_back, far_back, n_group)
    gathered = lax.all_to_all(copies, group, 0, 0, tiled=True)
    columns_mine, _ = lax.optimization_barrier((columns_mine, copies))
    columns_other = lax.ppermute(columns_mine, "core", swap)
    term = project(columns_mine, columns_other, gathered, 4)
    rest = ("x_lo", "z_hi", "z_lo", "core")
    n_rest = lax.axis_size(rest)
    spread = lax.all_to_all(
        term.reshape(n_rest, term.shape[0] // n_rest, term.shape[1]), rest, 0, 0, tiled=True
    )
    return (query_grad, final_sum(spread))


def solution(mesh):
    axes = ("y", "x_hi", "x_lo", "z_hi", "z_lo", "core")
    fine = Mesh(mesh.devices.reshape(4, 2, 2, 2, 4, 2), axes)
    dp, ctx = axes[:4], axes[4:]
    return jax.shard_map(
        per_device,
        mesh=fine,
        in_specs=(P(dp, ctx, None),) * 5 + (P(dp, None),),
        out_specs=(P(dp, ctx, None), P(axes, None)),
        check_vma=False,
    )
```

```python
import jax
import jax.numpy as jnp
from jax import lax
from jax.experimental import pallas as pl
from jax.experimental.pallas import tpu as pltpu
from jax.sharding import Mesh, PartitionSpec as P

H = 16
KV = 2
DH = 128
GROUP = H // KV
SCALE = 1.0 / DH**0.5
LOG2E = 1.4426950408889634
REACH = 2
MASKED = -1e30
MIB = 1024 * 1024
SMALL = pltpu.CompilerParams(vmem_limit_bytes=4 * MIB)


def dot_nt(left, right):
    return lax.dot_general(
        left, right, (((1,), (1,)), ((), ())), preferred_element_type=jnp.float32
    )


def dot_nn(left, right):
    return jnp.dot(left, right, preferred_element_type=jnp.float32)


def whole(shape, dtype=jnp.bfloat16):
    return jax.ShapeDtypeStruct(shape, dtype)


HBM = pl.BlockSpec(memory_space=pltpu.HBM)
SCALAR = pl.BlockSpec(memory_space=pltpu.SMEM)


def pair_kernel(keys, values, swapped, out):
    rows = keys.shape[0]
    out[:rows, :DH] = keys[...]
    out[:rows, DH:] = values[...]
    out[rows:] = swapped[:, 2 * GROUP * DH :]


def chip_pairs(keys, values, swapped):
    return pl.pallas_call(
        pair_kernel,
        out_shape=whole((2 * keys.shape[0], 2 * DH)),
        compiler_params=SMALL,
        cost_estimate=pl.CostEstimate(flops=0, bytes_accessed=256 * 1024, transcendentals=0),
    )(keys, values, swapped)


def chunk_kernel(place_ref, columns, *refs):
    outs, sems = refs[:-1], refs[-1]
    width = outs[0].shape[1]
    copies = []
    for k, out in enumerate(outs):
        start = pl.multiple_of((place_ref[0] ^ k) * width, width)
        copies.append(pltpu.make_async_copy(columns.at[:, pl.ds(start, width)], out, sems.at[k]))
    for copy in copies:
        copy.start()
    for copy in copies:
        copy.wait()


def split_columns(place, columns, chunks):
    rows, width = columns.shape
    return pl.pallas_call(
        chunk_kernel,
        out_shape=(whole((rows, width // chunks)),) * chunks,
        in_specs=[SCALAR, HBM],
        out_specs=(HBM,) * chunks,
        scratch_shapes=[pltpu.SemaphoreType.DMA((chunks,))],
        compiler_params=SMALL,
        cost_estimate=pl.CostEstimate(flops=0, bytes_accessed=4 * MIB, transcendentals=0),
    )(place, columns)


def attention_kernel(
    queries, out_grad, swapped, chip_pair, near_pair, far_pair, bias,
    dq_mine, dq_other, own_grad, near_grad, far_grad, dk_acc, dv_acc,
):
    wide = GROUP * DH
    pairs = jnp.concatenate([chip_pair[...], near_pair[...], far_pair[...]], axis=0)
    key, value = pairs[:, :DH], pairs[:, DH:]
    key_t = key.T
    rows = queries.shape[0]
    for head in range(GROUP):
        cols = slice(head * DH, (head + 1) * DH)
        grad_cols = slice(wide + head * DH, wide + (head + 1) * DH)
        query = jnp.concatenate([queries[:, cols], swapped[:, cols]], axis=0)
        grad = jnp.concatenate([out_grad[:, cols], swapped[:, grad_cols]], axis=0)
        score = dot_nt(key, query) * (SCALE * LOG2E) + bias[...]
        top = jnp.max(score, axis=0, keepdims=True)
        weight = jnp.exp2(score - top)
        inverse = 1.0 / jnp.sum(weight, axis=0, keepdims=True)
        prob = weight * inverse
        prob_half = prob.astype(jnp.bfloat16)
        prob_grad = dot_nt(value, grad)
        delta = jnp.sum(prob_half.astype(jnp.float32) * prob_grad, axis=0, keepdims=True)
        score_grad = (prob * (prob_grad - delta) * SCALE).astype(jnp.bfloat16)
        dq = dot_nn(key_t, score_grad).T.astype(jnp.bfloat16)
        dq_mine[:, cols] = dq[:rows]
        dq_other[:, cols] = dq[rows:]
        dk = dot_nn(score_grad, query)
        dv = dot_nn(prob_half, grad)
        if head == 0:
            dk_acc[...] = dk
            dv_acc[...] = dv
        else:
            dk_acc[...] += dk
            dv_acc[...] += dv
    chip = 2 * rows
    own_grad[:, :DH] = dk_acc[:chip]
    own_grad[:, DH:] = dv_acc[:chip]
    near_grad[:, :DH] = dk_acc[chip : 2 * chip].astype(jnp.bfloat16)
    near_grad[:, DH:] = dv_acc[chip : 2 * chip].astype(jnp.bfloat16)
    far_grad[:, :DH] = dk_acc[2 * chip :].astype(jnp.bfloat16)
    far_grad[:, DH:] = dv_acc[2 * chip :].astype(jnp.bfloat16)


def attention(queries, out_grad, swapped, blocks, bias):
    rows = queries.shape[0]
    chip = 2 * rows
    keys = chip * (REACH + 1)
    return pl.pallas_call(
        attention_kernel,
        out_shape=(
            whole((rows, GROUP * DH)),
            whole((rows, GROUP * DH)),
            whole((chip, 2 * DH), jnp.float32),
            whole((chip, 2 * DH)),
            whole((chip, 2 * DH)),
        ),
        scratch_shapes=[
            pltpu.VMEM((keys, DH), jnp.float32),
            pltpu.VMEM((keys, DH), jnp.float32),
        ],
        compiler_params=pltpu.CompilerParams(vmem_limit_bytes=16 * MIB),
        cost_estimate=pl.CostEstimate(
            flops=40 * keys * chip * DH * GROUP,
            bytes_accessed=4 * 1024 * 1024,
            transcendentals=keys * chip * GROUP,
        ),
    )(queries, out_grad, swapped, *blocks, bias)


def combine_kernel(own, near, far, out):
    total = own[...] + near[...].astype(jnp.float32) + far[...].astype(jnp.float32)
    turned = total.T.astype(jnp.bfloat16)
    for i in range(out.shape[0]):
        out[i] = turned


def combine(own, near, far, copies):
    return pl.pallas_call(
        combine_kernel,
        out_shape=whole((copies, own.shape[1], own.shape[0])),
        compiler_params=SMALL,
        cost_estimate=pl.CostEstimate(flops=0, bytes_accessed=2 * 1024 * 1024, transcendentals=0),
    )(own, near, far)


def assemble_kernel(core_ref, mine, other, out):
    width = mine.shape[1]
    core = core_ref[0]
    out[:, pl.ds(pl.multiple_of(core * width, width), width)] = mine[...]
    out[:, pl.ds(pl.multiple_of((1 - core) * width, width), width)] = other[...]


def assemble(core, mine, other):
    return pl.pallas_call(
        assemble_kernel,
        out_shape=whole((mine.shape[0], 2 * mine.shape[1])),
        in_specs=[SCALAR, pl.BlockSpec(), pl.BlockSpec()],
        compiler_params=SMALL,
        cost_estimate=pl.CostEstimate(flops=0, bytes_accessed=MIB, transcendentals=0),
    )(core, mine, other)


def project_kernel(place_ref, *refs):
    pieces, grads, out = refs[:-2], refs[-2], refs[-1]
    places = range(len(pieces) // 2)
    left = jnp.concatenate([grads[place_ref[0] ^ k] for k in places], axis=1)
    right = jnp.concatenate([ref[...] for ref in pieces], axis=0)
    out[...] = dot_nn(left, right).T.astype(jnp.bfloat16)


def project(place, pieces, grads, blocks):
    rows, columns = pieces[0].shape
    width = grads.shape[1]
    step = columns // blocks
    return pl.pallas_call(
        project_kernel,
        out_shape=whole((columns, width)),
        grid=(blocks,),
        in_specs=[SCALAR]
        + [pl.BlockSpec((rows, step), lambda i: (0, i))] * len(pieces)
        + [pl.BlockSpec(grads.shape, lambda i: (0, 0, 0))],
        out_specs=pl.BlockSpec((step, width), lambda i: (i, 0)),
        compiler_params=pltpu.CompilerParams(vmem_limit_bytes=16 * MIB),
        cost_estimate=pl.CostEstimate(
            flops=2 * len(pieces) * rows * columns * width,
            bytes_accessed=6 * MIB,
            transcendentals=0,
        ),
    )(place, *pieces, grads)


def final_kernel(parts, out):
    for head in range(KV):
        total = parts[head].astype(jnp.float32)
        for i in range(1, parts.shape[0] // KV):
            total = total + parts[KV * i + head].astype(jnp.float32)
        out[:, head * DH : (head + 1) * DH] = total[:, :DH]
        out[:, (KV + head) * DH : (KV + head + 1) * DH] = total[:, DH:]


def final_sum(parts):
    return pl.pallas_call(
        final_kernel,
        out_shape=whole((parts.shape[1], 2 * KV * DH), jnp.float32),
        compiler_params=SMALL,
        cost_estimate=pl.CostEstimate(flops=0, bytes_accessed=512 * 1024, transcendentals=0),
    )(parts)


def per_device(queries, keys, values, out_grad, layer_input, segment_ids):
    rows = queries.shape[1]
    chip = 2 * rows
    z_lo = lax.axis_index("z_lo")
    core = lax.axis_index("core")
    n_chips = lax.axis_size("z_lo")
    swap = [(0, 1), (1, 0)]
    core_ref = core.astype(jnp.int32).reshape(1)
    place_ref = lax.axis_index("y").astype(jnp.int32).reshape(1)

    def half_of(array, which):
        width = array.shape[-1] // 2
        return lax.dynamic_slice_in_dim(array[0], which * width, width, 1)

    sources = (queries, out_grad, keys, values)
    q_mine, do_mine, k_mine, v_mine = (half_of(array, core) for array in sources)
    swapped = lax.ppermute(
        jnp.concatenate([half_of(array, 1 - core) for array in sources], axis=1), "core", swap
    )
    chip_pair = chip_pairs(k_mine, v_mine, swapped)

    def behind(distance):
        return [
            (chip_at * 2 + c, (chip_at + distance) * 2 + c)
            for chip_at in range(n_chips - distance)
            for c in range(2)
        ]

    blocks = [chip_pair] + [
        lax.ppermute(chip_pair, ("z_lo", "core"), behind(distance)) for distance in (2, 1)
    ][::-1]

    n_y = lax.axis_size("y")
    chunks = split_columns(place_ref, layer_input[0], n_y)
    chunks, _ = lax.optimization_barrier((chunks, chip_pair))
    pieces = [chunks[0]] + [
        lax.ppermute(chunks[k], "y", [(i, i ^ k) for i in range(n_y)]) for k in range(1, n_y)
    ]

    seg_row = segment_ids[0]
    lane = jnp.arange(rows, dtype=jnp.int32)

    def places(chip_at, which):
        start = chip_at * chip + which * rows
        return (start + lane, lax.dynamic_slice_in_dim(seg_row, jnp.maximum(start, 0), rows, 0))

    key_places = [
        places(z_lo - distance, which)
        for distance in range(REACH + 1)
        for which in (core, 1 - core)
    ]
    key_pos = jnp.concatenate([place[0] for place in key_places])[:, None]
    key_doc = jnp.concatenate([place[1] for place in key_places])[:, None]
    query_pos = jnp.concatenate([place[0] for place in key_places[:2]])[None, :]
    query_doc = jnp.concatenate([place[1] for place in key_places[:2]])[None, :]
    allowed = (key_pos >= 0) & (key_pos <= query_pos) & (key_doc == query_doc)
    bias = jnp.where(allowed, 0.0, MASKED).astype(jnp.float32)

    dq_mine, dq_other, own_grad, near_grad, far_grad = attention(
        q_mine, do_mine, swapped, blocks, bias
    )
    dq_back = lax.ppermute(dq_other, "core", swap)
    query_grad = assemble(core_ref, dq_mine, dq_back)[None]

    near_back, far_back = (
        lax.ppermute(part, ("z_lo", "core"), [(b, a) for a, b in behind(distance)])
        for distance, part in ((1, near_grad), (2, far_grad))
    )

    near_back, query_grad = lax.optimization_barrier((near_back, query_grad))

    copies = combine(own_grad, near_back, far_back, n_y)
    gathered = lax.all_to_all(copies, "y", 0, 0, tiled=True)
    pieces, _ = lax.optimization_barrier((pieces, copies))
    both = [part for piece in pieces for part in (piece, lax.ppermute(piece, "core", swap))]
    term = project(place_ref, both, gathered, 4)
    n_x = lax.axis_size("x")
    over_x = lax.all_to_all(term.reshape(n_x, -1, term.shape[1]), "x", 0, 0, tiled=True)
    term = jnp.sum(over_x.astype(jnp.float32), axis=0).astype(jnp.bfloat16)
    rest = ("z_hi", "z_lo", "core")
    n_rest = lax.axis_size(rest)
    spread = lax.all_to_all(
        term.reshape(n_rest, term.shape[0] // n_rest, term.shape[1]), rest, 0, 0, tiled=True
    )
    return (query_grad, final_sum(spread))


def solution(mesh):
    axes = ("y", "x", "z_hi", "z_lo", "core")
    fine = Mesh(mesh.devices.reshape(4, 4, 2, 4, 2), axes)
    dp, ctx = axes[:3], axes[3:]
    return jax.shard_map(
        per_device,
        mesh=fine,
        in_specs=(P(dp, ctx, None),) * 5 + (P(dp, None),),
        out_specs=(P(dp, ctx, None), P(axes, None)),
        check_vma=False,
    )
```

```python
import functools

import jax
import jax.numpy as jnp
from jax import lax
from jax.experimental import pallas as pl
from jax.experimental.pallas import tpu as pltpu
from jax.sharding import Mesh, PartitionSpec as P

H = 16
KV = 2
DH = 128
GROUP = H // KV
SCALE = 1.0 / DH**0.5
LOG2E = 1.4426950408889634
REACH = 2
MASKED = -1e30
MIB = 1024 * 1024
SMALL = pltpu.CompilerParams(vmem_limit_bytes=4 * MIB)


def dot_nt(left, right):
    return lax.dot_general(
        left, right, (((1,), (1,)), ((), ())), preferred_element_type=jnp.float32
    )


def dot_nn(left, right):
    return jnp.dot(left, right, preferred_element_type=jnp.float32)


def whole(shape, dtype=jnp.bfloat16):
    return jax.ShapeDtypeStruct(shape, dtype)


HBM = pl.BlockSpec(memory_space=pltpu.HBM)
SCALAR = pl.BlockSpec(memory_space=pltpu.SMEM)


def pair_kernel(keys, values, swapped, out):
    rows = keys.shape[0]
    out[:rows, :DH] = keys[...]
    out[:rows, DH:] = values[...]
    out[rows:] = swapped[...]


def chip_pairs(keys, values, swapped):
    return pl.pallas_call(
        pair_kernel,
        out_shape=whole((2 * keys.shape[0], 2 * DH)),
        compiler_params=SMALL,
        cost_estimate=pl.CostEstimate(flops=0, bytes_accessed=256 * 1024, transcendentals=0),
    )(keys, values, swapped)


def chunk_kernel(place_ref, columns, *refs):
    outs, sems = refs[:-1], refs[-1]
    width = outs[0].shape[1]
    copies = []
    for k, out in enumerate(outs):
        start = pl.multiple_of((place_ref[0] ^ k) * width, width)
        copies.append(pltpu.make_async_copy(columns.at[:, pl.ds(start, width)], out, sems.at[k]))
    for copy in copies:
        copy.start()
    for copy in copies:
        copy.wait()


def split_columns(place, columns, chunks):
    rows, width = columns.shape
    return pl.pallas_call(
        chunk_kernel,
        out_shape=(whole((rows, width // chunks)),) * chunks,
        in_specs=[SCALAR, HBM],
        out_specs=(HBM,) * chunks,
        scratch_shapes=[pltpu.SemaphoreType.DMA((chunks,))],
        compiler_params=SMALL,
        cost_estimate=pl.CostEstimate(flops=0, bytes_accessed=4 * MIB, transcendentals=0),
    )(place, columns)


def attention_kernel(
    queries, out_grad, q_other, do_other, chip_pair, near_pair, far_pair, bias,
    dq_mine, dq_other, own_grad, near_grad, far_grad, dk_acc, dv_acc,
):
    pairs = jnp.concatenate([chip_pair[...], near_pair[...], far_pair[...]], axis=0)
    key, value = pairs[:, :DH], pairs[:, DH:]
    key_t = key.T
    rows = queries.shape[0]
    for head in range(GROUP):
        cols = slice(head * DH, (head + 1) * DH)
        query = jnp.concatenate([queries[:, cols], q_other[:, cols]], axis=0)
        grad = jnp.concatenate([out_grad[:, cols], do_other[:, cols]], axis=0)
        score = dot_nt(key, query) * (SCALE * LOG2E) + bias[...]
        top = jnp.max(score, axis=0, keepdims=True)
        weight = jnp.exp2(score - top)
        inverse = 1.0 / jnp.sum(weight, axis=0, keepdims=True)
        prob = weight * inverse
        prob_half = prob.astype(jnp.bfloat16)
        prob_grad = dot_nt(value, grad)
        delta = jnp.sum(prob_half.astype(jnp.float32) * prob_grad, axis=0, keepdims=True)
        score_grad = (prob * (prob_grad - delta) * SCALE).astype(jnp.bfloat16)
        dq = dot_nn(key_t, score_grad).T.astype(jnp.bfloat16)
        dq_mine[:, cols] = dq[:rows]
        dq_other[:, cols] = dq[rows:]
        dk = dot_nn(score_grad, query)
        dv = dot_nn(prob_half, grad)
        if head == 0:
            dk_acc[...] = dk
            dv_acc[...] = dv
        else:
            dk_acc[...] += dk
            dv_acc[...] += dv
    chip = 2 * rows
    own_grad[:, :DH] = dk_acc[:chip]
    own_grad[:, DH:] = dv_acc[:chip]
    near_grad[:, :DH] = dk_acc[chip : 2 * chip].astype(jnp.bfloat16)
    near_grad[:, DH:] = dv_acc[chip : 2 * chip].astype(jnp.bfloat16)
    far_grad[:, :DH] = dk_acc[2 * chip :].astype(jnp.bfloat16)
    far_grad[:, DH:] = dv_acc[2 * chip :].astype(jnp.bfloat16)


def attention(queries, out_grad, q_other, do_other, blocks, bias):
    rows = queries.shape[0]
    chip = 2 * rows
    keys = chip * (REACH + 1)
    return pl.pallas_call(
        attention_kernel,
        out_shape=(
            whole((rows, GROUP * DH)),
            whole((rows, GROUP * DH)),
            whole((chip, 2 * DH), jnp.float32),
            whole((chip, 2 * DH)),
            whole((chip, 2 * DH)),
        ),
        scratch_shapes=[
            pltpu.VMEM((keys, DH), jnp.float32),
            pltpu.VMEM((keys, DH), jnp.float32),
        ],
        compiler_params=pltpu.CompilerParams(vmem_limit_bytes=16 * MIB),
        cost_estimate=pl.CostEstimate(
            flops=40 * keys * chip * DH * GROUP,
            bytes_accessed=4 * 1024 * 1024,
            transcendentals=keys * chip * GROUP,
        ),
    )(queries, out_grad, q_other, do_other, *blocks, bias)


def combine_kernel(own, near, far, out):
    total = own[...] + near[...].astype(jnp.float32) + far[...].astype(jnp.float32)
    turned = total.T.astype(jnp.bfloat16)
    for i in range(out.shape[0]):
        out[i] = turned


def combine(own, near, far, copies):
    return pl.pallas_call(
        combine_kernel,
        out_shape=whole((copies, own.shape[1], own.shape[0])),
        compiler_params=SMALL,
        cost_estimate=pl.CostEstimate(flops=0, bytes_accessed=2 * 1024 * 1024, transcendentals=0),
    )(own, near, far)


def assemble_kernel(core_ref, mine, other, out):
    width = mine.shape[1]
    core = core_ref[0]
    out[:, pl.ds(pl.multiple_of(core * width, width), width)] = mine[...]
    out[:, pl.ds(pl.multiple_of((1 - core) * width, width), width)] = other[...]


def assemble(core, mine, other):
    return pl.pallas_call(
        assemble_kernel,
        out_shape=whole((mine.shape[0], 2 * mine.shape[1])),
        in_specs=[SCALAR, pl.BlockSpec(), pl.BlockSpec()],
        compiler_params=SMALL,
        cost_estimate=pl.CostEstimate(flops=0, bytes_accessed=MIB, transcendentals=0),
    )(core, mine, other)


def project_kernel(places_ref, *refs, offset):
    pieces, grads, out = refs[:-2], refs[-2], refs[-1]
    step = out.shape[0]
    columns = pl.ds(pl.multiple_of((places_ref[1] ^ offset) * step, step), step)
    left = jnp.concatenate([grads[places_ref[0] ^ k] for k in range(len(pieces) // 2)], axis=1)
    right = jnp.concatenate([ref[:, columns] for ref in pieces], axis=0)
    out[...] = dot_nn(left, right).T.astype(out.dtype)


def project(places, pieces, grads, blocks, offset, dtype):
    rows, columns = pieces[0].shape
    width = grads.shape[1]
    step = columns // blocks
    return pl.pallas_call(
        functools.partial(project_kernel, offset=offset),
        out_shape=whole((step, width), dtype),
        in_specs=[SCALAR] + [pl.BlockSpec()] * (len(pieces) + 1),
        compiler_params=pltpu.CompilerParams(vmem_limit_bytes=16 * MIB),
        cost_estimate=pl.CostEstimate(
            flops=2 * len(pieces) * rows * step * width,
            bytes_accessed=2 * MIB,
            transcendentals=0,
        ),
    )(places, *pieces, grads)


def add_kernel(*refs):
    total = refs[0][...]
    for ref in refs[1:-1]:
        total = total + ref[...].astype(jnp.float32)
    refs[-1][...] = total.astype(jnp.bfloat16)


def add_parts(own, parts):
    return pl.pallas_call(
        add_kernel,
        out_shape=whole(own.shape),
        compiler_params=SMALL,
        cost_estimate=pl.CostEstimate(flops=0, bytes_accessed=2 * MIB, transcendentals=0),
    )(own, *parts)


def final_kernel(parts, out):
    for head in range(KV):
        total = parts[head].astype(jnp.float32)
        for i in range(1, parts.shape[0] // KV):
            total = total + parts[KV * i + head].astype(jnp.float32)
        out[:, head * DH : (head + 1) * DH] = total[:, :DH]
        out[:, (KV + head) * DH : (KV + head + 1) * DH] = total[:, DH:]


def final_sum(parts):
    return pl.pallas_call(
        final_kernel,
        out_shape=whole((parts.shape[1], 2 * KV * DH), jnp.float32),
        compiler_params=SMALL,
        cost_estimate=pl.CostEstimate(flops=0, bytes_accessed=512 * 1024, transcendentals=0),
    )(parts)


def per_device(queries, keys, values, out_grad, layer_input, segment_ids):
    rows = queries.shape[1]
    chip = 2 * rows
    z_lo = lax.axis_index("z_lo")
    core = lax.axis_index("core")
    n_chips = lax.axis_size("z_lo")
    swap = [(0, 1), (1, 0)]
    core_ref = core.astype(jnp.int32).reshape(1)
    places_ref = jnp.stack([lax.axis_index("y"), lax.axis_index("x")]).astype(jnp.int32)

    def half_of(array, which):
        width = array.shape[-1] // 2
        return lax.dynamic_slice_in_dim(array[0], which * width, width, 1)

    k_mine, v_mine = half_of(keys, core), half_of(values, core)
    chip_pair = chip_pairs(
        k_mine,
        v_mine,
        lax.ppermute(
            jnp.concatenate([half_of(keys, 1 - core), half_of(values, 1 - core)], axis=1), "core", swap
        ),
    )
    q_mine, do_mine = half_of(queries, core), half_of(out_grad, core)
    q_out, do_out = half_of(queries, 1 - core), half_of(out_grad, 1 - core)
    q_out, do_out, _ = lax.optimization_barrier((q_out, do_out, chip_pair))
    q_other, do_other = (lax.ppermute(part, "core", swap) for part in (q_out, do_out))

    def behind(distance):
        return [
            (chip_at * 2 + c, (chip_at + distance) * 2 + c)
            for chip_at in range(n_chips - distance)
            for c in range(2)
        ]

    blocks = [chip_pair] + [
        lax.ppermute(chip_pair, ("z_lo", "core"), behind(distance)) for distance in (2, 1)
    ][::-1]

    n_y = lax.axis_size("y")
    chunks = split_columns(places_ref, layer_input[0], n_y)
    chunks, _ = lax.optimization_barrier((chunks, (q_other, do_other)))
    pieces = [chunks[0]] + [
        lax.ppermute(chunks[k], "y", [(i, i ^ k) for i in range(n_y)]) for k in range(1, n_y)
    ]

    seg_row = segment_ids[0]
    lane = jnp.arange(rows, dtype=jnp.int32)

    def places(chip_at, which):
        start = chip_at * chip + which * rows
        return (start + lane, lax.dynamic_slice_in_dim(seg_row, jnp.maximum(start, 0), rows, 0))

    key_places = [
        places(z_lo - distance, which)
        for distance in range(REACH + 1)
        for which in (core, 1 - core)
    ]
    key_pos = jnp.concatenate([place[0] for place in key_places])[:, None]
    key_doc = jnp.concatenate([place[1] for place in key_places])[:, None]
    query_pos = jnp.concatenate([place[0] for place in key_places[:2]])[None, :]
    query_doc = jnp.concatenate([place[1] for place in key_places[:2]])[None, :]
    allowed = (key_pos >= 0) & (key_pos <= query_pos) & (key_doc == query_doc)
    bias = jnp.where(allowed, 0.0, MASKED).astype(jnp.float32)

    dq_mine, dq_other, own_grad, near_grad, far_grad = attention(
        q_mine, do_mine, q_other, do_other, blocks, bias
    )
    dq_back = lax.ppermute(dq_other, "core", swap)
    query_grad = assemble(core_ref, dq_mine, dq_back)[None]

    far_back, near_back = (
        lax.ppermute(part, ("z_lo", "core"), [(b, a) for a, b in behind(distance)])
        for distance, part in ((2, far_grad), (1, near_grad))
    )

    near_back, query_grad = lax.optimization_barrier((near_back, query_grad))

    copies = combine(own_grad, near_back, far_back, n_y)
    gathered = lax.all_to_all(copies, "y", 0, 0, tiled=True)
    pieces, _ = lax.optimization_barrier((pieces, copies))
    both = [part for piece in pieces for part in (piece, lax.ppermute(piece, "core", swap))]
    n_x = lax.axis_size("x")
    parts = []
    for k in (2, 1, 3):
        term = project(places_ref, both, gathered, n_x, k, jnp.bfloat16)
        parts.append(lax.ppermute(term, "x", [(i, i ^ k) for i in range(n_x)]))
    term = add_parts(project(places_ref, both, gathered, n_x, 0, jnp.float32), parts)
    rest = ("z_hi", "z_lo", "core")
    n_rest = lax.axis_size(rest)
    spread = lax.all_to_all(
        term.reshape(n_rest, term.shape[0] // n_rest, term.shape[1]), rest, 0, 0, tiled=True
    )
    return (query_grad, final_sum(spread))


def solution(mesh):
    axes = ("y", "x", "z_hi", "z_lo", "core")
    fine = Mesh(mesh.devices.reshape(4, 4, 2, 4, 2), axes)
    dp, ctx = axes[:3], axes[3:]
    return jax.shard_map(
        per_device,
        mesh=fine,
        in_specs=(P(dp, ctx, None),) * 5 + (P(dp, None),),
        out_specs=(P(dp, ctx, None), P(axes, None)),
        check_vma=False,
    )
```

```python
import functools

import jax
import jax.numpy as jnp
from jax import lax
from jax.experimental import pallas as pl
from jax.experimental.pallas import tpu as pltpu
from jax.sharding import Mesh, PartitionSpec as P

H = 16
KV = 2
DH = 128
GROUP = H // KV
SCALE = 1.0 / DH**0.5
LOG2E = 1.4426950408889634
REACH = 2
MASKED = -1e30
MIB = 1024 * 1024
SMALL = pltpu.CompilerParams(vmem_limit_bytes=4 * MIB)


def dot_nt(left, right):
    return lax.dot_general(
        left, right, (((1,), (1,)), ((), ())), preferred_element_type=jnp.float32
    )


def dot_nn(left, right):
    return jnp.dot(left, right, preferred_element_type=jnp.float32)


def whole(shape, dtype=jnp.bfloat16):
    return jax.ShapeDtypeStruct(shape, dtype)


HBM = pl.BlockSpec(memory_space=pltpu.HBM)
SCALAR = pl.BlockSpec(memory_space=pltpu.SMEM)


def pair_kernel(keys, values, swapped, out):
    rows = keys.shape[0]
    out[:rows, :DH] = keys[...]
    out[:rows, DH:] = values[...]
    out[rows:] = swapped[...]


def chip_pairs(keys, values, swapped):
    return pl.pallas_call(
        pair_kernel,
        out_shape=whole((2 * keys.shape[0], 2 * DH)),
        compiler_params=SMALL,
        cost_estimate=pl.CostEstimate(flops=0, bytes_accessed=256 * 1024, transcendentals=0),
    )(keys, values, swapped)


def chunk_kernel(place_ref, columns, *refs):
    outs, sems = refs[:-1], refs[-1]
    width = outs[0].shape[1]
    copies = []
    for k, out in enumerate(outs):
        start = pl.multiple_of((place_ref[0] ^ k) * width, width)
        copies.append(pltpu.make_async_copy(columns.at[:, pl.ds(start, width)], out, sems.at[k]))
    for copy in copies:
        copy.start()
    for copy in copies:
        copy.wait()


def split_columns(place, columns, chunks):
    rows, width = columns.shape
    return pl.pallas_call(
        chunk_kernel,
        out_shape=(whole((rows, width // chunks)),) * chunks,
        in_specs=[SCALAR, HBM],
        out_specs=(HBM,) * chunks,
        scratch_shapes=[pltpu.SemaphoreType.DMA((chunks,))],
        compiler_params=SMALL,
        cost_estimate=pl.CostEstimate(flops=0, bytes_accessed=4 * MIB, transcendentals=0),
    )(place, columns)


def bias_kernel(here_ref, docs, out):
    z_lo, core = here_ref[0], here_ref[1]
    rows = out.shape[1] // 2
    chip = 2 * rows
    shape = (rows, rows)
    down = lax.broadcasted_iota(jnp.int32, shape, 0)
    along = lax.broadcasted_iota(jnp.int32, shape, 1)

    def place(distance, which):
        start = (z_lo - distance) * chip + (core ^ which) * rows
        held = pl.ds(pl.multiple_of(jnp.maximum(start, 0), rows), rows)
        return start, jnp.broadcast_to(docs[:, held].astype(jnp.float32), shape)

    queries = [place(0, which) for which in range(2)]
    for block in range(2 * (REACH + 1)):
        key_start, key_row = place(block // 2, block % 2)
        key_doc, key_pos = key_row.T, key_start + down
        for which, (query_start, query_doc) in enumerate(queries):
            allowed = (key_pos >= 0) & (key_pos <= query_start + along) & (key_doc == query_doc)
            out[block * rows : (block + 1) * rows, which * rows : (which + 1) * rows] = jnp.where(
                allowed, 0.0, MASKED
            )


def make_bias(here, docs, rows):
    return pl.pallas_call(
        bias_kernel,
        out_shape=whole((2 * rows * (REACH + 1), 2 * rows), jnp.float32),
        in_specs=[SCALAR, pl.BlockSpec()],
        compiler_params=SMALL,
        cost_estimate=pl.CostEstimate(flops=0, bytes_accessed=MIB, transcendentals=0),
    )(here, docs)


def attention_kernel(
    q_mine, do_mine, q_other, do_other, chip_pair, near_pair, far_pair, bias,
    near_grad, far_grad, score_grads, probs, dk_acc, dv_acc,
):
    pairs = jnp.concatenate([chip_pair[...], near_pair[...], far_pair[...]], axis=0)
    key, value = pairs[:, :DH], pairs[:, DH:]
    chip = chip_pair.shape[0]

    def load(head):
        cols = slice(head * DH, (head + 1) * DH)
        return (
            jnp.concatenate([q_mine[:, cols], q_other[:, cols]], axis=0),
            jnp.concatenate([do_mine[:, cols], do_other[:, cols]], axis=0),
        )

    def products(head):
        query, grad = load(head)
        return dot_nt(key, query), dot_nt(value, grad)

    ahead = products(0)
    for head in range(GROUP):
        raw, prob_grad = ahead
        if head + 1 < GROUP:
            ahead = products(head + 1)
        score = raw * (SCALE * LOG2E) + bias[...]
        top = jnp.max(score, axis=0, keepdims=True)
        weight = jnp.exp2(score - top)
        inverse = 1.0 / jnp.sum(weight, axis=0, keepdims=True)
        prob = weight * inverse
        prob_half = prob.astype(jnp.bfloat16)
        delta = jnp.sum(prob_half.astype(jnp.float32) * prob_grad, axis=0, keepdims=True)
        score_grad = (prob * (prob_grad - delta) * SCALE).astype(jnp.bfloat16)
        score_grads[head] = score_grad
        probs[head] = prob_half[:chip]
        query, grad = load(head)
        dk = dot_nn(score_grad[chip:], query)
        dv = dot_nn(prob_half[chip:], grad)
        if head == 0:
            dk_acc[...] = dk
            dv_acc[...] = dv
        else:
            dk_acc[...] += dk
            dv_acc[...] += dv
    for out, start in ((near_grad, 0), (far_grad, chip)):
        out[:, :DH] = dk_acc[start : start + chip].astype(jnp.bfloat16)
        out[:, DH:] = dv_acc[start : start + chip].astype(jnp.bfloat16)


def attention(operands, bias):
    rows = operands[0].shape[0]
    chip = 2 * rows
    keys = chip * (REACH + 1)
    return pl.pallas_call(
        attention_kernel,
        out_shape=(
            whole((chip, 2 * DH)),
            whole((chip, 2 * DH)),
            whole((GROUP, keys, chip)),
            whole((GROUP, chip, chip)),
        ),
        scratch_shapes=[
            pltpu.VMEM((keys - chip, DH), jnp.float32),
            pltpu.VMEM((keys - chip, DH), jnp.float32),
        ],
        compiler_params=pltpu.CompilerParams(vmem_limit_bytes=24 * MIB),
        cost_estimate=pl.CostEstimate(
            flops=40 * keys * chip * DH * GROUP,
            bytes_accessed=4 * MIB,
            transcendentals=keys * chip * GROUP,
        ),
    )(*operands, bias)


def own_kernel(
    q_mine, do_mine, q_other, do_other, chip_pair, near_pair, far_pair, score_grads, probs,
    dq_mine, dq_other, own_grad,
):
    key_t = jnp.concatenate([ref[:, :DH] for ref in (chip_pair, near_pair, far_pair)], axis=0).T
    rows, chip = q_mine.shape[0], chip_pair.shape[0]
    for head in range(GROUP):
        cols = slice(head * DH, (head + 1) * DH)
        query = jnp.concatenate([q_mine[:, cols], q_other[:, cols]], axis=0)
        grad = jnp.concatenate([do_mine[:, cols], do_other[:, cols]], axis=0)
        dq = dot_nn(key_t, score_grads[head]).T.astype(jnp.bfloat16)
        dq_mine[:, cols] = dq[:rows]
        dq_other[:, cols] = dq[rows:]
        dk = dot_nn(score_grads[head, :chip], query)
        dv = dot_nn(probs[head], grad)
        if head == 0:
            own_grad[:, :DH] = dk
            own_grad[:, DH:] = dv
        else:
            own_grad[:, :DH] += dk
            own_grad[:, DH:] += dv


def own_gradients(operands, score_grads, probs):
    rows = operands[0].shape[0]
    chip = 2 * rows
    return pl.pallas_call(
        own_kernel,
        out_shape=(
            whole((rows, GROUP * DH)),
            whole((rows, GROUP * DH)),
            whole((chip, 2 * DH), jnp.float32),
        ),
        compiler_params=pltpu.CompilerParams(vmem_limit_bytes=24 * MIB),
        cost_estimate=pl.CostEstimate(
            flops=6 * score_grads.size * DH, bytes_accessed=6 * MIB, transcendentals=0
        ),
    )(*operands, score_grads, probs)


def combine_kernel(own, near, far, out):
    total = own[...] + near[...].astype(jnp.float32) + far[...].astype(jnp.float32)
    turned = total.T.astype(jnp.bfloat16)
    for i in range(out.shape[0]):
        out[i] = turned


def combine(own, near, far, copies):
    return pl.pallas_call(
        combine_kernel,
        out_shape=whole((copies, own.shape[1], own.shape[0])),
        compiler_params=SMALL,
        cost_estimate=pl.CostEstimate(flops=0, bytes_accessed=2 * 1024 * 1024, transcendentals=0),
    )(own, near, far)


def assemble_kernel(here_ref, mine, other, out):
    width = mine.shape[1]
    core = here_ref[1]
    out[:, pl.ds(pl.multiple_of(core * width, width), width)] = mine[...]
    out[:, pl.ds(pl.multiple_of((1 - core) * width, width), width)] = other[...]


def assemble(here, mine, other):
    return pl.pallas_call(
        assemble_kernel,
        out_shape=whole((mine.shape[0], 2 * mine.shape[1])),
        in_specs=[SCALAR, pl.BlockSpec(), pl.BlockSpec()],
        compiler_params=SMALL,
        cost_estimate=pl.CostEstimate(flops=0, bytes_accessed=MIB, transcendentals=0),
    )(here, mine, other)


def project_kernel(places_ref, *refs, offset):
    pieces, grads, out = refs[:-2], refs[-2], refs[-1]
    step = out.shape[0]
    columns = pl.ds(pl.multiple_of((places_ref[1] ^ offset) * step, step), step)
    left = jnp.concatenate([grads[places_ref[0] ^ k] for k in range(len(pieces) // 2)], axis=1)
    right = jnp.concatenate([ref[:, columns] for ref in pieces], axis=0)
    out[...] = dot_nn(left, right).T.astype(out.dtype)


def project(places, pieces, grads, blocks, offset, dtype):
    rows, columns = pieces[0].shape
    width = grads.shape[1]
    step = columns // blocks
    return pl.pallas_call(
        functools.partial(project_kernel, offset=offset),
        out_shape=whole((step, width), dtype),
        in_specs=[SCALAR] + [pl.BlockSpec()] * (len(pieces) + 1),
        compiler_params=pltpu.CompilerParams(vmem_limit_bytes=16 * MIB),
        cost_estimate=pl.CostEstimate(
            flops=2 * len(pieces) * rows * step * width,
            bytes_accessed=2 * MIB,
            transcendentals=0,
        ),
    )(places, *pieces, grads)


def add_kernel(*refs):
    total = refs[0][...]
    for ref in refs[1:-1]:
        total = total + ref[...].astype(jnp.float32)
    refs[-1][...] = total.astype(jnp.bfloat16)


def add_parts(own, parts):
    return pl.pallas_call(
        add_kernel,
        out_shape=whole(own.shape),
        compiler_params=SMALL,
        cost_estimate=pl.CostEstimate(flops=0, bytes_accessed=2 * MIB, transcendentals=0),
    )(own, *parts)


def final_kernel(parts, out):
    for head in range(KV):
        total = parts[head].astype(jnp.float32)
        for i in range(1, parts.shape[0] // KV):
            total = total + parts[KV * i + head].astype(jnp.float32)
        out[:, head * DH : (head + 1) * DH] = total[:, :DH]
        out[:, (KV + head) * DH : (KV + head + 1) * DH] = total[:, DH:]


def final_sum(parts):
    return pl.pallas_call(
        final_kernel,
        out_shape=whole((parts.shape[1], 2 * KV * DH), jnp.float32),
        compiler_params=SMALL,
        cost_estimate=pl.CostEstimate(flops=0, bytes_accessed=512 * 1024, transcendentals=0),
    )(parts)


def per_device(queries, keys, values, out_grad, layer_input, segment_ids):
    rows = queries.shape[1]
    chip = 2 * rows
    z_lo = lax.axis_index("z_lo")
    core = lax.axis_index("core")
    n_chips = lax.axis_size("z_lo")
    swap = [(0, 1), (1, 0)]
    here_ref = jnp.stack([z_lo, core]).astype(jnp.int32)
    places_ref = jnp.stack([lax.axis_index("y"), lax.axis_index("x")]).astype(jnp.int32)

    def half_of(array, which):
        width = array.shape[-1] // 2
        return lax.dynamic_slice_in_dim(array[0], which * width, width, 1)

    k_mine, v_mine = half_of(keys, core), half_of(values, core)
    chip_pair = chip_pairs(
        k_mine,
        v_mine,
        lax.ppermute(
            jnp.concatenate([half_of(keys, 1 - core), half_of(values, 1 - core)], axis=1), "core", swap
        ),
    )
    q_mine, do_mine = half_of(queries, core), half_of(out_grad, core)
    q_out, do_out = half_of(queries, 1 - core), half_of(out_grad, 1 - core)
    q_out, do_out, _ = lax.optimization_barrier((q_out, do_out, chip_pair))
    q_other, do_other = (lax.ppermute(part, "core", swap) for part in (q_out, do_out))

    def behind(distance):
        return [
            (chip_at * 2 + c, (chip_at + distance) * 2 + c)
            for chip_at in range(n_chips - distance)
            for c in range(2)
        ]

    blocks = [chip_pair] + [
        lax.ppermute(chip_pair, ("z_lo", "core"), behind(distance)) for distance in (2, 1)
    ][::-1]

    n_y = lax.axis_size("y")
    chunks = split_columns(places_ref, layer_input[0], n_y)
    chunks, _ = lax.optimization_barrier((chunks, (q_other, do_other)))
    pieces = [chunks[0]] + [
        lax.ppermute(chunks[k], "y", [(i, i ^ k) for i in range(n_y)]) for k in range(1, n_y)
    ]

    operands = (q_mine, do_mine, q_other, do_other, *blocks)
    near_grad, far_grad, score_grads, probs = attention(
        operands, make_bias(here_ref, segment_ids, rows)
    )
    dq_mine, dq_other, own_grad = own_gradients(operands, score_grads, probs)
    far_back, near_back = (
        lax.ppermute(part, ("z_lo", "core"), [(b, a) for a, b in behind(distance)])
        for distance, part in ((2, far_grad), (1, near_grad))
    )

    copies = combine(own_grad, near_back, far_back, n_y)
    gathered = lax.all_to_all(copies, "y", 0, 0, tiled=True)
    pieces, _ = lax.optimization_barrier((pieces, copies))
    both = [part for piece in pieces for part in (piece, lax.ppermute(piece, "core", swap))]
    n_x = lax.axis_size("x")
    dq_other, gathered = lax.optimization_barrier((dq_other, gathered))
    dq_back = lax.ppermute(dq_other, "core", swap)
    query_grad = assemble(here_ref, dq_mine, dq_back)[None]
    parts = []
    for k in (3, 1, 2):
        term = project(places_ref, both, gathered, n_x, k, jnp.bfloat16)
        parts.append(lax.ppermute(term, "x", [(i, i ^ k) for i in range(n_x)]))
    own_term = project(places_ref, both, gathered, n_x, 0, jnp.float32)
    parts, query_grad = lax.optimization_barrier((parts, query_grad))
    term = add_parts(own_term, parts)
    rest = ("z_hi", "z_lo", "core")
    n_rest = lax.axis_size(rest)
    spread = lax.all_to_all(
        term.reshape(n_rest, term.shape[0] // n_rest, term.shape[1]), rest, 0, 0, tiled=True
    )
    return (query_grad, final_sum(spread))


def solution(mesh):
    axes = ("y", "x", "z_hi", "z_lo", "core")
    fine = Mesh(mesh.devices.reshape(4, 4, 2, 4, 2), axes)
    dp, ctx = axes[:3], axes[3:]
    return jax.shard_map(
        per_device,
        mesh=fine,
        in_specs=(P(dp, ctx, None),) * 5 + (P(dp, None),),
        out_specs=(P(dp, ctx, None), P(axes, None)),
        check_vma=False,
    )
```

```python
import functools

import jax
import jax.numpy as jnp
from jax import lax
from jax.experimental import pallas as pl
from jax.experimental.pallas import tpu as pltpu
from jax.sharding import Mesh, PartitionSpec as P

H = 16
KV = 2
DH = 128
GROUP = H // KV
SCALE = 1.0 / DH**0.5
LOG2E = 1.4426950408889634
REACH = 2
MASKED = -1e30
MIB = 1024 * 1024
SMALL = pltpu.CompilerParams(vmem_limit_bytes=4 * MIB)


def dot_nt(left, right):
    return lax.dot_general(
        left, right, (((1,), (1,)), ((), ())), preferred_element_type=jnp.float32
    )


def dot_nn(left, right):
    return jnp.dot(left, right, preferred_element_type=jnp.float32)


def whole(shape, dtype=jnp.bfloat16):
    return jax.ShapeDtypeStruct(shape, dtype)


HBM = pl.BlockSpec(memory_space=pltpu.HBM)
SCALAR = pl.BlockSpec(memory_space=pltpu.SMEM)


def pair_kernel(keys, values, swapped, out):
    rows = keys.shape[0]
    out[:rows, :DH] = keys[...]
    out[:rows, DH:] = values[...]
    out[rows:] = swapped[...]


def chip_pairs(keys, values, swapped):
    return pl.pallas_call(
        pair_kernel,
        out_shape=whole((2 * keys.shape[0], 2 * DH)),
        compiler_params=SMALL,
        cost_estimate=pl.CostEstimate(flops=0, bytes_accessed=256 * 1024, transcendentals=0),
    )(keys, values, swapped)


def chunk_kernel(place_ref, columns, *refs):
    outs, sems = refs[:-1], refs[-1]
    width = outs[0].shape[1]
    copies = []
    for k, out in enumerate(outs):
        start = pl.multiple_of((place_ref[0] ^ k) * width, width)
        copies.append(pltpu.make_async_copy(columns.at[:, pl.ds(start, width)], out, sems.at[k]))
    for copy in copies:
        copy.start()
    for copy in copies:
        copy.wait()


def split_columns(place, columns, chunks):
    rows, width = columns.shape
    return pl.pallas_call(
        chunk_kernel,
        out_shape=(whole((rows, width // chunks)),) * chunks,
        in_specs=[SCALAR, HBM],
        out_specs=(HBM,) * chunks,
        scratch_shapes=[pltpu.SemaphoreType.DMA((chunks,))],
        compiler_params=SMALL,
        cost_estimate=pl.CostEstimate(flops=0, bytes_accessed=4 * MIB, transcendentals=0),
    )(place, columns)


def bias_kernel(here_ref, docs, out):
    z_lo, core = here_ref[0], here_ref[1]
    rows = out.shape[1] // 2
    chip = 2 * rows
    shape = (rows, rows)
    down = lax.broadcasted_iota(jnp.int32, shape, 0)
    along = lax.broadcasted_iota(jnp.int32, shape, 1)

    def place(distance, which):
        start = (z_lo - distance) * chip + (core ^ which) * rows
        held = pl.ds(pl.multiple_of(jnp.maximum(start, 0), rows), rows)
        return start, jnp.broadcast_to(docs[:, held].astype(jnp.float32), shape)

    queries = [place(0, which) for which in range(2)]
    for block in range(2 * (REACH + 1)):
        key_start, key_row = place(block // 2, block % 2)
        key_doc, key_pos = key_row.T, key_start + down
        for which, (query_start, query_doc) in enumerate(queries):
            allowed = (key_pos >= 0) & (key_pos <= query_start + along) & (key_doc == query_doc)
            out[block * rows : (block + 1) * rows, which * rows : (which + 1) * rows] = jnp.where(
                allowed, 0.0, MASKED
            )


def make_bias(here, docs, rows):
    return pl.pallas_call(
        bias_kernel,
        out_shape=whole((2 * rows * (REACH + 1), 2 * rows), jnp.float32),
        in_specs=[SCALAR, pl.BlockSpec()],
        compiler_params=SMALL,
        cost_estimate=pl.CostEstimate(flops=0, bytes_accessed=MIB, transcendentals=0),
    )(here, docs)


def attention_kernel(
    q_mine, do_mine, q_other, do_other, chip_pair, near_pair, far_pair, bias,
    near_grad, far_grad, score_grads, probs, dk_acc, dv_acc,
):
    pairs = jnp.concatenate([chip_pair[...], near_pair[...], far_pair[...]], axis=0)
    key, value = pairs[:, :DH], pairs[:, DH:]
    chip = chip_pair.shape[0]

    def load(head):
        cols = slice(head * DH, (head + 1) * DH)
        return (
            jnp.concatenate([q_mine[:, cols], q_other[:, cols]], axis=0),
            jnp.concatenate([do_mine[:, cols], do_other[:, cols]], axis=0),
        )

    def products(head):
        query, grad = load(head)
        return dot_nt(key, query), dot_nt(value, grad)

    ahead = products(0)
    for head in range(GROUP):
        raw, prob_grad = ahead
        if head + 1 < GROUP:
            ahead = products(head + 1)
        score = raw * (SCALE * LOG2E) + bias[...]
        top = jnp.max(score, axis=0, keepdims=True)
        weight = jnp.exp2(score - top)
        inverse = 1.0 / jnp.sum(weight, axis=0, keepdims=True)
        prob = weight * inverse
        prob_half = prob.astype(jnp.bfloat16)
        delta = jnp.sum(prob_half.astype(jnp.float32) * prob_grad, axis=0, keepdims=True)
        score_grad = (prob * (prob_grad - delta) * SCALE).astype(jnp.bfloat16)
        score_grads[head] = score_grad
        probs[head] = prob_half[:chip]
        query, grad = load(head)
        dk = dot_nn(score_grad[chip:], query)
        dv = dot_nn(prob_half[chip:], grad)
        if head == 0:
            dk_acc[...] = dk
            dv_acc[...] = dv
        else:
            dk_acc[...] += dk
            dv_acc[...] += dv
    for out, start in ((near_grad, 0), (far_grad, chip)):
        out[:, :DH] = dk_acc[start : start + chip].astype(jnp.bfloat16)
        out[:, DH:] = dv_acc[start : start + chip].astype(jnp.bfloat16)


def attention(operands, bias):
    rows = operands[0].shape[0]
    chip = 2 * rows
    keys = chip * (REACH + 1)
    return pl.pallas_call(
        attention_kernel,
        out_shape=(
            whole((chip, 2 * DH)),
            whole((chip, 2 * DH)),
            whole((GROUP, keys, chip)),
            whole((GROUP, chip, chip)),
        ),
        scratch_shapes=[
            pltpu.VMEM((keys - chip, DH), jnp.float32),
            pltpu.VMEM((keys - chip, DH), jnp.float32),
        ],
        compiler_params=pltpu.CompilerParams(vmem_limit_bytes=24 * MIB),
        cost_estimate=pl.CostEstimate(
            flops=40 * keys * chip * DH * GROUP,
            bytes_accessed=4 * MIB,
            transcendentals=keys * chip * GROUP,
        ),
    )(*operands, bias)


def own_kernel(
    q_mine, do_mine, q_other, do_other, chip_pair, near_pair, far_pair, score_grads, probs,
    dq_mine, dq_other, own_grad,
):
    key_t = jnp.concatenate([ref[:, :DH] for ref in (chip_pair, near_pair, far_pair)], axis=0).T
    rows, chip = q_mine.shape[0], chip_pair.shape[0]
    for head in range(GROUP):
        cols = slice(head * DH, (head + 1) * DH)
        query = jnp.concatenate([q_mine[:, cols], q_other[:, cols]], axis=0)
        grad = jnp.concatenate([do_mine[:, cols], do_other[:, cols]], axis=0)
        dq = dot_nn(key_t, score_grads[head]).T.astype(jnp.bfloat16)
        dq_mine[:, cols] = dq[:rows]
        dq_other[:, cols] = dq[rows:]
        dk = dot_nn(score_grads[head, :chip], query)
        dv = dot_nn(probs[head], grad)
        if head == 0:
            own_grad[:, :DH] = dk
            own_grad[:, DH:] = dv
        else:
            own_grad[:, :DH] += dk
            own_grad[:, DH:] += dv


def own_gradients(operands, score_grads, probs):
    rows = operands[0].shape[0]
    chip = 2 * rows
    return pl.pallas_call(
        own_kernel,
        out_shape=(
            whole((rows, GROUP * DH)),
            whole((rows, GROUP * DH)),
            whole((chip, 2 * DH), jnp.float32),
        ),
        compiler_params=pltpu.CompilerParams(vmem_limit_bytes=24 * MIB),
        cost_estimate=pl.CostEstimate(
            flops=6 * score_grads.size * DH, bytes_accessed=6 * MIB, transcendentals=0
        ),
    )(*operands, score_grads, probs)


def combine_kernel(own, near, far, out):
    total = own[...] + near[...].astype(jnp.float32) + far[...].astype(jnp.float32)
    out[...] = total.T.astype(jnp.bfloat16)


def combine(own, near, far):
    return pl.pallas_call(
        combine_kernel,
        out_shape=whole((own.shape[1], own.shape[0])),
        compiler_params=SMALL,
        cost_estimate=pl.CostEstimate(flops=0, bytes_accessed=MIB, transcendentals=0),
    )(own, near, far)


def stack_kernel(*refs):
    for i, ref in enumerate(refs[:-1]):
        refs[-1][i] = ref[...]


def stack(pieces):
    return pl.pallas_call(
        stack_kernel,
        out_shape=whole((len(pieces),) + pieces[0].shape),
        compiler_params=pltpu.CompilerParams(vmem_limit_bytes=16 * MIB),
        cost_estimate=pl.CostEstimate(flops=0, bytes_accessed=4 * MIB, transcendentals=0),
    )(*pieces)


def assemble_kernel(here_ref, mine, other, out):
    width = mine.shape[1]
    core = here_ref[1]
    out[:, pl.ds(pl.multiple_of(core * width, width), width)] = mine[...]
    out[:, pl.ds(pl.multiple_of((1 - core) * width, width), width)] = other[...]


def assemble(here, mine, other):
    return pl.pallas_call(
        assemble_kernel,
        out_shape=whole((mine.shape[0], 2 * mine.shape[1])),
        in_specs=[SCALAR, pl.BlockSpec(), pl.BlockSpec()],
        compiler_params=SMALL,
        cost_estimate=pl.CostEstimate(flops=0, bytes_accessed=MIB, transcendentals=0),
    )(here, mine, other)


def project_kernel(places_ref, mine, other, *refs, offset):
    grads, out = refs[:-1], refs[-1]
    step = out.shape[0]
    columns = pl.ds(pl.multiple_of((places_ref[1] ^ offset) * step, step), step)
    left = jnp.concatenate([ref[...] for ref in grads], axis=1)
    right = jnp.concatenate(
        [ref[k, :, columns] for k in range(len(grads)) for ref in (mine, other)], axis=0
    )
    out[...] = dot_nn(left, right).T.astype(out.dtype)


def project(places, mine, other, grads, blocks, offset, dtype):
    rows, columns = mine.shape[1:]
    width = grads[0].shape[0]
    step = columns // blocks
    return pl.pallas_call(
        functools.partial(project_kernel, offset=offset),
        out_shape=whole((step, width), dtype),
        in_specs=[SCALAR] + [pl.BlockSpec()] * (len(grads) + 2),
        compiler_params=pltpu.CompilerParams(vmem_limit_bytes=16 * MIB),
        cost_estimate=pl.CostEstimate(
            flops=4 * len(grads) * rows * step * width,
            bytes_accessed=2 * MIB,
            transcendentals=0,
        ),
    )(places, mine, other, *grads)


def add_kernel(*refs):
    total = refs[0][...]
    for ref in refs[1:-1]:
        total = total + ref[...].astype(jnp.float32)
    refs[-1][...] = total.astype(jnp.bfloat16)


def add_parts(own, parts):
    return pl.pallas_call(
        add_kernel,
        out_shape=whole(own.shape),
        compiler_params=SMALL,
        cost_estimate=pl.CostEstimate(flops=0, bytes_accessed=2 * MIB, transcendentals=0),
    )(own, *parts)


def final_kernel(parts, out):
    for head in range(KV):
        total = parts[head].astype(jnp.float32)
        for i in range(1, parts.shape[0] // KV):
            total = total + parts[KV * i + head].astype(jnp.float32)
        out[:, head * DH : (head + 1) * DH] = total[:, :DH]
        out[:, (KV + head) * DH : (KV + head + 1) * DH] = total[:, DH:]


def final_sum(parts):
    return pl.pallas_call(
        final_kernel,
        out_shape=whole((parts.shape[1], 2 * KV * DH), jnp.float32),
        compiler_params=SMALL,
        cost_estimate=pl.CostEstimate(flops=0, bytes_accessed=512 * 1024, transcendentals=0),
    )(parts)


def per_device(queries, keys, values, out_grad, layer_input, segment_ids):
    rows = queries.shape[1]
    chip = 2 * rows
    z_lo = lax.axis_index("z_lo")
    core = lax.axis_index("core")
    n_chips = lax.axis_size("z_lo")
    swap = [(0, 1), (1, 0)]
    here_ref = jnp.stack([z_lo, core]).astype(jnp.int32)
    places_ref = jnp.stack([lax.axis_index("y"), lax.axis_index("x")]).astype(jnp.int32)

    def half_of(array, which):
        width = array.shape[-1] // 2
        return lax.dynamic_slice_in_dim(array[0], which * width, width, 1)

    k_mine, v_mine = half_of(keys, core), half_of(values, core)
    chip_pair = chip_pairs(
        k_mine,
        v_mine,
        lax.ppermute(
            jnp.concatenate([half_of(keys, 1 - core), half_of(values, 1 - core)], axis=1), "core", swap
        ),
    )
    q_mine, do_mine = half_of(queries, core), half_of(out_grad, core)
    q_out, do_out = half_of(queries, 1 - core), half_of(out_grad, 1 - core)
    q_out, do_out, _ = lax.optimization_barrier((q_out, do_out, chip_pair))
    q_other, do_other = (lax.ppermute(part, "core", swap) for part in (q_out, do_out))

    def behind(distance):
        return [
            (chip_at * 2 + c, (chip_at + distance) * 2 + c)
            for chip_at in range(n_chips - distance)
            for c in range(2)
        ]

    blocks = [chip_pair] + [
        lax.ppermute(chip_pair, ("z_lo", "core"), behind(distance)) for distance in (2, 1)
    ][::-1]

    n_y = lax.axis_size("y")
    chunks = split_columns(places_ref, layer_input[0], n_y)
    chunks, _ = lax.optimization_barrier((chunks, (q_other, do_other)))
    pieces = [chunks[0]] + [
        lax.ppermute(chunks[k], "y", [(i, i ^ k) for i in range(n_y)]) for k in range(1, n_y)
    ]
    docs, _ = lax.optimization_barrier((segment_ids, chunks[0]))

    operands = (q_mine, do_mine, q_other, do_other, *blocks)
    near_grad, far_grad, score_grads, probs = attention(
        operands, make_bias(here_ref, docs, rows)
    )
    dq_mine, dq_other, own_grad = own_gradients(operands, score_grads, probs)
    far_back, near_back = (
        lax.ppermute(part, ("z_lo", "core"), [(b, a) for a, b in behind(distance)])
        for distance, part in ((2, far_grad), (1, near_grad))
    )

    def along_y(part, k):
        return lax.ppermute(part, "y", [(i, i ^ k) for i in range(n_y)])

    grad = combine(own_grad, near_back, far_back)
    grads = [grad] + [along_y(grad, k) for k in range(1, n_y)]
    pieces, grads[1:3] = lax.optimization_barrier((pieces, grads[1:3]))
    mine = stack(pieces)
    other = lax.ppermute(mine, "core", swap)
    n_x = lax.axis_size("x")
    dq_other, grads = lax.optimization_barrier((dq_other, grads))
    dq_back = lax.ppermute(dq_other, "core", swap)
    query_grad = assemble(here_ref, dq_mine, dq_back)[None]
    parts = []
    for k in (3, 1, 2):
        term = project(places_ref, mine, other, grads, n_x, k, jnp.bfloat16)
        parts.append(lax.ppermute(term, "x", [(i, i ^ k) for i in range(n_x)]))
    own_term = project(places_ref, mine, other, grads, n_x, 0, jnp.float32)
    parts, query_grad = lax.optimization_barrier((parts, query_grad))
    term = add_parts(own_term, parts)
    rest = ("z_hi", "z_lo", "core")
    n_rest = lax.axis_size(rest)
    spread = lax.all_to_all(
        term.reshape(n_rest, term.shape[0] // n_rest, term.shape[1]), rest, 0, 0, tiled=True
    )
    return (query_grad, final_sum(spread))


def solution(mesh):
    axes = ("y", "x", "z_hi", "z_lo", "core")
    fine = Mesh(mesh.devices.reshape(4, 4, 2, 4, 2), axes)
    dp, ctx = axes[:3], axes[3:]
    return jax.shard_map(
        per_device,
        mesh=fine,
        in_specs=(P(dp, ctx, None),) * 5 + (P(dp, None),),
        out_specs=(P(dp, ctx, None), P(axes, None)),
        check_vma=False,
    )
```

```python
import functools

import jax
import jax.numpy as jnp
from jax import lax
from jax.experimental import pallas as pl
from jax.experimental.pallas import tpu as pltpu
from jax.sharding import Mesh, PartitionSpec as P

H = 16
KV = 2
DH = 128
GROUP = H // KV
SCALE = 1.0 / DH**0.5
LOG2E = 1.4426950408889634
REACH = 2
MASKED = -1e30
MIB = 1024 * 1024
SMALL = pltpu.CompilerParams(vmem_limit_bytes=4 * MIB)


def dot_nt(left, right):
    return lax.dot_general(
        left, right, (((1,), (1,)), ((), ())), preferred_element_type=jnp.float32
    )


def dot_nn(left, right):
    return jnp.dot(left, right, preferred_element_type=jnp.float32)


def whole(shape, dtype=jnp.bfloat16):
    return jax.ShapeDtypeStruct(shape, dtype)


HBM = pl.BlockSpec(memory_space=pltpu.HBM)
SCALAR = pl.BlockSpec(memory_space=pltpu.SMEM)


def pair_kernel(keys, values, swapped, out):
    rows = keys.shape[0]
    out[:rows, :DH] = keys[...]
    out[:rows, DH:] = values[...]
    out[rows:] = swapped[...]


def chip_pairs(keys, values, swapped):
    return pl.pallas_call(
        pair_kernel,
        out_shape=whole((2 * keys.shape[0], 2 * DH)),
        compiler_params=SMALL,
        cost_estimate=pl.CostEstimate(flops=0, bytes_accessed=256 * 1024, transcendentals=0),
    )(keys, values, swapped)


def chunk_kernel(place_ref, columns, *refs):
    outs, sems = refs[:-1], refs[-1]
    width = outs[0].shape[1]
    copies = []
    for k, out in enumerate(outs):
        start = pl.multiple_of((place_ref[0] ^ k) * width, width)
        copies.append(pltpu.make_async_copy(columns.at[:, pl.ds(start, width)], out, sems.at[k]))
    for copy in copies:
        copy.start()
    for copy in copies:
        copy.wait()


def split_columns(place, columns, chunks):
    rows, width = columns.shape
    return pl.pallas_call(
        chunk_kernel,
        out_shape=(whole((rows, width // chunks)),) * chunks,
        in_specs=[SCALAR, HBM],
        out_specs=(HBM,) * chunks,
        scratch_shapes=[pltpu.SemaphoreType.DMA((chunks,))],
        compiler_params=SMALL,
        cost_estimate=pl.CostEstimate(flops=0, bytes_accessed=4 * MIB, transcendentals=0),
    )(place, columns)


def bias_kernel(here_ref, docs, out):
    z_lo, core = here_ref[0], here_ref[1]
    rows = out.shape[1] // 2
    chip = 2 * rows
    shape = (rows, rows)
    down = lax.broadcasted_iota(jnp.int32, shape, 0)
    along = lax.broadcasted_iota(jnp.int32, shape, 1)

    def place(distance, which):
        start = (z_lo - distance) * chip + (core ^ which) * rows
        held = pl.ds(pl.multiple_of(jnp.maximum(start, 0), rows), rows)
        return start, jnp.broadcast_to(docs[:, held].astype(jnp.float32), shape)

    queries = [place(0, which) for which in range(2)]
    for block in range(2 * (REACH + 1)):
        key_start, key_row = place(block // 2, block % 2)
        key_doc, key_pos = key_row.T, key_start + down
        for which, (query_start, query_doc) in enumerate(queries):
            allowed = (key_pos >= 0) & (key_pos <= query_start + along) & (key_doc == query_doc)
            out[block * rows : (block + 1) * rows, which * rows : (which + 1) * rows] = jnp.where(
                allowed, 0.0, MASKED
            )


def make_bias(here, docs, rows):
    return pl.pallas_call(
        bias_kernel,
        out_shape=whole((2 * rows * (REACH + 1), 2 * rows), jnp.float32),
        in_specs=[SCALAR, pl.BlockSpec()],
        compiler_params=SMALL,
        cost_estimate=pl.CostEstimate(flops=0, bytes_accessed=MIB, transcendentals=0),
    )(here, docs)


def attention_kernel(
    q_mine, do_mine, q_other, do_other, chip_pair, near_pair, far_pair, bias,
    near_grad, far_grad, score_grads, probs, dk_acc, dv_acc,
):
    pairs = jnp.concatenate([chip_pair[...], near_pair[...], far_pair[...]], axis=0)
    key, value = pairs[:, :DH], pairs[:, DH:]
    chip = chip_pair.shape[0]

    def load(head):
        cols = slice(head * DH, (head + 1) * DH)
        return (
            jnp.concatenate([q_mine[:, cols], q_other[:, cols]], axis=0),
            jnp.concatenate([do_mine[:, cols], do_other[:, cols]], axis=0),
        )

    def products(head):
        query, grad = load(head)
        return dot_nt(key, query), dot_nt(value, grad)

    ahead = products(0)
    for head in range(GROUP):
        raw, prob_grad = ahead
        if head + 1 < GROUP:
            ahead = products(head + 1)
        score = raw * (SCALE * LOG2E) + bias[...]
        top = jnp.max(score, axis=0, keepdims=True)
        weight = jnp.exp2(score - top)
        inverse = 1.0 / jnp.sum(weight, axis=0, keepdims=True)
        prob = weight * inverse
        prob_half = prob.astype(jnp.bfloat16)
        delta = jnp.sum(prob_half.astype(jnp.float32) * prob_grad, axis=0, keepdims=True)
        score_grad = (prob * (prob_grad - delta) * SCALE).astype(jnp.bfloat16)
        score_grads[head] = score_grad
        probs[head] = prob_half[:chip]
        query, grad = load(head)
        dk = dot_nn(score_grad[chip:], query)
        dv = dot_nn(prob_half[chip:], grad)
        if head == 0:
            dk_acc[...] = dk
            dv_acc[...] = dv
        else:
            dk_acc[...] += dk
            dv_acc[...] += dv
    for out, start in ((near_grad, 0), (far_grad, chip)):
        out[:, :DH] = dk_acc[start : start + chip].astype(jnp.bfloat16)
        out[:, DH:] = dv_acc[start : start + chip].astype(jnp.bfloat16)


def attention(operands, bias):
    rows = operands[0].shape[0]
    chip = 2 * rows
    keys = chip * (REACH + 1)
    return pl.pallas_call(
        attention_kernel,
        out_shape=(
            whole((chip, 2 * DH)),
            whole((chip, 2 * DH)),
            whole((GROUP, keys, chip)),
            whole((GROUP, chip, chip)),
        ),
        scratch_shapes=[
            pltpu.VMEM((keys - chip, DH), jnp.float32),
            pltpu.VMEM((keys - chip, DH), jnp.float32),
        ],
        compiler_params=pltpu.CompilerParams(vmem_limit_bytes=24 * MIB),
        cost_estimate=pl.CostEstimate(
            flops=40 * keys * chip * DH * GROUP,
            bytes_accessed=4 * MIB,
            transcendentals=keys * chip * GROUP,
        ),
    )(*operands, bias)


def own_kernel(
    q_mine, do_mine, q_other, do_other, chip_pair, near_pair, far_pair, score_grads, probs,
    dq_mine, dq_other, own_grad,
):
    key_t = jnp.concatenate([ref[:, :DH] for ref in (chip_pair, near_pair, far_pair)], axis=0).T
    rows, chip = q_mine.shape[0], chip_pair.shape[0]
    for head in range(GROUP):
        cols = slice(head * DH, (head + 1) * DH)
        query = jnp.concatenate([q_mine[:, cols], q_other[:, cols]], axis=0)
        grad = jnp.concatenate([do_mine[:, cols], do_other[:, cols]], axis=0)
        dq = dot_nn(key_t, score_grads[head]).T.astype(jnp.bfloat16)
        dq_mine[:, cols] = dq[:rows]
        dq_other[:, cols] = dq[rows:]
        dk = dot_nn(score_grads[head, :chip], query)
        dv = dot_nn(probs[head], grad)
        if head == 0:
            own_grad[:, :DH] = dk
            own_grad[:, DH:] = dv
        else:
            own_grad[:, :DH] += dk
            own_grad[:, DH:] += dv


def own_gradients(operands, score_grads, probs):
    rows = operands[0].shape[0]
    chip = 2 * rows
    return pl.pallas_call(
        own_kernel,
        out_shape=(
            whole((rows, GROUP * DH)),
            whole((rows, GROUP * DH)),
            whole((chip, 2 * DH), jnp.float32),
        ),
        compiler_params=pltpu.CompilerParams(vmem_limit_bytes=24 * MIB),
        cost_estimate=pl.CostEstimate(
            flops=6 * score_grads.size * DH, bytes_accessed=6 * MIB, transcendentals=0
        ),
    )(*operands, score_grads, probs)


def combine_kernel(own, near, far, out):
    total = own[...] + near[...].astype(jnp.float32) + far[...].astype(jnp.float32)
    out[...] = total.T.astype(jnp.bfloat16)


def combine(own, near, far):
    return pl.pallas_call(
        combine_kernel,
        out_shape=whole((own.shape[1], own.shape[0])),
        compiler_params=SMALL,
        cost_estimate=pl.CostEstimate(flops=0, bytes_accessed=MIB, transcendentals=0),
    )(own, near, far)


def stack_kernel(*refs):
    for i, ref in enumerate(refs[:-1]):
        refs[-1][i] = ref[...]


def stack(pieces):
    return pl.pallas_call(
        stack_kernel,
        out_shape=whole((len(pieces),) + pieces[0].shape),
        compiler_params=pltpu.CompilerParams(vmem_limit_bytes=16 * MIB),
        cost_estimate=pl.CostEstimate(flops=0, bytes_accessed=4 * MIB, transcendentals=0),
    )(*pieces)


def assemble_kernel(here_ref, mine, other, out):
    width = mine.shape[1]
    core = here_ref[1]
    out[:, pl.ds(pl.multiple_of(core * width, width), width)] = mine[...]
    out[:, pl.ds(pl.multiple_of((1 - core) * width, width), width)] = other[...]


def assemble(here, mine, other):
    return pl.pallas_call(
        assemble_kernel,
        out_shape=whole((mine.shape[0], 2 * mine.shape[1])),
        in_specs=[SCALAR, pl.BlockSpec(), pl.BlockSpec()],
        compiler_params=SMALL,
        cost_estimate=pl.CostEstimate(flops=0, bytes_accessed=MIB, transcendentals=0),
    )(here, mine, other)


def project_kernel(places_ref, mine, other, *refs, offset):
    grads, out = refs[:-1], refs[-1]
    step = out.shape[0]
    columns = pl.ds(pl.multiple_of((places_ref[1] ^ offset) * step, step), step)
    left = jnp.concatenate([ref[...] for ref in grads], axis=1)
    right = jnp.concatenate(
        [ref[k, :, columns] for k in range(len(grads)) for ref in (mine, other)], axis=0
    )
    out[...] = dot_nn(left, right).T.astype(out.dtype)


def project(places, mine, other, grads, blocks, offset, dtype):
    rows, columns = mine.shape[1:]
    width = grads[0].shape[0]
    step = columns // blocks
    return pl.pallas_call(
        functools.partial(project_kernel, offset=offset),
        out_shape=whole((step, width), dtype),
        in_specs=[SCALAR] + [pl.BlockSpec()] * (len(grads) + 2),
        compiler_params=pltpu.CompilerParams(vmem_limit_bytes=16 * MIB),
        cost_estimate=pl.CostEstimate(
            flops=4 * len(grads) * rows * step * width,
            bytes_accessed=2 * MIB,
            transcendentals=0,
        ),
    )(places, mine, other, *grads)


def add_kernel(*refs):
    total = refs[0][...]
    for ref in refs[1:-1]:
        total = total + ref[...].astype(jnp.float32)
    refs[-1][...] = total.astype(jnp.bfloat16)


def add_parts(own, parts):
    return pl.pallas_call(
        add_kernel,
        out_shape=whole(own.shape),
        compiler_params=SMALL,
        cost_estimate=pl.CostEstimate(flops=0, bytes_accessed=2 * MIB, transcendentals=0),
    )(own, *parts)


def final_kernel(parts, out):
    for head in range(KV):
        total = parts[head].astype(jnp.float32)
        for i in range(1, parts.shape[0] // KV):
            total = total + parts[KV * i + head].astype(jnp.float32)
        out[:, head * DH : (head + 1) * DH] = total[:, :DH]
        out[:, (KV + head) * DH : (KV + head + 1) * DH] = total[:, DH:]


def final_sum(parts):
    return pl.pallas_call(
        final_kernel,
        out_shape=whole((parts.shape[1], 2 * KV * DH), jnp.float32),
        compiler_params=SMALL,
        cost_estimate=pl.CostEstimate(flops=0, bytes_accessed=512 * 1024, transcendentals=0),
    )(parts)


def per_device(queries, keys, values, out_grad, layer_input, segment_ids):
    rows = queries.shape[1]
    chip = 2 * rows
    z_lo = lax.axis_index("z_lo")
    core = lax.axis_index("core")
    n_chips = lax.axis_size("z_lo")
    swap = [(0, 1), (1, 0)]
    here_ref = jnp.stack([z_lo, core]).astype(jnp.int32)
    places_ref = jnp.stack([lax.axis_index("y"), lax.axis_index("x")]).astype(jnp.int32)

    def half_of(array, which):
        width = array.shape[-1] // 2
        return lax.dynamic_slice_in_dim(array[0], which * width, width, 1)

    k_mine, v_mine = half_of(keys, core), half_of(values, core)
    chip_pair = chip_pairs(
        k_mine,
        v_mine,
        lax.ppermute(
            jnp.concatenate([half_of(keys, 1 - core), half_of(values, 1 - core)], axis=1), "core", swap
        ),
    )
    q_mine, do_mine = half_of(queries, core), half_of(out_grad, core)
    q_out, do_out = half_of(queries, 1 - core), half_of(out_grad, 1 - core)
    q_out, do_out, _ = lax.optimization_barrier((q_out, do_out, chip_pair))
    q_other, do_other = (lax.ppermute(part, "core", swap) for part in (q_out, do_out))

    def behind(distance):
        return [
            (chip_at * 2 + c, (chip_at + distance) * 2 + c)
            for chip_at in range(n_chips - distance)
            for c in range(2)
        ]

    blocks = [chip_pair] + [
        lax.ppermute(chip_pair, ("z_lo", "core"), behind(distance)) for distance in (2, 1)
    ][::-1]

    n_y = lax.axis_size("y")
    chunks = split_columns(places_ref, layer_input[0], n_y)
    chunks, _ = lax.optimization_barrier((chunks, (q_other, do_other)))
    pieces = [chunks[0]] + [
        lax.ppermute(chunks[k], "y", [(i, i ^ k) for i in range(n_y)]) for k in range(1, n_y)
    ]
    docs, _ = lax.optimization_barrier((segment_ids, chunks[0]))

    operands = (q_mine, do_mine, q_other, do_other, *blocks)
    near_grad, far_grad, score_grads, probs = attention(
        operands, make_bias(here_ref, docs, rows)
    )
    dq_mine, dq_other, own_grad = own_gradients(operands, score_grads, probs)
    far_back, near_back = (
        lax.ppermute(part, ("z_lo", "core"), [(b, a) for a, b in behind(distance)])
        for distance, part in ((2, far_grad), (1, near_grad))
    )

    def along_y(part, k):
        return lax.ppermute(part, "y", [(i, i ^ k) for i in range(n_y)])

    grad = combine(own_grad, near_back, far_back)
    grads = [grad] + [along_y(grad, k) for k in range(1, n_y)]
    pieces, grads[1] = lax.optimization_barrier((pieces, grads[1]))
    mine = stack(pieces)
    other = lax.ppermute(mine, "core", swap)
    n_x = lax.axis_size("x")
    dq_other, grads = lax.optimization_barrier((dq_other, grads))
    dq_back = lax.ppermute(dq_other, "core", swap)
    query_grad = assemble(here_ref, dq_mine, dq_back)[None]
    parts = []
    for k in (2, 1, 3):
        term = project(places_ref, mine, other, grads, n_x, k, jnp.bfloat16)
        parts.append(lax.ppermute(term, "x", [(i, i ^ k) for i in range(n_x)]))
    own_term = project(places_ref, mine, other, grads, n_x, 0, jnp.float32)
    parts, query_grad = lax.optimization_barrier((parts, query_grad))
    term = add_parts(own_term, parts)
    rest = ("z_hi", "z_lo", "core")
    n_rest = lax.axis_size(rest)
    spread = lax.all_to_all(
        term.reshape(n_rest, term.shape[0] // n_rest, term.shape[1]), rest, 0, 0, tiled=True
    )
    return (query_grad, final_sum(spread))


def solution(mesh):
    axes = ("y", "x", "z_hi", "z_lo", "core")
    fine = Mesh(mesh.devices.reshape(4, 4, 2, 4, 2), axes)
    dp, ctx = axes[:3], axes[3:]
    return jax.shard_map(
        per_device,
        mesh=fine,
        in_specs=(P(dp, ctx, None),) * 5 + (P(dp, None),),
        out_specs=(P(dp, ctx, None), P(axes, None)),
        check_vma=False,
    )
```

```python
import functools

import jax
import jax.numpy as jnp
from jax import lax
from jax.experimental import pallas as pl
from jax.experimental.pallas import tpu as pltpu
from jax.sharding import Mesh, PartitionSpec as P

H = 16
KV = 2
DH = 128
GROUP = H // KV
SCALE = 1.0 / DH**0.5
LOG2E = 1.4426950408889634
REACH = 2
MASKED = -1e30
MIB = 1024 * 1024
SMALL = pltpu.CompilerParams(vmem_limit_bytes=4 * MIB)


def dot_nt(left, right):
    return lax.dot_general(
        left, right, (((1,), (1,)), ((), ())), preferred_element_type=jnp.float32
    )


def dot_nn(left, right):
    return jnp.dot(left, right, preferred_element_type=jnp.float32)


def whole(shape, dtype=jnp.bfloat16):
    return jax.ShapeDtypeStruct(shape, dtype)


HBM = pl.BlockSpec(memory_space=pltpu.HBM)
SCALAR = pl.BlockSpec(memory_space=pltpu.SMEM)


def pair_kernel(keys, values, swapped, out):
    rows = keys.shape[0]
    out[:rows, :DH] = keys[...]
    out[:rows, DH:] = values[...]
    out[rows:] = swapped[...]


def chip_pairs(keys, values, swapped):
    return pl.pallas_call(
        pair_kernel,
        out_shape=whole((2 * keys.shape[0], 2 * DH)),
        compiler_params=SMALL,
        cost_estimate=pl.CostEstimate(flops=0, bytes_accessed=256 * 1024, transcendentals=0),
    )(keys, values, swapped)


def chunk_kernel(places_ref, mine, other, *refs):
    outs, sems = refs[:-1], refs[-1]
    n = len(outs)
    rows, step = mine.shape[0], outs[0].shape[1] // n
    y, x, core = places_ref[0], places_ref[1], places_ref[2]
    copies = []
    for k, out in enumerate(outs):
        for i in range(n):
            block = jnp.where(core == 0, (y ^ k) * n + i, i * n + (x ^ k))
            held = pl.ds(pl.multiple_of(block * step, step), step)
            for half, part in enumerate((mine, other)):
                copies.append(
                    pltpu.make_async_copy(
                        part.at[:, held],
                        out.at[half * rows : (half + 1) * rows, i * step : (i + 1) * step],
                        sems.at[len(copies)],
                    )
                )
    for copy in copies:
        copy.start()
    for copy in copies:
        copy.wait()


def split_columns(places, mine, other, chunks):
    rows, width = mine.shape
    return pl.pallas_call(
        chunk_kernel,
        out_shape=(whole((2 * rows, width // chunks)),) * chunks,
        in_specs=[SCALAR, HBM, HBM],
        out_specs=(HBM,) * chunks,
        scratch_shapes=[pltpu.SemaphoreType.DMA((2 * chunks * chunks,))],
        compiler_params=SMALL,
        cost_estimate=pl.CostEstimate(flops=0, bytes_accessed=8 * MIB, transcendentals=0),
    )(places, mine, other)


def bias_kernel(here_ref, docs, out):
    z_lo, core = here_ref[0], here_ref[1]
    rows = out.shape[1] // 2
    chip = 2 * rows
    shape = (rows, rows)
    down = lax.broadcasted_iota(jnp.int32, shape, 0)
    along = lax.broadcasted_iota(jnp.int32, shape, 1)

    def place(distance, which):
        start = (z_lo - distance) * chip + (core ^ which) * rows
        held = pl.ds(pl.multiple_of(jnp.maximum(start, 0), rows), rows)
        return start, jnp.broadcast_to(docs[:, held].astype(jnp.float32), shape)

    queries = [place(0, which) for which in range(2)]
    for block in range(2 * (REACH + 1)):
        key_start, key_row = place(block // 2, block % 2)
        key_doc, key_pos = key_row.T, key_start + down
        for which, (query_start, query_doc) in enumerate(queries):
            allowed = (key_pos >= 0) & (key_pos <= query_start + along) & (key_doc == query_doc)
            out[block * rows : (block + 1) * rows, which * rows : (which + 1) * rows] = jnp.where(
                allowed, 0.0, MASKED
            )


def make_bias(here, docs, rows):
    return pl.pallas_call(
        bias_kernel,
        out_shape=whole((2 * rows * (REACH + 1), 2 * rows), jnp.float32),
        in_specs=[SCALAR, pl.BlockSpec()],
        compiler_params=SMALL,
        cost_estimate=pl.CostEstimate(flops=0, bytes_accessed=MIB, transcendentals=0),
    )(here, docs)


def attention_kernel(
    q_mine, do_mine, q_other, do_other, chip_pair, near_pair, far_pair, bias,
    near_grad, far_grad, score_grads, probs, dk_acc, dv_acc,
):
    pairs = jnp.concatenate([chip_pair[...], near_pair[...], far_pair[...]], axis=0)
    key, value = pairs[:, :DH], pairs[:, DH:]
    chip = chip_pair.shape[0]

    def load(head):
        cols = slice(head * DH, (head + 1) * DH)
        return (
            jnp.concatenate([q_mine[:, cols], q_other[:, cols]], axis=0),
            jnp.concatenate([do_mine[:, cols], do_other[:, cols]], axis=0),
        )

    def products(head):
        query, grad = load(head)
        return dot_nt(key, query), dot_nt(value, grad)

    ahead = products(0)
    for head in range(GROUP):
        raw, prob_grad = ahead
        if head + 1 < GROUP:
            ahead = products(head + 1)
        score = raw * (SCALE * LOG2E) + bias[...]
        top = jnp.max(score, axis=0, keepdims=True)
        weight = jnp.exp2(score - top)
        inverse = 1.0 / jnp.sum(weight, axis=0, keepdims=True)
        prob = weight * inverse
        prob_half = prob.astype(jnp.bfloat16)
        delta = jnp.sum(prob_half.astype(jnp.float32) * prob_grad, axis=0, keepdims=True)
        score_grad = (prob * (prob_grad - delta) * SCALE).astype(jnp.bfloat16)
        score_grads[head] = score_grad
        probs[head] = prob_half[:chip]
        query, grad = load(head)
        dk = dot_nn(score_grad[chip:], query)
        dv = dot_nn(prob_half[chip:], grad)
        if head == 0:
            dk_acc[...] = dk
            dv_acc[...] = dv
        else:
            dk_acc[...] += dk
            dv_acc[...] += dv
    for out, start in ((near_grad, 0), (far_grad, chip)):
        out[:, :DH] = dk_acc[start : start + chip].astype(jnp.bfloat16)
        out[:, DH:] = dv_acc[start : start + chip].astype(jnp.bfloat16)


def attention(operands, bias):
    rows = operands[0].shape[0]
    chip = 2 * rows
    keys = chip * (REACH + 1)
    return pl.pallas_call(
        attention_kernel,
        out_shape=(
            whole((chip, 2 * DH)),
            whole((chip, 2 * DH)),
            whole((GROUP, keys, chip)),
            whole((GROUP, chip, chip)),
        ),
        scratch_shapes=[
            pltpu.VMEM((keys - chip, DH), jnp.float32),
            pltpu.VMEM((keys - chip, DH), jnp.float32),
        ],
        compiler_params=pltpu.CompilerParams(vmem_limit_bytes=24 * MIB),
        cost_estimate=pl.CostEstimate(
            flops=40 * keys * chip * DH * GROUP,
            bytes_accessed=4 * MIB,
            transcendentals=keys * chip * GROUP,
        ),
    )(*operands, bias)


def own_kernel(
    q_mine, do_mine, q_other, do_other, chip_pair, near_pair, far_pair, score_grads, probs,
    dq_mine, dq_other, own_grad,
):
    key_t = jnp.concatenate([ref[:, :DH] for ref in (chip_pair, near_pair, far_pair)], axis=0).T
    rows, chip = q_mine.shape[0], chip_pair.shape[0]
    for head in range(GROUP):
        cols = slice(head * DH, (head + 1) * DH)
        query = jnp.concatenate([q_mine[:, cols], q_other[:, cols]], axis=0)
        grad = jnp.concatenate([do_mine[:, cols], do_other[:, cols]], axis=0)
        dq = dot_nn(key_t, score_grads[head]).T.astype(jnp.bfloat16)
        dq_mine[:, cols] = dq[:rows]
        dq_other[:, cols] = dq[rows:]
        dk = dot_nn(score_grads[head, :chip], query)
        dv = dot_nn(probs[head], grad)
        if head == 0:
            own_grad[:, :DH] = dk
            own_grad[:, DH:] = dv
        else:
            own_grad[:, :DH] += dk
            own_grad[:, DH:] += dv


def own_gradients(operands, score_grads, probs):
    rows = operands[0].shape[0]
    chip = 2 * rows
    return pl.pallas_call(
        own_kernel,
        out_shape=(
            whole((rows, GROUP * DH)),
            whole((rows, GROUP * DH)),
            whole((chip, 2 * DH), jnp.float32),
        ),
        compiler_params=pltpu.CompilerParams(vmem_limit_bytes=24 * MIB),
        cost_estimate=pl.CostEstimate(
            flops=6 * score_grads.size * DH, bytes_accessed=6 * MIB, transcendentals=0
        ),
    )(*operands, score_grads, probs)


def combine_kernel(own, near, far, out):
    total = own[...] + near[...].astype(jnp.float32) + far[...].astype(jnp.float32)
    out[...] = total.T.astype(jnp.bfloat16)


def combine(own, near, far):
    return pl.pallas_call(
        combine_kernel,
        out_shape=whole((own.shape[1], own.shape[0])),
        compiler_params=SMALL,
        cost_estimate=pl.CostEstimate(flops=0, bytes_accessed=MIB, transcendentals=0),
    )(own, near, far)


def assemble_kernel(here_ref, mine, other, out):
    width = mine.shape[1]
    core = here_ref[1]
    out[:, pl.ds(pl.multiple_of(core * width, width), width)] = mine[...]
    out[:, pl.ds(pl.multiple_of((1 - core) * width, width), width)] = other[...]


def assemble(here, mine, other):
    return pl.pallas_call(
        assemble_kernel,
        out_shape=whole((mine.shape[0], 2 * mine.shape[1])),
        in_specs=[SCALAR, pl.BlockSpec(), pl.BlockSpec()],
        compiler_params=SMALL,
        cost_estimate=pl.CostEstimate(flops=0, bytes_accessed=MIB, transcendentals=0),
    )(here, mine, other)


def project_kernel(places_ref, *refs, offset):
    n = len(refs) // 2
    pieces, grads, out = refs[:n], refs[n:-1], refs[-1]
    step = out.shape[0]
    place = jnp.where(places_ref[2] == 0, places_ref[1], places_ref[0]) ^ offset
    columns = pl.ds(pl.multiple_of(place * step, step), step)
    left = jnp.concatenate([ref[...] for ref in grads], axis=1)
    right = jnp.concatenate([ref[:, columns] for ref in pieces], axis=0)
    out[...] = dot_nn(left, right).T.astype(out.dtype)


def project(places, pieces, grads, offset, dtype):
    rows, columns = pieces[0].shape
    width = grads[0].shape[0]
    step = columns // len(pieces)
    return pl.pallas_call(
        functools.partial(project_kernel, offset=offset),
        out_shape=whole((step, width), dtype),
        in_specs=[SCALAR] + [pl.BlockSpec()] * (2 * len(pieces)),
        compiler_params=pltpu.CompilerParams(vmem_limit_bytes=16 * MIB),
        cost_estimate=pl.CostEstimate(
            flops=2 * len(pieces) * rows * step * width,
            bytes_accessed=2 * MIB,
            transcendentals=0,
        ),
    )(places, *pieces, *grads)


def add_kernel(*refs):
    total = refs[0][...]
    for ref in refs[1:-1]:
        total = total + ref[...].astype(jnp.float32)
    refs[-1][...] = total.astype(jnp.bfloat16)


def add_parts(own, parts):
    return pl.pallas_call(
        add_kernel,
        out_shape=whole(own.shape),
        compiler_params=SMALL,
        cost_estimate=pl.CostEstimate(flops=0, bytes_accessed=2 * MIB, transcendentals=0),
    )(own, *parts)


def final_kernel(parts, out):
    for head in range(KV):
        total = parts[head].astype(jnp.float32)
        for i in range(1, parts.shape[0] // KV):
            total = total + parts[KV * i + head].astype(jnp.float32)
        out[:, head * DH : (head + 1) * DH] = total[:, :DH]
        out[:, (KV + head) * DH : (KV + head + 1) * DH] = total[:, DH:]


def final_sum(parts):
    return pl.pallas_call(
        final_kernel,
        out_shape=whole((parts.shape[1], 2 * KV * DH), jnp.float32),
        compiler_params=SMALL,
        cost_estimate=pl.CostEstimate(flops=0, bytes_accessed=512 * 1024, transcendentals=0),
    )(parts)


def per_device(queries, keys, values, out_grad, layer_input, segment_ids):
    rows = queries.shape[1]
    chip = 2 * rows
    z_lo = lax.axis_index("z_lo")
    core = lax.axis_index("core")
    n_chips = lax.axis_size("z_lo")
    swap = [(0, 1), (1, 0)]
    here_ref = jnp.stack([z_lo, core]).astype(jnp.int32)
    places_ref = jnp.stack([lax.axis_index("y"), lax.axis_index("x"), core]).astype(jnp.int32)
    n_side = lax.axis_size("y")

    def cross(part, k, first):
        def pair(y, x, c):
            along_y = (c == 0) == first
            there = (y ^ k, x) if along_y else (y, x ^ k)
            return ((y * n_side + x) * 2 + c, (there[0] * n_side + there[1]) * 2 + c)

        pairs = [pair(y, x, c) for y in range(n_side) for x in range(n_side) for c in range(2)]
        return lax.ppermute(part, ("y", "x", "core"), pairs)


    def half_of(array, which):
        width = array.shape[-1] // 2
        return lax.dynamic_slice_in_dim(array[0], which * width, width, 1)

    k_mine, v_mine = half_of(keys, core), half_of(values, core)
    chip_pair = chip_pairs(
        k_mine,
        v_mine,
        lax.ppermute(
            jnp.concatenate([half_of(keys, 1 - core), half_of(values, 1 - core)], axis=1), "core", swap
        ),
    )
    q_mine, do_mine = half_of(queries, core), half_of(out_grad, core)
    q_out, do_out = half_of(queries, 1 - core), half_of(out_grad, 1 - core)
    q_out, do_out, _ = lax.optimization_barrier((q_out, do_out, chip_pair))
    q_other, do_other = (lax.ppermute(part, "core", swap) for part in (q_out, do_out))

    def behind(distance):
        return [
            (chip_at * 2 + c, (chip_at + distance) * 2 + c)
            for chip_at in range(n_chips - distance)
            for c in range(2)
        ]

    blocks = [chip_pair] + [
        lax.ppermute(chip_pair, ("z_lo", "core"), behind(distance)) for distance in (2, 1)
    ][::-1]

    chunks = split_columns(
        places_ref, layer_input[0], lax.ppermute(layer_input[0], "core", swap), n_side
    )
    chunks, _ = lax.optimization_barrier((chunks, (q_other, do_other)))
    pieces = [chunks[0]] + [cross(chunks[k], k, True) for k in range(1, n_side)]
    docs, _ = lax.optimization_barrier((segment_ids, chunks[0]))

    operands = (q_mine, do_mine, q_other, do_other, *blocks)
    near_grad, far_grad, score_grads, probs = attention(
        operands, make_bias(here_ref, docs, rows)
    )
    dq_mine, dq_other, own_grad = own_gradients(operands, score_grads, probs)
    far_back, near_back = (
        lax.ppermute(part, ("z_lo", "core"), [(b, a) for a, b in behind(distance)])
        for distance, part in ((2, far_grad), (1, near_grad))
    )

    grad = combine(own_grad, near_back, far_back)
    grads = [grad] + [cross(grad, k, True) for k in range(1, n_side)]
    pieces, grads, dq_other = lax.optimization_barrier((pieces, grads, dq_other))
    parts = []
    for k in (2, 1, 3):
        parts.append(cross(project(places_ref, pieces, grads, k, jnp.bfloat16), k, False))
    own_term = project(places_ref, pieces, grads, 0, jnp.float32)
    dq_back = lax.ppermute(dq_other, "core", swap)
    query_grad = assemble(here_ref, dq_mine, dq_back)[None]
    parts, query_grad = lax.optimization_barrier((parts, query_grad))
    term = add_parts(own_term, parts)
    rest = ("z_hi", "z_lo", "core")
    n_rest = lax.axis_size(rest)
    spread = lax.all_to_all(
        term.reshape(n_rest, term.shape[0] // n_rest, term.shape[1]), rest, 0, 0, tiled=True
    )
    return (query_grad, final_sum(spread))


def solution(mesh):
    axes = ("y", "x", "z_hi", "z_lo", "core")
    fine = Mesh(mesh.devices.reshape(4, 4, 2, 4, 2), axes)
    dp, ctx = axes[:3], axes[3:]
    return jax.shard_map(
        per_device,
        mesh=fine,
        in_specs=(P(dp, ctx, None),) * 5 + (P(dp, None),),
        out_specs=(P(dp, ctx, None), P(axes, None)),
        check_vma=False,
    )
```

```python
import functools

import jax
import jax.numpy as jnp
from jax import lax
from jax.experimental import pallas as pl
from jax.experimental.pallas import tpu as pltpu
from jax.sharding import Mesh, PartitionSpec as P

H = 16
KV = 2
DH = 128
GROUP = H // KV
SCALE = 1.0 / DH**0.5
LOG2E = 1.4426950408889634
REACH = 2
MASKED = -1e30
MIB = 1024 * 1024
SMALL = pltpu.CompilerParams(vmem_limit_bytes=4 * MIB)


def dot_nt(left, right):
    return lax.dot_general(
        left, right, (((1,), (1,)), ((), ())), preferred_element_type=jnp.float32
    )


def dot_nn(left, right):
    return jnp.dot(left, right, preferred_element_type=jnp.float32)


def whole(shape, dtype=jnp.bfloat16):
    return jax.ShapeDtypeStruct(shape, dtype)


SCALAR = pl.BlockSpec(memory_space=pltpu.SMEM)


def pair_kernel(keys, values, swapped, out):
    rows = keys.shape[0]
    out[:rows, :DH] = keys[...]
    out[:rows, DH:] = values[...]
    out[rows:] = swapped[...]


def chip_pairs(keys, values, swapped):
    return pl.pallas_call(
        pair_kernel,
        out_shape=whole((2 * keys.shape[0], 2 * DH)),
        compiler_params=SMALL,
        cost_estimate=pl.CostEstimate(flops=0, bytes_accessed=256 * 1024, transcendentals=0),
    )(keys, values, swapped)


def block_of(places_ref, k, i, n):
    y, x, core = places_ref[0], places_ref[1], places_ref[2]
    return jnp.where(core == 0, (y ^ k) * n + i, i * n + (x ^ k))


def chunk_kernel(places_ref, mine, other, *outs):
    n = len(outs) + 1
    rows, step = mine.shape[0], outs[0].shape[1] // n
    for k, out in enumerate(outs, 1):
        for i in range(n):
            held = pl.ds(pl.multiple_of(block_of(places_ref, k, i, n) * step, step), step)
            out[:rows, i * step : (i + 1) * step] = mine[:, held]
            out[rows:, i * step : (i + 1) * step] = other[:, held]


def split_columns(places, mine, other, chunks):
    rows, width = mine.shape
    return pl.pallas_call(
        chunk_kernel,
        out_shape=(whole((2 * rows, width // chunks)),) * (chunks - 1),
        in_specs=[SCALAR, pl.BlockSpec(), pl.BlockSpec()],
        compiler_params=pltpu.CompilerParams(vmem_limit_bytes=16 * MIB),
        cost_estimate=pl.CostEstimate(flops=0, bytes_accessed=6 * MIB, transcendentals=0),
    )(places, mine, other)


def bias_kernel(here_ref, docs, out):
    z_lo, core = here_ref[0], here_ref[1]
    rows = out.shape[1] // 2
    chip = 2 * rows
    shape = (rows, rows)
    down = lax.broadcasted_iota(jnp.int32, shape, 0)
    along = lax.broadcasted_iota(jnp.int32, shape, 1)

    def place(distance, which):
        start = (z_lo - distance) * chip + (core ^ which) * rows
        held = pl.ds(pl.multiple_of(jnp.maximum(start, 0), rows), rows)
        return start, jnp.broadcast_to(docs[:, held].astype(jnp.float32), shape)

    queries = [place(0, which) for which in range(2)]
    for block in range(2 * (REACH + 1)):
        key_start, key_row = place(block // 2, block % 2)
        key_doc, key_pos = key_row.T, key_start + down
        for which, (query_start, query_doc) in enumerate(queries):
            allowed = (key_pos >= 0) & (key_pos <= query_start + along) & (key_doc == query_doc)
            out[block * rows : (block + 1) * rows, which * rows : (which + 1) * rows] = jnp.where(
                allowed, 0.0, MASKED
            )


def make_bias(here, docs, rows):
    return pl.pallas_call(
        bias_kernel,
        out_shape=whole((2 * rows * (REACH + 1), 2 * rows), jnp.float32),
        in_specs=[SCALAR, pl.BlockSpec()],
        compiler_params=SMALL,
        cost_estimate=pl.CostEstimate(flops=0, bytes_accessed=MIB, transcendentals=0),
    )(here, docs)


def attention_kernel(
    q_mine, do_mine, q_other, do_other, chip_pair, near_pair, far_pair, bias,
    near_grad, far_grad, score_grads, probs, dk_acc, dv_acc,
):
    pairs = jnp.concatenate([chip_pair[...], near_pair[...], far_pair[...]], axis=0)
    key, value = pairs[:, :DH], pairs[:, DH:]
    chip = chip_pair.shape[0]

    def load(head):
        cols = slice(head * DH, (head + 1) * DH)
        return (
            jnp.concatenate([q_mine[:, cols], q_other[:, cols]], axis=0),
            jnp.concatenate([do_mine[:, cols], do_other[:, cols]], axis=0),
        )

    def products(head):
        query, grad = load(head)
        return dot_nt(key, query), dot_nt(value, grad)

    ahead = products(0)
    for head in range(GROUP):
        raw, prob_grad = ahead
        if head + 1 < GROUP:
            ahead = products(head + 1)
        score = raw * (SCALE * LOG2E) + bias[...]
        top = jnp.max(score, axis=0, keepdims=True)
        weight = jnp.exp2(score - top)
        inverse = 1.0 / jnp.sum(weight, axis=0, keepdims=True)
        prob = weight * inverse
        prob_half = prob.astype(jnp.bfloat16)
        delta = jnp.sum(prob_half.astype(jnp.float32) * prob_grad, axis=0, keepdims=True)
        score_grad = (prob * (prob_grad - delta) * SCALE).astype(jnp.bfloat16)
        score_grads[head] = score_grad
        probs[head] = prob_half[:chip]
        query, grad = load(head)
        dk = dot_nn(score_grad[chip:], query)
        dv = dot_nn(prob_half[chip:], grad)
        if head == 0:
            dk_acc[...] = dk
            dv_acc[...] = dv
        else:
            dk_acc[...] += dk
            dv_acc[...] += dv
    for out, start in ((near_grad, 0), (far_grad, chip)):
        out[:, :DH] = dk_acc[start : start + chip].astype(jnp.bfloat16)
        out[:, DH:] = dv_acc[start : start + chip].astype(jnp.bfloat16)


def attention(operands, bias):
    rows = operands[0].shape[0]
    chip = 2 * rows
    keys = chip * (REACH + 1)
    return pl.pallas_call(
        attention_kernel,
        out_shape=(
            whole((chip, 2 * DH)),
            whole((chip, 2 * DH)),
            whole((GROUP, keys, chip)),
            whole((GROUP, chip, chip)),
        ),
        scratch_shapes=[
            pltpu.VMEM((keys - chip, DH), jnp.float32),
            pltpu.VMEM((keys - chip, DH), jnp.float32),
        ],
        compiler_params=pltpu.CompilerParams(vmem_limit_bytes=24 * MIB),
        cost_estimate=pl.CostEstimate(
            flops=40 * keys * chip * DH * GROUP,
            bytes_accessed=4 * MIB,
            transcendentals=keys * chip * GROUP,
        ),
    )(*operands, bias)


def own_kernel(
    q_mine, do_mine, q_other, do_other, chip_pair, near_pair, far_pair, score_grads, probs,
    dq_mine, dq_other, own_grad,
):
    key_t = jnp.concatenate([ref[:, :DH] for ref in (chip_pair, near_pair, far_pair)], axis=0).T
    rows, chip = q_mine.shape[0], chip_pair.shape[0]
    for head in range(GROUP):
        cols = slice(head * DH, (head + 1) * DH)
        query = jnp.concatenate([q_mine[:, cols], q_other[:, cols]], axis=0)
        grad = jnp.concatenate([do_mine[:, cols], do_other[:, cols]], axis=0)
        dq = dot_nn(key_t, score_grads[head]).T.astype(jnp.bfloat16)
        dq_mine[:, cols] = dq[:rows]
        dq_other[:, cols] = dq[rows:]
        dk = dot_nn(score_grads[head, :chip], query)
        dv = dot_nn(probs[head], grad)
        if head == 0:
            own_grad[:, :DH] = dk
            own_grad[:, DH:] = dv
        else:
            own_grad[:, :DH] += dk
            own_grad[:, DH:] += dv


def own_gradients(operands, score_grads, probs):
    rows = operands[0].shape[0]
    chip = 2 * rows
    return pl.pallas_call(
        own_kernel,
        out_shape=(
            whole((rows, GROUP * DH)),
            whole((rows, GROUP * DH)),
            whole((chip, 2 * DH), jnp.float32),
        ),
        compiler_params=pltpu.CompilerParams(vmem_limit_bytes=24 * MIB),
        cost_estimate=pl.CostEstimate(
            flops=6 * score_grads.size * DH, bytes_accessed=6 * MIB, transcendentals=0
        ),
    )(*operands, score_grads, probs)


def combine_kernel(own, near, far, out):
    total = own[...] + near[...].astype(jnp.float32) + far[...].astype(jnp.float32)
    out[...] = total.T.astype(jnp.bfloat16)


def combine(own, near, far):
    return pl.pallas_call(
        combine_kernel,
        out_shape=whole((own.shape[1], own.shape[0])),
        compiler_params=SMALL,
        cost_estimate=pl.CostEstimate(flops=0, bytes_accessed=MIB, transcendentals=0),
    )(own, near, far)


def assemble_kernel(here_ref, mine, other, out):
    width = mine.shape[1]
    core = here_ref[1]
    out[:, pl.ds(pl.multiple_of(core * width, width), width)] = mine[...]
    out[:, pl.ds(pl.multiple_of((1 - core) * width, width), width)] = other[...]


def assemble(here, mine, other):
    return pl.pallas_call(
        assemble_kernel,
        out_shape=whole((mine.shape[0], 2 * mine.shape[1])),
        in_specs=[SCALAR, pl.BlockSpec(), pl.BlockSpec()],
        compiler_params=SMALL,
        cost_estimate=pl.CostEstimate(flops=0, bytes_accessed=MIB, transcendentals=0),
    )(here, mine, other)


def project_kernel(places_ref, mine, other, *refs, offset):
    n = len(refs) // 2
    pieces, grads, out = refs[: n - 1], refs[n - 1 : -1], refs[-1]
    step = out.shape[0]
    place = jnp.where(places_ref[2] == 0, places_ref[1], places_ref[0]) ^ offset
    columns = pl.ds(pl.multiple_of(place * step, step), step)
    held = pl.ds(pl.multiple_of(block_of(places_ref, 0, place, n) * step, step), step)
    left = jnp.concatenate([ref[...] for ref in grads], axis=1)
    right = jnp.concatenate(
        [mine[:, held], other[:, held]] + [ref[:, columns] for ref in pieces], axis=0
    )
    out[...] = dot_nn(left, right).T.astype(out.dtype)


def project(places, own, pieces, grads, offset, dtype):
    rows, columns = pieces[0].shape
    width = grads[0].shape[0]
    step = columns // len(grads)
    return pl.pallas_call(
        functools.partial(project_kernel, offset=offset),
        out_shape=whole((step, width), dtype),
        in_specs=[SCALAR] + [pl.BlockSpec()] * (1 + 2 * len(grads)),
        compiler_params=pltpu.CompilerParams(vmem_limit_bytes=16 * MIB),
        cost_estimate=pl.CostEstimate(
            flops=2 * len(grads) * rows * step * width,
            bytes_accessed=2 * MIB,
            transcendentals=0,
        ),
    )(places, *own, *pieces, *grads)


def add_kernel(*refs):
    total = refs[0][...]
    for ref in refs[1:-1]:
        total = total + ref[...].astype(jnp.float32)
    refs[-1][...] = total.astype(jnp.bfloat16)


def add_parts(own, parts):
    return pl.pallas_call(
        add_kernel,
        out_shape=whole(own.shape),
        compiler_params=SMALL,
        cost_estimate=pl.CostEstimate(flops=0, bytes_accessed=2 * MIB, transcendentals=0),
    )(own, *parts)


def final_kernel(parts, out):
    for head in range(KV):
        total = parts[head].astype(jnp.float32)
        for i in range(1, parts.shape[0] // KV):
            total = total + parts[KV * i + head].astype(jnp.float32)
        out[:, head * DH : (head + 1) * DH] = total[:, :DH]
        out[:, (KV + head) * DH : (KV + head + 1) * DH] = total[:, DH:]


def final_sum(parts):
    return pl.pallas_call(
        final_kernel,
        out_shape=whole((parts.shape[1], 2 * KV * DH), jnp.float32),
        compiler_params=SMALL,
        cost_estimate=pl.CostEstimate(flops=0, bytes_accessed=512 * 1024, transcendentals=0),
    )(parts)


def per_device(queries, keys, values, out_grad, layer_input, segment_ids):
    rows = queries.shape[1]
    chip = 2 * rows
    z_lo = lax.axis_index("z_lo")
    core = lax.axis_index("core")
    n_chips = lax.axis_size("z_lo")
    swap = [(0, 1), (1, 0)]
    here_ref = jnp.stack([z_lo, core]).astype(jnp.int32)
    places_ref = jnp.stack([lax.axis_index("y"), lax.axis_index("x"), core]).astype(jnp.int32)
    n_side = lax.axis_size("y")

    def cross(part, k, first):
        def pair(y, x, c):
            along_y = (c == 0) == first
            there = (y ^ k, x) if along_y else (y, x ^ k)
            return ((y * n_side + x) * 2 + c, (there[0] * n_side + there[1]) * 2 + c)

        pairs = [pair(y, x, c) for y in range(n_side) for x in range(n_side) for c in range(2)]
        return lax.ppermute(part, ("y", "x", "core"), pairs)


    def half_of(array, which):
        width = array.shape[-1] // 2
        return lax.dynamic_slice_in_dim(array[0], which * width, width, 1)

    k_mine, v_mine = half_of(keys, core), half_of(values, core)
    chip_pair = chip_pairs(
        k_mine,
        v_mine,
        lax.ppermute(
            jnp.concatenate([half_of(keys, 1 - core), half_of(values, 1 - core)], axis=1), "core", swap
        ),
    )
    q_mine, do_mine = half_of(queries, core), half_of(out_grad, core)
    q_out, do_out = half_of(queries, 1 - core), half_of(out_grad, 1 - core)
    q_out, do_out, _ = lax.optimization_barrier((q_out, do_out, chip_pair))
    q_other, do_other = (lax.ppermute(part, "core", swap) for part in (q_out, do_out))

    def behind(distance):
        return [
            (chip_at * 2 + c, (chip_at + distance) * 2 + c)
            for chip_at in range(n_chips - distance)
            for c in range(2)
        ]

    blocks = [chip_pair] + [
        lax.ppermute(chip_pair, ("z_lo", "core"), behind(distance)) for distance in (2, 1)
    ][::-1]

    own = (layer_input[0], lax.ppermute(layer_input[0], "core", swap))
    chunks = split_columns(places_ref, *own, n_side)
    chunks, _ = lax.optimization_barrier((chunks, (q_other, do_other)))
    pieces = [cross(chunk, k, True) for k, chunk in enumerate(chunks, 1)]
    docs, _ = lax.optimization_barrier((segment_ids, chunks[0]))

    operands = (q_mine, do_mine, q_other, do_other, *blocks)
    near_grad, far_grad, score_grads, probs = attention(
        operands, make_bias(here_ref, docs, rows)
    )
    dq_mine, dq_other, own_grad = own_gradients(operands, score_grads, probs)
    far_back, near_back = (
        lax.ppermute(part, ("z_lo", "core"), [(b, a) for a, b in behind(distance)])
        for distance, part in ((2, far_grad), (1, near_grad))
    )

    grad = combine(own_grad, near_back, far_back)
    grads = [grad] + [cross(grad, k, True) for k in range(1, n_side)]
    dq_other, grads[2:] = lax.optimization_barrier((dq_other, grads[2:]))
    dq_back = lax.ppermute(dq_other, "core", swap)
    query_grad = assemble(here_ref, dq_mine, dq_back)[None]
    pieces, grads, query_grad = lax.optimization_barrier((pieces, grads, query_grad))
    terms = [project(places_ref, own, pieces, grads, k, jnp.bfloat16) for k in (2, 1, 3)]
    parts = [cross(term, k, False) for term, k in zip(terms, (2, 1, 3))]
    own_term = project(places_ref, own, pieces, grads, 0, jnp.float32)
    term = add_parts(own_term, parts)
    rest = ("z_hi", "z_lo", "core")
    n_rest = lax.axis_size(rest)
    spread = lax.all_to_all(
        term.reshape(n_rest, term.shape[0] // n_rest, term.shape[1]), rest, 0, 0, tiled=True
    )
    return (query_grad, final_sum(spread))


def solution(mesh):
    axes = ("y", "x", "z_hi", "z_lo", "core")
    fine = Mesh(mesh.devices.reshape(4, 4, 2, 4, 2), axes)
    dp, ctx = axes[:3], axes[3:]
    return jax.shard_map(
        per_device,
        mesh=fine,
        in_specs=(P(dp, ctx, None),) * 5 + (P(dp, None),),
        out_specs=(P(dp, ctx, None), P(axes, None)),
        check_vma=False,
    )
```

```python
import functools

import jax
import jax.numpy as jnp
from jax import lax
from jax.experimental import pallas as pl
from jax.experimental.pallas import tpu as pltpu
from jax.sharding import Mesh, PartitionSpec as P

H = 16
KV = 2
DH = 128
GROUP = H // KV
SCALE = 1.0 / DH**0.5
LOG2E = 1.4426950408889634
REACH = 2
MASKED = -1e30
MIB = 1024 * 1024
SMALL = pltpu.CompilerParams(vmem_limit_bytes=4 * MIB)


def dot_nt(left, right):
    return lax.dot_general(
        left, right, (((1,), (1,)), ((), ())), preferred_element_type=jnp.float32
    )


def dot_nn(left, right):
    return jnp.dot(left, right, preferred_element_type=jnp.float32)


def whole(shape, dtype=jnp.bfloat16):
    return jax.ShapeDtypeStruct(shape, dtype)


SCALAR = pl.BlockSpec(memory_space=pltpu.SMEM)


def pair_kernel(keys, values, swapped, out):
    rows = keys.shape[0]
    out[:rows, :DH] = keys[...]
    out[:rows, DH:] = values[...]
    out[rows:] = swapped[...]


def chip_pairs(keys, values, swapped):
    return pl.pallas_call(
        pair_kernel,
        out_shape=whole((2 * keys.shape[0], 2 * DH)),
        compiler_params=SMALL,
        cost_estimate=pl.CostEstimate(flops=0, bytes_accessed=256 * 1024, transcendentals=0),
    )(keys, values, swapped)


def block_of(places_ref, k, i, n):
    y, x, core = places_ref[0], places_ref[1], places_ref[2]
    return jnp.where(core == 0, (y ^ k) * n + i, i * n + (x ^ k))


def chunk_kernel(places_ref, mine, other, *outs, places):
    n = mine.shape[1] // outs[0].shape[1]
    rows, step = mine.shape[0], outs[0].shape[1] // n
    for k, out in zip(places, outs):
        for i in range(n):
            held = pl.ds(pl.multiple_of(block_of(places_ref, k, i, n) * step, step), step)
            out[:rows, i * step : (i + 1) * step] = mine[:, held]
            out[rows:, i * step : (i + 1) * step] = other[:, held]


def split_columns(places_ref, mine, other, chunks, places):
    rows, width = mine.shape
    return pl.pallas_call(
        functools.partial(chunk_kernel, places=places),
        out_shape=(whole((2 * rows, width // chunks)),) * len(places),
        in_specs=[SCALAR, pl.BlockSpec(), pl.BlockSpec()],
        compiler_params=pltpu.CompilerParams(vmem_limit_bytes=16 * MIB),
        cost_estimate=pl.CostEstimate(flops=0, bytes_accessed=6 * MIB, transcendentals=0),
    )(places_ref, mine, other)


def bias_kernel(here_ref, docs, out):
    z_lo, core = here_ref[0], here_ref[1]
    rows = out.shape[1] // 2
    chip = 2 * rows
    shape = (rows, rows)
    down = lax.broadcasted_iota(jnp.int32, shape, 0)
    along = lax.broadcasted_iota(jnp.int32, shape, 1)

    def place(distance, which):
        start = (z_lo - distance) * chip + (core ^ which) * rows
        held = pl.ds(pl.multiple_of(jnp.maximum(start, 0), rows), rows)
        return start, jnp.broadcast_to(docs[:, held].astype(jnp.float32), shape)

    queries = [place(0, which) for which in range(2)]
    for block in range(2 * (REACH + 1)):
        key_start, key_row = place(block // 2, block % 2)
        key_doc, key_pos = key_row.T, key_start + down
        for which, (query_start, query_doc) in enumerate(queries):
            allowed = (key_pos >= 0) & (key_pos <= query_start + along) & (key_doc == query_doc)
            out[block * rows : (block + 1) * rows, which * rows : (which + 1) * rows] = jnp.where(
                allowed, 0.0, MASKED
            )


def make_bias(here, docs, rows):
    return pl.pallas_call(
        bias_kernel,
        out_shape=whole((2 * rows * (REACH + 1), 2 * rows), jnp.float32),
        in_specs=[SCALAR, pl.BlockSpec()],
        compiler_params=SMALL,
        cost_estimate=pl.CostEstimate(flops=0, bytes_accessed=MIB, transcendentals=0),
    )(here, docs)


def attention_kernel(
    q_mine, do_mine, q_other, do_other, chip_pair, near_pair, far_pair, bias,
    near_grad, far_grad, score_grads, probs, dk_acc, dv_acc,
):
    pairs = jnp.concatenate([chip_pair[...], near_pair[...], far_pair[...]], axis=0)
    key, value = pairs[:, :DH], pairs[:, DH:]
    chip = chip_pair.shape[0]

    def load(head):
        cols = slice(head * DH, (head + 1) * DH)
        return (
            jnp.concatenate([q_mine[:, cols], q_other[:, cols]], axis=0),
            jnp.concatenate([do_mine[:, cols], do_other[:, cols]], axis=0),
        )

    def products(head):
        query, grad = load(head)
        return dot_nt(key, query), dot_nt(value, grad)

    ahead = products(0)
    for head in range(GROUP):
        raw, prob_grad = ahead
        if head + 1 < GROUP:
            ahead = products(head + 1)
        score = raw * (SCALE * LOG2E) + bias[...]
        top = jnp.max(score, axis=0, keepdims=True)
        weight = jnp.exp2(score - top)
        inverse = 1.0 / jnp.sum(weight, axis=0, keepdims=True)
        prob = weight * inverse
        prob_half = prob.astype(jnp.bfloat16)
        delta = jnp.sum(prob_half.astype(jnp.float32) * prob_grad, axis=0, keepdims=True)
        score_grad = (prob * (prob_grad - delta) * SCALE).astype(jnp.bfloat16)
        score_grads[head] = score_grad
        probs[head] = prob_half[:chip]
        query, grad = load(head)
        dk = dot_nn(score_grad[chip:], query)
        dv = dot_nn(prob_half[chip:], grad)
        if head == 0:
            dk_acc[...] = dk
            dv_acc[...] = dv
        else:
            dk_acc[...] += dk
            dv_acc[...] += dv
    for out, start in ((near_grad, 0), (far_grad, chip)):
        out[:, :DH] = dk_acc[start : start + chip].astype(jnp.bfloat16)
        out[:, DH:] = dv_acc[start : start + chip].astype(jnp.bfloat16)


def attention(operands, bias):
    rows = operands[0].shape[0]
    chip = 2 * rows
    keys = chip * (REACH + 1)
    return pl.pallas_call(
        attention_kernel,
        out_shape=(
            whole((chip, 2 * DH)),
            whole((chip, 2 * DH)),
            whole((GROUP, keys, chip)),
            whole((GROUP, chip, chip)),
        ),
        scratch_shapes=[
            pltpu.VMEM((keys - chip, DH), jnp.float32),
            pltpu.VMEM((keys - chip, DH), jnp.float32),
        ],
        compiler_params=pltpu.CompilerParams(vmem_limit_bytes=24 * MIB),
        cost_estimate=pl.CostEstimate(
            flops=150 * keys * chip * DH * GROUP,
            bytes_accessed=4 * MIB,
            transcendentals=keys * chip * GROUP,
        ),
    )(*operands, bias)


def own_kernel(
    q_mine, do_mine, q_other, do_other, chip_pair, near_pair, far_pair, score_grads, probs,
    dq_mine, dq_other, own_grad,
):
    key_t = jnp.concatenate([ref[:, :DH] for ref in (chip_pair, near_pair, far_pair)], axis=0).T
    rows, chip = q_mine.shape[0], chip_pair.shape[0]
    for head in range(GROUP):
        cols = slice(head * DH, (head + 1) * DH)
        query = jnp.concatenate([q_mine[:, cols], q_other[:, cols]], axis=0)
        grad = jnp.concatenate([do_mine[:, cols], do_other[:, cols]], axis=0)
        dq = dot_nn(key_t, score_grads[head]).T.astype(jnp.bfloat16)
        dq_mine[:, cols] = dq[:rows]
        dq_other[:, cols] = dq[rows:]
        dk = dot_nn(score_grads[head, :chip], query)
        dv = dot_nn(probs[head], grad)
        if head == 0:
            own_grad[:, :DH] = dk
            own_grad[:, DH:] = dv
        else:
            own_grad[:, :DH] += dk
            own_grad[:, DH:] += dv


def own_gradients(operands, score_grads, probs):
    rows = operands[0].shape[0]
    chip = 2 * rows
    return pl.pallas_call(
        own_kernel,
        out_shape=(
            whole((rows, GROUP * DH)),
            whole((rows, GROUP * DH)),
            whole((chip, 2 * DH), jnp.float32),
        ),
        compiler_params=pltpu.CompilerParams(vmem_limit_bytes=24 * MIB),
        cost_estimate=pl.CostEstimate(
            flops=6 * score_grads.size * DH, bytes_accessed=6 * MIB, transcendentals=0
        ),
    )(*operands, score_grads, probs)


def combine_kernel(own, near, far, out):
    total = own[...] + near[...].astype(jnp.float32) + far[...].astype(jnp.float32)
    out[...] = total.T.astype(jnp.bfloat16)


def combine(own, near, far):
    return pl.pallas_call(
        combine_kernel,
        out_shape=whole((own.shape[1], own.shape[0])),
        compiler_params=SMALL,
        cost_estimate=pl.CostEstimate(flops=0, bytes_accessed=MIB, transcendentals=0),
    )(own, near, far)


def assemble_kernel(here_ref, mine, other, out):
    width = mine.shape[1]
    core = here_ref[1]
    out[:, pl.ds(pl.multiple_of(core * width, width), width)] = mine[...]
    out[:, pl.ds(pl.multiple_of((1 - core) * width, width), width)] = other[...]


def assemble(here, mine, other):
    return pl.pallas_call(
        assemble_kernel,
        out_shape=whole((mine.shape[0], 2 * mine.shape[1])),
        in_specs=[SCALAR, pl.BlockSpec(), pl.BlockSpec()],
        compiler_params=SMALL,
        cost_estimate=pl.CostEstimate(flops=0, bytes_accessed=MIB, transcendentals=0),
    )(here, mine, other)


def project_kernel(places_ref, *refs, offset):
    n = len(refs) // 2
    pieces, grads, out = refs[:n], refs[n:-1], refs[-1]
    step = out.shape[0]
    place = jnp.where(places_ref[2] == 0, places_ref[1], places_ref[0]) ^ offset
    columns = pl.ds(pl.multiple_of(place * step, step), step)
    left = jnp.concatenate([ref[...] for ref in grads], axis=1)
    right = jnp.concatenate([ref[:, columns] for ref in pieces], axis=0)
    out[...] = dot_nn(left, right).T.astype(out.dtype)


def project(places, pieces, grads, offset, dtype):
    rows, columns = pieces[0].shape
    width = grads[0].shape[0]
    step = columns // len(pieces)
    return pl.pallas_call(
        functools.partial(project_kernel, offset=offset),
        out_shape=whole((step, width), dtype),
        in_specs=[SCALAR] + [pl.BlockSpec()] * (2 * len(pieces)),
        compiler_params=pltpu.CompilerParams(vmem_limit_bytes=16 * MIB),
        cost_estimate=pl.CostEstimate(
            flops=2 * len(pieces) * rows * step * width,
            bytes_accessed=2 * MIB,
            transcendentals=0,
        ),
    )(places, *pieces, *grads)


def add_kernel(*refs):
    total = refs[0][...]
    for ref in refs[1:-1]:
        total = total + ref[...].astype(jnp.float32)
    refs[-1][...] = total.astype(jnp.bfloat16)


def add_parts(own, parts):
    return pl.pallas_call(
        add_kernel,
        out_shape=whole(own.shape),
        compiler_params=SMALL,
        cost_estimate=pl.CostEstimate(flops=0, bytes_accessed=2 * MIB, transcendentals=0),
    )(own, *parts)


def final_kernel(parts, out):
    for head in range(KV):
        total = parts[head].astype(jnp.float32)
        for i in range(1, parts.shape[0] // KV):
            total = total + parts[KV * i + head].astype(jnp.float32)
        out[:, head * DH : (head + 1) * DH] = total[:, :DH]
        out[:, (KV + head) * DH : (KV + head + 1) * DH] = total[:, DH:]


def final_sum(parts):
    return pl.pallas_call(
        final_kernel,
        out_shape=whole((parts.shape[1], 2 * KV * DH), jnp.float32),
        compiler_params=SMALL,
        cost_estimate=pl.CostEstimate(flops=0, bytes_accessed=512 * 1024, transcendentals=0),
    )(parts)


def per_device(queries, keys, values, out_grad, layer_input, segment_ids):
    rows = queries.shape[1]
    chip = 2 * rows
    z_lo = lax.axis_index("z_lo")
    core = lax.axis_index("core")
    n_chips = lax.axis_size("z_lo")
    swap = [(0, 1), (1, 0)]
    here_ref = jnp.stack([z_lo, core]).astype(jnp.int32)
    places_ref = jnp.stack([lax.axis_index("y"), lax.axis_index("x"), core]).astype(jnp.int32)
    n_side = lax.axis_size("y")

    def cross(part, k, first):
        def pair(y, x, c):
            along_y = (c == 0) == first
            there = (y ^ k, x) if along_y else (y, x ^ k)
            return ((y * n_side + x) * 2 + c, (there[0] * n_side + there[1]) * 2 + c)

        pairs = [pair(y, x, c) for y in range(n_side) for x in range(n_side) for c in range(2)]
        return lax.ppermute(part, ("y", "x", "core"), pairs)


    def half_of(array, which):
        width = array.shape[-1] // 2
        return lax.dynamic_slice_in_dim(array[0], which * width, width, 1)

    k_mine, v_mine = half_of(keys, core), half_of(values, core)
    chip_pair = chip_pairs(
        k_mine,
        v_mine,
        lax.ppermute(
            jnp.concatenate([half_of(keys, 1 - core), half_of(values, 1 - core)], axis=1), "core", swap
        ),
    )
    q_mine, do_mine = half_of(queries, core), half_of(out_grad, core)
    q_out, do_out = half_of(queries, 1 - core), half_of(out_grad, 1 - core)
    q_out, do_out, _ = lax.optimization_barrier((q_out, do_out, chip_pair))
    q_other, do_other = (lax.ppermute(part, "core", swap) for part in (q_out, do_out))

    def behind(distance):
        return [
            (chip_at * 2 + c, (chip_at + distance) * 2 + c)
            for chip_at in range(n_chips - distance)
            for c in range(2)
        ]

    blocks = [chip_pair] + [
        lax.ppermute(chip_pair, ("z_lo", "core"), behind(distance)) for distance in (2, 1)
    ][::-1]

    own = (layer_input[0], lax.ppermute(layer_input[0], "core", swap))
    chunks = split_columns(places_ref, *own, n_side, range(1, n_side))
    chunks, _ = lax.optimization_barrier((chunks, (q_other, do_other)))
    pieces = [cross(chunk, k, True) for k, chunk in enumerate(chunks, 1)]
    docs, _ = lax.optimization_barrier((segment_ids, chunks[0]))

    operands = (q_mine, do_mine, q_other, do_other, *blocks)
    near_grad, far_grad, score_grads, probs = attention(
        operands, make_bias(here_ref, docs, rows)
    )
    dq_mine, dq_other, own_grad = own_gradients(operands, score_grads, probs)
    far_back, near_back = (
        lax.ppermute(part, ("z_lo", "core"), [(b, a) for a, b in behind(distance)])
        for distance, part in ((2, far_grad), (1, near_grad))
    )

    (own_piece,) = split_columns(places_ref, *own, n_side, (0,))
    far_back, own_piece = lax.optimization_barrier((far_back, own_piece))
    grad = combine(own_grad, near_back, far_back)
    late, pieces[0], dq_other = lax.optimization_barrier((grad, pieces[0], dq_other))
    grads = [grad] + [cross(late if k == 1 else grad, k, True) for k in range(1, n_side)]
    dq_back = lax.ppermute(dq_other, "core", swap)
    query_grad = assemble(here_ref, dq_mine, dq_back)[None]
    pieces, grads, query_grad = lax.optimization_barrier((pieces, grads, query_grad))
    pieces = [own_piece] + list(pieces)
    terms = [project(places_ref, pieces, grads, k, jnp.bfloat16) for k in (2, 1, 3)]
    parts = [cross(term, k, False) for term, k in zip(terms, (2, 1, 3))]
    own_term = project(places_ref, pieces, grads, 0, jnp.float32)
    term = add_parts(own_term, parts)
    rest = ("z_hi", "z_lo", "core")
    n_rest = lax.axis_size(rest)
    spread = lax.all_to_all(
        term.reshape(n_rest, term.shape[0] // n_rest, term.shape[1]), rest, 0, 0, tiled=True
    )
    return (query_grad, final_sum(spread))


def solution(mesh):
    axes = ("y", "x", "z_hi", "z_lo", "core")
    fine = Mesh(mesh.devices.reshape(4, 4, 2, 4, 2), axes)
    dp, ctx = axes[:3], axes[3:]
    return jax.shard_map(
        per_device,
        mesh=fine,
        in_specs=(P(dp, ctx, None),) * 5 + (P(dp, None),),
        out_specs=(P(dp, ctx, None), P(axes, None)),
        check_vma=False,
    )
```

```python
import functools

import jax
import jax.numpy as jnp
from jax import lax
from jax.experimental import pallas as pl
from jax.experimental.pallas import tpu as pltpu
from jax.sharding import Mesh, PartitionSpec as P

H = 16
KV = 2
DH = 128
GROUP = H // KV
SCALE = 1.0 / DH**0.5
LOG2E = 1.4426950408889634
REACH = 2
MASKED = -1e30
MIB = 1024 * 1024
SMALL = pltpu.CompilerParams(vmem_limit_bytes=4 * MIB)


def dot_nt(left, right):
    return lax.dot_general(
        left, right, (((1,), (1,)), ((), ())), preferred_element_type=jnp.float32
    )


def dot_nn(left, right):
    return jnp.dot(left, right, preferred_element_type=jnp.float32)


def whole(shape, dtype=jnp.bfloat16):
    return jax.ShapeDtypeStruct(shape, dtype)


SCALAR = pl.BlockSpec(memory_space=pltpu.SMEM)


def pair_kernel(keys, values, swapped, out):
    rows = keys.shape[0]
    out[:rows, :DH] = keys[...]
    out[:rows, DH:] = values[...]
    out[rows:] = swapped[...]


def chip_pairs(keys, values, swapped):
    return pl.pallas_call(
        pair_kernel,
        out_shape=whole((2 * keys.shape[0], 2 * DH)),
        compiler_params=SMALL,
        cost_estimate=pl.CostEstimate(flops=0, bytes_accessed=256 * 1024, transcendentals=0),
    )(keys, values, swapped)


def block_of(places_ref, k, i, n):
    y, x, core = places_ref[0], places_ref[1], places_ref[2]
    return jnp.where(core == 0, (y ^ k) * n + i, i * n + (x ^ k))


def chunk_kernel(places_ref, mine, other, *refs, places):
    outs, sems = refs[:-1], refs[-1]
    n = mine.shape[1] // outs[0].shape[1]
    rows, step = mine.shape[0], outs[0].shape[1] // n
    parts = [
        (out, i, pl.ds(pl.multiple_of(block_of(places_ref, k, i, n) * step, step), step))
        for k, out in zip(places, outs)
        for i in range(n)
    ]
    copies = [
        pltpu.make_async_copy(
            other.at[:, held], out.at[rows:, i * step : (i + 1) * step], sems.at[index]
        )
        for index, (out, i, held) in enumerate(parts)
    ]
    for copy in copies:
        copy.start()
    for out, i, held in parts:
        out[:rows, i * step : (i + 1) * step] = mine[:, held]
    for copy in copies:
        copy.wait()


def split_columns(places_ref, mine, other, chunks, places):
    rows, width = mine.shape
    return pl.pallas_call(
        functools.partial(chunk_kernel, places=places),
        out_shape=(whole((2 * rows, width // chunks)),) * len(places),
        in_specs=[SCALAR, pl.BlockSpec(), pl.BlockSpec(memory_space=pl.ANY)],
        scratch_shapes=[pltpu.SemaphoreType.DMA((chunks * len(places),))],
        compiler_params=pltpu.CompilerParams(vmem_limit_bytes=16 * MIB),
        cost_estimate=pl.CostEstimate(flops=0, bytes_accessed=6 * MIB, transcendentals=0),
    )(places_ref, mine, other)


def bias_kernel(here_ref, docs, out):
    z_lo, core = here_ref[0], here_ref[1]
    rows = out.shape[1] // 2
    chip = 2 * rows
    shape = (rows, rows)
    down = lax.broadcasted_iota(jnp.int32, shape, 0)
    along = lax.broadcasted_iota(jnp.int32, shape, 1)

    def place(distance, which):
        start = (z_lo - distance) * chip + (core ^ which) * rows
        held = pl.ds(pl.multiple_of(jnp.maximum(start, 0), rows), rows)
        return start, jnp.broadcast_to(docs[:, held].astype(jnp.float32), shape)

    queries = [place(0, which) for which in range(2)]
    for block in range(2 * (REACH + 1)):
        key_start, key_row = place(block // 2, block % 2)
        key_doc, key_pos = key_row.T, key_start + down
        for which, (query_start, query_doc) in enumerate(queries):
            allowed = (key_pos >= 0) & (key_pos <= query_start + along) & (key_doc == query_doc)
            out[block * rows : (block + 1) * rows, which * rows : (which + 1) * rows] = jnp.where(
                allowed, 0.0, MASKED
            )


def make_bias(here, docs, rows):
    return pl.pallas_call(
        bias_kernel,
        out_shape=whole((2 * rows * (REACH + 1), 2 * rows), jnp.float32),
        in_specs=[SCALAR, pl.BlockSpec()],
        compiler_params=SMALL,
        cost_estimate=pl.CostEstimate(flops=0, bytes_accessed=MIB, transcendentals=0),
    )(here, docs)


def attention_kernel(
    q_mine, do_mine, q_other, do_other, chip_pair, near_pair, far_pair, bias,
    near_grad, far_grad, score_grads, probs, dk_acc, dv_acc,
):
    pairs = jnp.concatenate([chip_pair[...], near_pair[...], far_pair[...]], axis=0)
    key, value = pairs[:, :DH], pairs[:, DH:]
    chip = chip_pair.shape[0]

    def load(head):
        cols = slice(head * DH, (head + 1) * DH)
        return (
            jnp.concatenate([q_mine[:, cols], q_other[:, cols]], axis=0),
            jnp.concatenate([do_mine[:, cols], do_other[:, cols]], axis=0),
        )

    def products(head):
        query, grad = load(head)
        return dot_nt(key, query), dot_nt(value, grad)

    ahead = products(0)
    for head in range(GROUP):
        raw, prob_grad = ahead
        if head + 1 < GROUP:
            ahead = products(head + 1)
        score = raw * (SCALE * LOG2E) + bias[...]
        top = jnp.max(score, axis=0, keepdims=True)
        weight = jnp.exp2(score - top)
        inverse = 1.0 / jnp.sum(weight, axis=0, keepdims=True)
        prob = weight * inverse
        prob_half = prob.astype(jnp.bfloat16)
        delta = jnp.sum(prob_half.astype(jnp.float32) * prob_grad, axis=0, keepdims=True)
        score_grad = (prob * (prob_grad - delta) * SCALE).astype(jnp.bfloat16)
        score_grads[head] = score_grad
        probs[head] = prob_half[:chip]
        query, grad = load(head)
        dk = dot_nn(score_grad[chip:], query)
        dv = dot_nn(prob_half[chip:], grad)
        if head == 0:
            dk_acc[...] = dk
            dv_acc[...] = dv
        else:
            dk_acc[...] += dk
            dv_acc[...] += dv
    for out, start in ((near_grad, 0), (far_grad, chip)):
        out[:, :DH] = dk_acc[start : start + chip].astype(jnp.bfloat16)
        out[:, DH:] = dv_acc[start : start + chip].astype(jnp.bfloat16)


def attention(operands, bias):
    rows = operands[0].shape[0]
    chip = 2 * rows
    keys = chip * (REACH + 1)
    return pl.pallas_call(
        attention_kernel,
        out_shape=(
            whole((chip, 2 * DH)),
            whole((chip, 2 * DH)),
            whole((GROUP, keys, chip)),
            whole((GROUP, chip, chip)),
        ),
        scratch_shapes=[
            pltpu.VMEM((keys - chip, DH), jnp.float32),
            pltpu.VMEM((keys - chip, DH), jnp.float32),
        ],
        compiler_params=pltpu.CompilerParams(vmem_limit_bytes=24 * MIB),
        cost_estimate=pl.CostEstimate(
            flops=150 * keys * chip * DH * GROUP,
            bytes_accessed=4 * MIB,
            transcendentals=keys * chip * GROUP,
        ),
    )(*operands, bias)


def own_kernel(
    q_mine, do_mine, q_other, do_other, chip_pair, near_pair, far_pair, score_grads, probs,
    dq_mine, dq_other, own_grad,
):
    key_t = jnp.concatenate([ref[:, :DH] for ref in (chip_pair, near_pair, far_pair)], axis=0).T
    rows, chip = q_mine.shape[0], chip_pair.shape[0]
    for head in range(GROUP):
        cols = slice(head * DH, (head + 1) * DH)
        query = jnp.concatenate([q_mine[:, cols], q_other[:, cols]], axis=0)
        grad = jnp.concatenate([do_mine[:, cols], do_other[:, cols]], axis=0)
        dq = dot_nn(key_t, score_grads[head]).T.astype(jnp.bfloat16)
        dq_mine[:, cols] = dq[:rows]
        dq_other[:, cols] = dq[rows:]
        dk = dot_nn(score_grads[head, :chip], query)
        dv = dot_nn(probs[head], grad)
        if head == 0:
            own_grad[:, :DH] = dk
            own_grad[:, DH:] = dv
        else:
            own_grad[:, :DH] += dk
            own_grad[:, DH:] += dv


def own_gradients(operands, score_grads, probs):
    rows = operands[0].shape[0]
    chip = 2 * rows
    return pl.pallas_call(
        own_kernel,
        out_shape=(
            whole((rows, GROUP * DH)),
            whole((rows, GROUP * DH)),
            whole((chip, 2 * DH), jnp.float32),
        ),
        compiler_params=pltpu.CompilerParams(vmem_limit_bytes=24 * MIB),
        cost_estimate=pl.CostEstimate(
            flops=6 * score_grads.size * DH, bytes_accessed=6 * MIB, transcendentals=0
        ),
    )(*operands, score_grads, probs)


def combine_kernel(own, near, far, out):
    total = own[...] + near[...].astype(jnp.float32) + far[...].astype(jnp.float32)
    out[...] = total.T.astype(jnp.bfloat16)


def combine(own, near, far):
    return pl.pallas_call(
        combine_kernel,
        out_shape=whole((own.shape[1], own.shape[0])),
        compiler_params=SMALL,
        cost_estimate=pl.CostEstimate(flops=0, bytes_accessed=MIB, transcendentals=0),
    )(own, near, far)


def assemble_kernel(here_ref, mine, other, out):
    width = mine.shape[1]
    core = here_ref[1]
    out[:, pl.ds(pl.multiple_of(core * width, width), width)] = mine[...]
    out[:, pl.ds(pl.multiple_of((1 - core) * width, width), width)] = other[...]


def assemble(here, mine, other):
    return pl.pallas_call(
        assemble_kernel,
        out_shape=whole((mine.shape[0], 2 * mine.shape[1])),
        in_specs=[SCALAR, pl.BlockSpec(), pl.BlockSpec()],
        compiler_params=SMALL,
        cost_estimate=pl.CostEstimate(flops=0, bytes_accessed=MIB, transcendentals=0),
    )(here, mine, other)


def project_kernel(places_ref, *refs, offset):
    n = len(refs) // 2
    pieces, grads, out = refs[:n], refs[n:-1], refs[-1]
    step = out.shape[0]
    place = jnp.where(places_ref[2] == 0, places_ref[1], places_ref[0]) ^ offset
    columns = pl.ds(pl.multiple_of(place * step, step), step)
    left = jnp.concatenate([ref[...] for ref in grads], axis=1)
    right = jnp.concatenate([ref[:, columns] for ref in pieces], axis=0)
    out[...] = dot_nn(left, right).T.astype(out.dtype)


def project(places, pieces, grads, offset, dtype):
    rows, columns = pieces[0].shape
    width = grads[0].shape[0]
    step = columns // len(pieces)
    return pl.pallas_call(
        functools.partial(project_kernel, offset=offset),
        out_shape=whole((step, width), dtype),
        in_specs=[SCALAR] + [pl.BlockSpec()] * (2 * len(pieces)),
        compiler_params=pltpu.CompilerParams(vmem_limit_bytes=16 * MIB),
        cost_estimate=pl.CostEstimate(
            flops=2 * len(pieces) * rows * step * width,
            bytes_accessed=2 * MIB,
            transcendentals=0,
        ),
    )(places, *pieces, *grads)


def add_kernel(*refs):
    total = refs[0][...]
    for ref in refs[1:-1]:
        total = total + ref[...].astype(jnp.float32)
    refs[-1][...] = total.astype(jnp.bfloat16)


def add_parts(own, parts):
    return pl.pallas_call(
        add_kernel,
        out_shape=whole(own.shape),
        compiler_params=SMALL,
        cost_estimate=pl.CostEstimate(flops=0, bytes_accessed=2 * MIB, transcendentals=0),
    )(own, *parts)


def final_kernel(parts, out):
    for head in range(KV):
        total = parts[head].astype(jnp.float32)
        for i in range(1, parts.shape[0] // KV):
            total = total + parts[KV * i + head].astype(jnp.float32)
        out[:, head * DH : (head + 1) * DH] = total[:, :DH]
        out[:, (KV + head) * DH : (KV + head + 1) * DH] = total[:, DH:]


def final_sum(parts):
    return pl.pallas_call(
        final_kernel,
        out_shape=whole((parts.shape[1], 2 * KV * DH), jnp.float32),
        compiler_params=SMALL,
        cost_estimate=pl.CostEstimate(flops=0, bytes_accessed=512 * 1024, transcendentals=0),
    )(parts)


def per_device(queries, keys, values, out_grad, layer_input, segment_ids):
    rows = queries.shape[1]
    chip = 2 * rows
    z_lo = lax.axis_index("z_lo")
    core = lax.axis_index("core")
    n_chips = lax.axis_size("z_lo")
    swap = [(0, 1), (1, 0)]
    here_ref = jnp.stack([z_lo, core]).astype(jnp.int32)
    places_ref = jnp.stack([lax.axis_index("y"), lax.axis_index("x"), core]).astype(jnp.int32)
    n_side = lax.axis_size("y")

    def cross(part, k, first):
        def pair(y, x, c):
            along_y = (c == 0) == first
            there = (y ^ k, x) if along_y else (y, x ^ k)
            return ((y * n_side + x) * 2 + c, (there[0] * n_side + there[1]) * 2 + c)

        pairs = [pair(y, x, c) for y in range(n_side) for x in range(n_side) for c in range(2)]
        return lax.ppermute(part, ("y", "x", "core"), pairs)


    def half_of(array, which):
        width = array.shape[-1] // 2
        return lax.dynamic_slice_in_dim(array[0], which * width, width, 1)

    k_mine, v_mine = half_of(keys, core), half_of(values, core)
    chip_pair = chip_pairs(
        k_mine,
        v_mine,
        lax.ppermute(
            jnp.concatenate([half_of(keys, 1 - core), half_of(values, 1 - core)], axis=1), "core", swap
        ),
    )
    q_mine, do_mine = half_of(queries, core), half_of(out_grad, core)
    q_out, do_out = half_of(queries, 1 - core), half_of(out_grad, 1 - core)
    q_out, do_out, _ = lax.optimization_barrier((q_out, do_out, chip_pair))
    q_other, do_other = (lax.ppermute(part, "core", swap) for part in (q_out, do_out))

    def behind(distance):
        return [
            (chip_at * 2 + c, (chip_at + distance) * 2 + c)
            for chip_at in range(n_chips - distance)
            for c in range(2)
        ]

    blocks = [chip_pair] + [
        lax.ppermute(chip_pair, ("z_lo", "core"), behind(distance)) for distance in (2, 1)
    ][::-1]

    own = (layer_input[0], lax.ppermute(layer_input[0], "core", swap))
    chunks = split_columns(places_ref, *own, n_side, range(1, n_side))
    chunks, _ = lax.optimization_barrier((chunks, (q_other, do_other)))
    pieces = [cross(chunk, k, True) for k, chunk in enumerate(chunks, 1)]
    docs, _ = lax.optimization_barrier((segment_ids, chunks[0]))

    operands = (q_mine, do_mine, q_other, do_other, *blocks)
    near_grad, far_grad, score_grads, probs = attention(
        operands, make_bias(here_ref, docs, rows)
    )
    dq_mine, dq_other, own_grad = own_gradients(operands, score_grads, probs)
    far_back, near_back = (
        lax.ppermute(part, ("z_lo", "core"), [(b, a) for a, b in behind(distance)])
        for distance, part in ((2, far_grad), (1, near_grad))
    )

    (own_piece,) = split_columns(places_ref, *own, n_side, (0,))
    far_back, own_piece = lax.optimization_barrier((far_back, own_piece))
    grad = combine(own_grad, near_back, far_back)
    late, pieces[0], dq_other = lax.optimization_barrier((grad, pieces[0], dq_other))
    grads = [grad] + [cross(late if k == 1 else grad, k, True) for k in range(1, n_side)]
    dq_back = lax.ppermute(dq_other, "core", swap)
    query_grad = assemble(here_ref, dq_mine, dq_back)[None]
    pieces, grads, query_grad = lax.optimization_barrier((pieces, grads, query_grad))
    pieces = [own_piece] + list(pieces)
    terms = [project(places_ref, pieces, grads, k, jnp.bfloat16) for k in (2, 1, 3)]
    parts = [cross(term, k, False) for term, k in zip(terms, (2, 1, 3))]
    own_term = project(places_ref, pieces, grads, 0, jnp.float32)
    term = add_parts(own_term, parts)
    rest = ("z_hi", "z_lo", "core")
    n_rest = lax.axis_size(rest)
    spread = lax.all_to_all(
        term.reshape(n_rest, term.shape[0] // n_rest, term.shape[1]), rest, 0, 0, tiled=True
    )
    return (query_grad, final_sum(spread))


def solution(mesh):
    axes = ("y", "x", "z_hi", "z_lo", "core")
    fine = Mesh(mesh.devices.reshape(4, 4, 2, 4, 2), axes)
    dp, ctx = axes[:3], axes[3:]
    return jax.shard_map(
        per_device,
        mesh=fine,
        in_specs=(P(dp, ctx, None),) * 5 + (P(dp, None),),
        out_specs=(P(dp, ctx, None), P(axes, None)),
        check_vma=False,
    )
```

```python
import functools

import jax
import jax.numpy as jnp
from jax import lax
from jax.experimental import pallas as pl
from jax.experimental.pallas import tpu as pltpu
from jax.sharding import Mesh, PartitionSpec as P

H = 16
KV = 2
DH = 128
GROUP = H // KV
SCALE = 1.0 / DH**0.5
LOG2E = 1.4426950408889634
REACH = 2
MASKED = -1e30
MIB = 1024 * 1024
SMALL = pltpu.CompilerParams(vmem_limit_bytes=4 * MIB)


def dot_nt(left, right):
    return lax.dot_general(
        left, right, (((1,), (1,)), ((), ())), preferred_element_type=jnp.float32
    )


def dot_nn(left, right):
    return jnp.dot(left, right, preferred_element_type=jnp.float32)


def whole(shape, dtype=jnp.bfloat16):
    return jax.ShapeDtypeStruct(shape, dtype)


SCALAR = pl.BlockSpec(memory_space=pltpu.SMEM)


def pair_kernel(keys, values, swapped, out):
    rows = keys.shape[0]
    out[:rows, :DH] = keys[...]
    out[:rows, DH:] = values[...]
    out[rows:] = swapped[...]


def chip_pairs(keys, values, swapped):
    return pl.pallas_call(
        pair_kernel,
        out_shape=whole((2 * keys.shape[0], 2 * DH)),
        compiler_params=SMALL,
        cost_estimate=pl.CostEstimate(flops=0, bytes_accessed=256 * 1024, transcendentals=0),
    )(keys, values, swapped)


def block_of(places_ref, k, i, n):
    y, x, core = places_ref[0], places_ref[1], places_ref[2]
    return jnp.where(core == 0, (y ^ k) * n + i, i * n + (x ^ k))


def chunk_kernel(places_ref, mine, other, *outs, places):
    n = mine.shape[1] // outs[0].shape[1]
    rows, step = mine.shape[0], outs[0].shape[1] // n
    for k, out in zip(places, outs):
        for i in range(n):
            held = pl.ds(pl.multiple_of(block_of(places_ref, k, i, n) * step, step), step)
            out[:rows, i * step : (i + 1) * step] = mine[:, held]
            out[rows:, i * step : (i + 1) * step] = other[:, held]


def split_columns(places_ref, mine, other, chunks, places):
    rows, width = mine.shape
    return pl.pallas_call(
        functools.partial(chunk_kernel, places=places),
        out_shape=(whole((2 * rows, width // chunks)),) * len(places),
        in_specs=[SCALAR, pl.BlockSpec(), pl.BlockSpec()],
        compiler_params=pltpu.CompilerParams(vmem_limit_bytes=16 * MIB),
        cost_estimate=pl.CostEstimate(flops=0, bytes_accessed=6 * MIB, transcendentals=0),
    )(places_ref, mine, other)


def bias_kernel(here_ref, docs, out):
    z_lo, core = here_ref[0], here_ref[1]
    rows = out.shape[1] // 2
    chip = 2 * rows
    shape = (rows, rows)
    down = lax.broadcasted_iota(jnp.int32, shape, 0)
    along = lax.broadcasted_iota(jnp.int32, shape, 1)

    def place(distance, which):
        start = (z_lo - distance) * chip + (core ^ which) * rows
        held = pl.ds(pl.multiple_of(jnp.maximum(start, 0), rows), rows)
        return start, jnp.broadcast_to(docs[:, held].astype(jnp.float32), shape)

    queries = [place(0, which) for which in range(2)]
    for block in range(2 * (REACH + 1)):
        key_start, key_row = place(block // 2, block % 2)
        key_doc, key_pos = key_row.T, key_start + down
        for which, (query_start, query_doc) in enumerate(queries):
            allowed = (key_pos >= 0) & (key_pos <= query_start + along) & (key_doc == query_doc)
            out[block * rows : (block + 1) * rows, which * rows : (which + 1) * rows] = jnp.where(
                allowed, 0.0, MASKED
            )


def make_bias(here, docs, rows):
    return pl.pallas_call(
        bias_kernel,
        out_shape=whole((2 * rows * (REACH + 1), 2 * rows), jnp.float32),
        in_specs=[SCALAR, pl.BlockSpec()],
        compiler_params=SMALL,
        cost_estimate=pl.CostEstimate(flops=0, bytes_accessed=MIB, transcendentals=0),
    )(here, docs)


def attention_kernel(
    q_mine, do_mine, q_other, do_other, chip_pair, near_pair, far_pair, bias,
    near_grad, far_grad, score_grads, probs, dk_acc, dv_acc,
):
    pairs = jnp.concatenate([chip_pair[...], near_pair[...], far_pair[...]], axis=0)
    key, value = pairs[:, :DH], pairs[:, DH:]
    chip = chip_pair.shape[0]

    def load(head):
        cols = slice(head * DH, (head + 1) * DH)
        return (
            jnp.concatenate([q_mine[:, cols], q_other[:, cols]], axis=0),
            jnp.concatenate([do_mine[:, cols], do_other[:, cols]], axis=0),
        )

    def products(head):
        query, grad = load(head)
        return dot_nt(key, query), dot_nt(value, grad)

    ahead = products(0)
    for head in range(GROUP):
        raw, prob_grad = ahead
        if head + 1 < GROUP:
            ahead = products(head + 1)
        score = raw * (SCALE * LOG2E) + bias[...]
        top = jnp.max(score, axis=0, keepdims=True)
        weight = jnp.exp2(score - top)
        inverse = 1.0 / jnp.sum(weight, axis=0, keepdims=True)
        prob = weight * inverse
        prob_half = prob.astype(jnp.bfloat16)
        delta = jnp.sum(prob_half.astype(jnp.float32) * prob_grad, axis=0, keepdims=True)
        score_grad = (prob * (prob_grad - delta) * SCALE).astype(jnp.bfloat16)
        score_grads[head] = score_grad
        probs[head] = prob_half[:chip]
        query, grad = load(head)
        dk = dot_nn(score_grad[chip:], query)
        dv = dot_nn(prob_half[chip:], grad)
        if head == 0:
            dk_acc[...] = dk
            dv_acc[...] = dv
        else:
            dk_acc[...] += dk
            dv_acc[...] += dv
    for out, start in ((near_grad, 0), (far_grad, chip)):
        out[:, :DH] = dk_acc[start : start + chip].astype(jnp.bfloat16)
        out[:, DH:] = dv_acc[start : start + chip].astype(jnp.bfloat16)


def attention(operands, bias):
    rows = operands[0].shape[0]
    chip = 2 * rows
    keys = chip * (REACH + 1)
    return pl.pallas_call(
        attention_kernel,
        out_shape=(
            whole((chip, 2 * DH)),
            whole((chip, 2 * DH)),
            whole((GROUP, keys, chip)),
            whole((GROUP, chip, chip)),
        ),
        scratch_shapes=[
            pltpu.VMEM((keys - chip, DH), jnp.float32),
            pltpu.VMEM((keys - chip, DH), jnp.float32),
        ],
        compiler_params=pltpu.CompilerParams(vmem_limit_bytes=24 * MIB),
        cost_estimate=pl.CostEstimate(
            flops=150 * keys * chip * DH * GROUP,
            bytes_accessed=4 * MIB,
            transcendentals=keys * chip * GROUP,
        ),
    )(*operands, bias)


def own_kernel(
    q_mine, do_mine, q_other, do_other, chip_pair, near_pair, far_pair, score_grads, probs,
    dq_mine, dq_other, own_grad,
):
    key_t = jnp.concatenate([ref[:, :DH] for ref in (chip_pair, near_pair, far_pair)], axis=0).T
    rows, chip = q_mine.shape[0], chip_pair.shape[0]
    for head in range(GROUP):
        cols = slice(head * DH, (head + 1) * DH)
        query = jnp.concatenate([q_mine[:, cols], q_other[:, cols]], axis=0)
        grad = jnp.concatenate([do_mine[:, cols], do_other[:, cols]], axis=0)
        dq = dot_nn(key_t, score_grads[head]).T.astype(jnp.bfloat16)
        dq_mine[:, cols] = dq[:rows]
        dq_other[:, cols] = dq[rows:]
        dk = dot_nn(score_grads[head, :chip], query)
        dv = dot_nn(probs[head], grad)
        if head == 0:
            own_grad[:, :DH] = dk
            own_grad[:, DH:] = dv
        else:
            own_grad[:, :DH] += dk
            own_grad[:, DH:] += dv


def own_gradients(operands, score_grads, probs):
    rows = operands[0].shape[0]
    chip = 2 * rows
    return pl.pallas_call(
        own_kernel,
        out_shape=(
            whole((rows, GROUP * DH)),
            whole((rows, GROUP * DH)),
            whole((chip, 2 * DH), jnp.float32),
        ),
        compiler_params=pltpu.CompilerParams(vmem_limit_bytes=24 * MIB),
        cost_estimate=pl.CostEstimate(
            flops=6 * score_grads.size * DH, bytes_accessed=6 * MIB, transcendentals=0
        ),
    )(*operands, score_grads, probs)


def combine_kernel(own, near, far, out):
    total = own[...] + near[...].astype(jnp.float32) + far[...].astype(jnp.float32)
    out[...] = total.T.astype(jnp.bfloat16)


def combine(own, near, far):
    return pl.pallas_call(
        combine_kernel,
        out_shape=whole((own.shape[1], own.shape[0])),
        compiler_params=SMALL,
        cost_estimate=pl.CostEstimate(flops=0, bytes_accessed=MIB, transcendentals=0),
    )(own, near, far)


def assemble_kernel(here_ref, mine, other, out):
    width = mine.shape[1]
    core = here_ref[1]
    out[:, pl.ds(pl.multiple_of(core * width, width), width)] = mine[...]
    out[:, pl.ds(pl.multiple_of((1 - core) * width, width), width)] = other[...]


def assemble(here, mine, other):
    return pl.pallas_call(
        assemble_kernel,
        out_shape=whole((mine.shape[0], 2 * mine.shape[1])),
        in_specs=[SCALAR, pl.BlockSpec(), pl.BlockSpec()],
        compiler_params=SMALL,
        cost_estimate=pl.CostEstimate(flops=0, bytes_accessed=MIB, transcendentals=0),
    )(here, mine, other)


def project_kernel(places_ref, *refs, offset):
    n = len(refs) // 2
    pieces, grads, out = refs[:n], refs[n:-1], refs[-1]
    step = out.shape[0]
    place = jnp.where(places_ref[2] == 0, places_ref[1], places_ref[0]) ^ offset
    columns = pl.ds(pl.multiple_of(place * step, step), step)
    left = jnp.concatenate([ref[...] for ref in grads], axis=1)
    right = jnp.concatenate([ref[:, columns] for ref in pieces], axis=0)
    out[...] = dot_nn(left, right).T.astype(out.dtype)


def project(places, pieces, grads, offset, dtype):
    rows, columns = pieces[0].shape
    width = grads[0].shape[0]
    step = columns // len(pieces)
    return pl.pallas_call(
        functools.partial(project_kernel, offset=offset),
        out_shape=whole((step, width), dtype),
        in_specs=[SCALAR] + [pl.BlockSpec()] * (2 * len(pieces)),
        compiler_params=pltpu.CompilerParams(vmem_limit_bytes=16 * MIB),
        cost_estimate=pl.CostEstimate(
            flops=2 * len(pieces) * rows * step * width,
            bytes_accessed=2 * MIB,
            transcendentals=0,
        ),
    )(places, *pieces, *grads)


def add_kernel(*refs):
    total = refs[0][...]
    for ref in refs[1:-1]:
        total = total + ref[...].astype(jnp.float32)
    refs[-1][...] = total.astype(jnp.bfloat16)


def add_parts(own, parts):
    return pl.pallas_call(
        add_kernel,
        out_shape=whole(own.shape),
        compiler_params=SMALL,
        cost_estimate=pl.CostEstimate(flops=0, bytes_accessed=2 * MIB, transcendentals=0),
    )(own, *parts)


def final_kernel(parts, out):
    for head in range(KV):
        total = parts[head].astype(jnp.float32)
        for i in range(1, parts.shape[0] // KV):
            total = total + parts[KV * i + head].astype(jnp.float32)
        out[:, head * DH : (head + 1) * DH] = total[:, :DH]
        out[:, (KV + head) * DH : (KV + head + 1) * DH] = total[:, DH:]


def final_sum(parts):
    return pl.pallas_call(
        final_kernel,
        out_shape=whole((parts.shape[1], 2 * KV * DH), jnp.float32),
        compiler_params=SMALL,
        cost_estimate=pl.CostEstimate(flops=0, bytes_accessed=512 * 1024, transcendentals=0),
    )(parts)


def per_device(queries, keys, values, out_grad, layer_input, segment_ids):
    rows = queries.shape[1]
    chip = 2 * rows
    z_lo = lax.axis_index("z_lo")
    core = lax.axis_index("core")
    n_chips = lax.axis_size("z_lo")
    swap = [(0, 1), (1, 0)]
    here_ref = jnp.stack([z_lo, core]).astype(jnp.int32)
    places_ref = jnp.stack([lax.axis_index("y"), lax.axis_index("x"), core]).astype(jnp.int32)
    n_side = lax.axis_size("y")

    def cross(part, k, first):
        def pair(y, x, c):
            along_y = (c == 0) == first
            there = (y ^ k, x) if along_y else (y, x ^ k)
            return ((y * n_side + x) * 2 + c, (there[0] * n_side + there[1]) * 2 + c)

        pairs = [pair(y, x, c) for y in range(n_side) for x in range(n_side) for c in range(2)]
        return lax.ppermute(part, ("y", "x", "core"), pairs)


    def half_of(array, which):
        width = array.shape[-1] // 2
        return lax.dynamic_slice_in_dim(array[0], which * width, width, 1)

    k_mine, v_mine = half_of(keys, core), half_of(values, core)
    swapped = lax.ppermute(
        jnp.concatenate([half_of(keys, 1 - core), half_of(values, 1 - core)], axis=1), "core", swap
    )
    q_mine, do_mine = half_of(queries, core), half_of(out_grad, core)
    q_out, do_out = half_of(queries, 1 - core), half_of(out_grad, 1 - core)
    swapped, q_out, do_out = lax.optimization_barrier((swapped, q_out, do_out))
    chip_pair = chip_pairs(k_mine, v_mine, swapped)
    columns, q_out, do_out, _ = lax.optimization_barrier((layer_input[0], q_out, do_out, chip_pair))
    q_other, do_other = (lax.ppermute(part, "core", swap) for part in (q_out, do_out))

    def behind(distance):
        return [
            (chip_at * 2 + c, (chip_at + distance) * 2 + c)
            for chip_at in range(n_chips - distance)
            for c in range(2)
        ]

    blocks = [chip_pair] + [
        lax.ppermute(chip_pair, ("z_lo", "core"), behind(distance)) for distance in (2, 1)
    ][::-1]

    own = (columns, lax.ppermute(columns, "core", swap))
    chunks = split_columns(places_ref, *own, n_side, range(1, n_side))
    chunks, _ = lax.optimization_barrier((chunks, (q_other, do_other)))
    pieces = [cross(chunk, k, True) for k, chunk in enumerate(chunks, 1)]
    docs, _ = lax.optimization_barrier((segment_ids, chunks[0]))

    operands = (q_mine, do_mine, q_other, do_other, *blocks)
    near_grad, far_grad, score_grads, probs = attention(
        operands, make_bias(here_ref, docs, rows)
    )
    dq_mine, dq_other, own_grad = own_gradients(operands, score_grads, probs)
    far_back, near_back = (
        lax.ppermute(part, ("z_lo", "core"), [(b, a) for a, b in behind(distance)])
        for distance, part in ((2, far_grad), (1, near_grad))
    )

    (own_piece,) = split_columns(places_ref, *own, n_side, (0,))
    far_back, own_piece = lax.optimization_barrier((far_back, own_piece))
    grad = combine(own_grad, near_back, far_back)
    late, pieces[0], dq_other = lax.optimization_barrier((grad, pieces[0], dq_other))
    grads = [grad] + [cross(late if k == 1 else grad, k, True) for k in range(1, n_side)]
    dq_back = lax.ppermute(dq_other, "core", swap)
    query_grad = assemble(here_ref, dq_mine, dq_back)[None]
    pieces, grads, query_grad = lax.optimization_barrier((pieces, grads, query_grad))
    pieces = [own_piece] + list(pieces)
    terms = [project(places_ref, pieces, grads, k, jnp.bfloat16) for k in (2, 1, 3)]
    parts = [cross(term, k, False) for term, k in zip(terms, (2, 1, 3))]
    own_term = project(places_ref, pieces, grads, 0, jnp.float32)
    term = add_parts(own_term, parts)
    rest = ("z_hi", "z_lo", "core")
    n_rest = lax.axis_size(rest)
    spread = lax.all_to_all(
        term.reshape(n_rest, term.shape[0] // n_rest, term.shape[1]), rest, 0, 0, tiled=True
    )
    return (query_grad, final_sum(spread))


def solution(mesh):
    axes = ("y", "x", "z_hi", "z_lo", "core")
    fine = Mesh(mesh.devices.reshape(4, 4, 2, 4, 2), axes)
    dp, ctx = axes[:3], axes[3:]
    return jax.shard_map(
        per_device,
        mesh=fine,
        in_specs=(P(dp, ctx, None),) * 5 + (P(dp, None),),
        out_specs=(P(dp, ctx, None), P(axes, None)),
        check_vma=False,
    )
```

```python
import functools

import jax
import jax.numpy as jnp
from jax import lax
from jax.experimental import pallas as pl
from jax.experimental.pallas import tpu as pltpu
from jax.sharding import Mesh, PartitionSpec as P

H = 16
KV = 2
DH = 128
GROUP = H // KV
SCALE = 1.0 / DH**0.5
LOG2E = 1.4426950408889634
REACH = 2
MASKED = -1e30
MIB = 1024 * 1024
SMALL = pltpu.CompilerParams(vmem_limit_bytes=4 * MIB)


def dot_nt(left, right):
    return lax.dot_general(
        left, right, (((1,), (1,)), ((), ())), preferred_element_type=jnp.float32
    )


def dot_nn(left, right):
    return jnp.dot(left, right, preferred_element_type=jnp.float32)


def whole(shape, dtype=jnp.bfloat16):
    return jax.ShapeDtypeStruct(shape, dtype)


SCALAR = pl.BlockSpec(memory_space=pltpu.SMEM)


def pair_kernel(keys, values, swapped, out):
    rows = keys.shape[0]
    out[:rows, :DH] = keys[...]
    out[:rows, DH:] = values[...]
    out[rows:] = swapped[...]


def chip_pairs(keys, values, swapped):
    return pl.pallas_call(
        pair_kernel,
        out_shape=whole((2 * keys.shape[0], 2 * DH)),
        compiler_params=SMALL,
        cost_estimate=pl.CostEstimate(flops=0, bytes_accessed=256 * 1024, transcendentals=0),
    )(keys, values, swapped)


def block_of(places_ref, k, i, n):
    y, x, core = places_ref[0], places_ref[1], places_ref[2]
    return jnp.where(core == 0, (y ^ k) * n + i, i * n + (x ^ k))


def chunk_kernel(places_ref, mine, other, *outs, places):
    n = mine.shape[1] // outs[0].shape[1]
    rows, step = mine.shape[0], outs[0].shape[1] // n
    for k, out in zip(places, outs):
        for i in range(n):
            held = pl.ds(pl.multiple_of(block_of(places_ref, k, i, n) * step, step), step)
            out[:rows, i * step : (i + 1) * step] = mine[:, held]
            out[rows:, i * step : (i + 1) * step] = other[:, held]


def split_columns(places_ref, mine, other, chunks, places):
    rows, width = mine.shape
    return pl.pallas_call(
        functools.partial(chunk_kernel, places=places),
        out_shape=(whole((2 * rows, width // chunks)),) * len(places),
        in_specs=[SCALAR, pl.BlockSpec(), pl.BlockSpec()],
        compiler_params=pltpu.CompilerParams(vmem_limit_bytes=16 * MIB),
        cost_estimate=pl.CostEstimate(flops=0, bytes_accessed=6 * MIB, transcendentals=0),
    )(places_ref, mine, other)


def bias_kernel(here_ref, docs, out):
    z_lo, core = here_ref[0], here_ref[1]
    rows = out.shape[1] // 2
    chip = 2 * rows
    shape = (rows, rows)
    down = lax.broadcasted_iota(jnp.int32, shape, 0)
    along = lax.broadcasted_iota(jnp.int32, shape, 1)

    def place(distance, which):
        start = (z_lo - distance) * chip + (core ^ which) * rows
        held = pl.ds(pl.multiple_of(jnp.maximum(start, 0), rows), rows)
        return start, jnp.broadcast_to(docs[:, held].astype(jnp.float32), shape)

    queries = [place(0, which) for which in range(2)]
    for block in range(2 * (REACH + 1)):
        key_start, key_row = place(block // 2, block % 2)
        key_doc, key_pos = key_row.T, key_start + down
        for which, (query_start, query_doc) in enumerate(queries):
            allowed = (key_pos >= 0) & (key_pos <= query_start + along) & (key_doc == query_doc)
            out[block * rows : (block + 1) * rows, which * rows : (which + 1) * rows] = jnp.where(
                allowed, 0.0, MASKED
            )


def make_bias(here, docs, rows):
    return pl.pallas_call(
        bias_kernel,
        out_shape=whole((2 * rows * (REACH + 1), 2 * rows), jnp.float32),
        in_specs=[SCALAR, pl.BlockSpec()],
        compiler_params=SMALL,
        cost_estimate=pl.CostEstimate(flops=0, bytes_accessed=MIB, transcendentals=0),
    )(here, docs)


def attention_kernel(
    q_mine, do_mine, q_other, do_other, chip_pair, near_pair, far_pair, bias,
    near_grad, far_grad, score_grads, probs, dk_acc, dv_acc,
):
    pairs = jnp.concatenate([chip_pair[...], near_pair[...], far_pair[...]], axis=0)
    key, value = pairs[:, :DH], pairs[:, DH:]
    chip = chip_pair.shape[0]

    def load(head):
        cols = slice(head * DH, (head + 1) * DH)
        return (
            jnp.concatenate([q_mine[:, cols], q_other[:, cols]], axis=0),
            jnp.concatenate([do_mine[:, cols], do_other[:, cols]], axis=0),
        )

    def products(head):
        query, grad = load(head)
        return dot_nt(key, query), dot_nt(value, grad)

    ahead = products(0)
    for head in range(GROUP):
        raw, prob_grad = ahead
        if head + 1 < GROUP:
            ahead = products(head + 1)
        score = raw * (SCALE * LOG2E) + bias[...]
        top = jnp.max(score, axis=0, keepdims=True)
        weight = jnp.exp2(score - top)
        inverse = 1.0 / jnp.sum(weight, axis=0, keepdims=True)
        prob = weight * inverse
        prob_half = prob.astype(jnp.bfloat16)
        delta = jnp.sum(prob_half.astype(jnp.float32) * prob_grad, axis=0, keepdims=True)
        score_grad = (prob * (prob_grad - delta) * SCALE).astype(jnp.bfloat16)
        score_grads[head] = score_grad
        probs[head] = prob_half[:chip]
        query, grad = load(head)
        dk = dot_nn(score_grad[chip:], query)
        dv = dot_nn(prob_half[chip:], grad)
        if head == 0:
            dk_acc[...] = dk
            dv_acc[...] = dv
        else:
            dk_acc[...] += dk
            dv_acc[...] += dv
    for out, start in ((near_grad, 0), (far_grad, chip)):
        out[:, :DH] = dk_acc[start : start + chip].astype(jnp.bfloat16)
        out[:, DH:] = dv_acc[start : start + chip].astype(jnp.bfloat16)


def attention(operands, bias):
    rows = operands[0].shape[0]
    chip = 2 * rows
    keys = chip * (REACH + 1)
    return pl.pallas_call(
        attention_kernel,
        out_shape=(
            whole((chip, 2 * DH)),
            whole((chip, 2 * DH)),
            whole((GROUP, keys, chip)),
            whole((GROUP, chip, chip)),
        ),
        scratch_shapes=[
            pltpu.VMEM((keys - chip, DH), jnp.float32),
            pltpu.VMEM((keys - chip, DH), jnp.float32),
        ],
        compiler_params=pltpu.CompilerParams(vmem_limit_bytes=24 * MIB),
        cost_estimate=pl.CostEstimate(
            flops=150 * keys * chip * DH * GROUP,
            bytes_accessed=4 * MIB,
            transcendentals=keys * chip * GROUP,
        ),
    )(*operands, bias)


def own_kernel(
    q_mine, do_mine, q_other, do_other, chip_pair, near_pair, far_pair, score_grads, probs,
    dq_mine, dq_other, own_grad,
):
    key_t = jnp.concatenate([ref[:, :DH] for ref in (chip_pair, near_pair, far_pair)], axis=0).T
    rows, chip = q_mine.shape[0], chip_pair.shape[0]
    for head in range(GROUP):
        cols = slice(head * DH, (head + 1) * DH)
        query = jnp.concatenate([q_mine[:, cols], q_other[:, cols]], axis=0)
        grad = jnp.concatenate([do_mine[:, cols], do_other[:, cols]], axis=0)
        dq = dot_nn(key_t, score_grads[head]).T.astype(jnp.bfloat16)
        dq_mine[:, cols] = dq[:rows]
        dq_other[:, cols] = dq[rows:]
        dk = dot_nn(score_grads[head, :chip], query)
        dv = dot_nn(probs[head], grad)
        if head == 0:
            own_grad[:, :DH] = dk
            own_grad[:, DH:] = dv
        else:
            own_grad[:, :DH] += dk
            own_grad[:, DH:] += dv


def own_gradients(operands, score_grads, probs):
    rows = operands[0].shape[0]
    chip = 2 * rows
    return pl.pallas_call(
        own_kernel,
        out_shape=(
            whole((rows, GROUP * DH)),
            whole((rows, GROUP * DH)),
            whole((chip, 2 * DH), jnp.float32),
        ),
        compiler_params=pltpu.CompilerParams(vmem_limit_bytes=24 * MIB),
        cost_estimate=pl.CostEstimate(
            flops=6 * score_grads.size * DH, bytes_accessed=6 * MIB, transcendentals=0
        ),
    )(*operands, score_grads, probs)


def combine_kernel(own, near, far, out):
    total = own[...] + near[...].astype(jnp.float32) + far[...].astype(jnp.float32)
    out[...] = total.T.astype(jnp.bfloat16)


def combine(own, near, far):
    return pl.pallas_call(
        combine_kernel,
        out_shape=whole((own.shape[1], own.shape[0])),
        compiler_params=SMALL,
        cost_estimate=pl.CostEstimate(flops=0, bytes_accessed=MIB, transcendentals=0),
    )(own, near, far)


def assemble_kernel(here_ref, mine, other, out):
    width = mine.shape[1]
    core = here_ref[1]
    out[:, pl.ds(pl.multiple_of(core * width, width), width)] = mine[...]
    out[:, pl.ds(pl.multiple_of((1 - core) * width, width), width)] = other[...]


def assemble(here, mine, other):
    return pl.pallas_call(
        assemble_kernel,
        out_shape=whole((mine.shape[0], 2 * mine.shape[1])),
        in_specs=[SCALAR, pl.BlockSpec(), pl.BlockSpec()],
        compiler_params=SMALL,
        cost_estimate=pl.CostEstimate(flops=0, bytes_accessed=MIB, transcendentals=0),
    )(here, mine, other)


def project_kernel(places_ref, *refs, offsets):
    n = (len(refs) - len(offsets)) // 2
    pieces, grads, outs = refs[:n], refs[n : 2 * n], refs[2 * n :]
    step = outs[0].shape[0]
    place = jnp.where(places_ref[2] == 0, places_ref[1], places_ref[0])
    left = jnp.concatenate([ref[...] for ref in grads], axis=1)
    for offset, out in zip(offsets, outs):
        columns = pl.ds(pl.multiple_of((place ^ offset) * step, step), step)
        right = jnp.concatenate([ref[:, columns] for ref in pieces], axis=0)
        out[...] = dot_nn(left, right).T.astype(out.dtype)


def project(places, pieces, grads, offsets, dtype):
    rows, columns = pieces[0].shape
    width = grads[0].shape[0]
    step = columns // len(pieces)
    return pl.pallas_call(
        functools.partial(project_kernel, offsets=offsets),
        out_shape=(whole((step, width), dtype),) * len(offsets),
        in_specs=[SCALAR] + [pl.BlockSpec()] * (2 * len(pieces)),
        compiler_params=pltpu.CompilerParams(vmem_limit_bytes=16 * MIB),
        cost_estimate=pl.CostEstimate(
            flops=2 * len(offsets) * len(pieces) * rows * step * width,
            bytes_accessed=2 * MIB * len(offsets),
            transcendentals=0,
        ),
    )(places, *pieces, *grads)


def add_kernel(*refs):
    total = refs[0][...]
    for ref in refs[1:-1]:
        total = total + ref[...].astype(jnp.float32)
    refs[-1][...] = total.astype(jnp.bfloat16)


def add_parts(own, parts):
    return pl.pallas_call(
        add_kernel,
        out_shape=whole(own.shape),
        compiler_params=SMALL,
        cost_estimate=pl.CostEstimate(flops=0, bytes_accessed=2 * MIB, transcendentals=0),
    )(own, *parts)


def final_kernel(parts, out):
    for head in range(KV):
        total = parts[head].astype(jnp.float32)
        for i in range(1, parts.shape[0] // KV):
            total = total + parts[KV * i + head].astype(jnp.float32)
        out[:, head * DH : (head + 1) * DH] = total[:, :DH]
        out[:, (KV + head) * DH : (KV + head + 1) * DH] = total[:, DH:]


def final_sum(parts):
    return pl.pallas_call(
        final_kernel,
        out_shape=whole((parts.shape[1], 2 * KV * DH), jnp.float32),
        compiler_params=SMALL,
        cost_estimate=pl.CostEstimate(flops=0, bytes_accessed=512 * 1024, transcendentals=0),
    )(parts)


def per_device(queries, keys, values, out_grad, layer_input, segment_ids):
    rows = queries.shape[1]
    chip = 2 * rows
    z_lo = lax.axis_index("z_lo")
    core = lax.axis_index("core")
    n_chips = lax.axis_size("z_lo")
    swap = [(0, 1), (1, 0)]
    here_ref = jnp.stack([z_lo, core]).astype(jnp.int32)
    places_ref = jnp.stack([lax.axis_index("y"), lax.axis_index("x"), core]).astype(jnp.int32)
    n_side = lax.axis_size("y")

    def cross(part, k, first):
        def pair(y, x, c):
            along_y = (c == 0) == first
            there = (y ^ k, x) if along_y else (y, x ^ k)
            return ((y * n_side + x) * 2 + c, (there[0] * n_side + there[1]) * 2 + c)

        pairs = [pair(y, x, c) for y in range(n_side) for x in range(n_side) for c in range(2)]
        return lax.ppermute(part, ("y", "x", "core"), pairs)


    def half_of(array, which):
        width = array.shape[-1] // 2
        return lax.dynamic_slice_in_dim(array[0], which * width, width, 1)

    k_mine, v_mine = half_of(keys, core), half_of(values, core)
    swapped = lax.ppermute(
        jnp.concatenate([half_of(keys, 1 - core), half_of(values, 1 - core)], axis=1), "core", swap
    )
    q_mine, do_mine = half_of(queries, core), half_of(out_grad, core)
    q_out, do_out = half_of(queries, 1 - core), half_of(out_grad, 1 - core)
    swapped, q_out, do_out = lax.optimization_barrier((swapped, q_out, do_out))
    chip_pair = chip_pairs(k_mine, v_mine, swapped)
    columns, q_out, do_out, _ = lax.optimization_barrier((layer_input[0], q_out, do_out, chip_pair))
    q_other, do_other = (lax.ppermute(part, "core", swap) for part in (q_out, do_out))

    def behind(distance):
        return [
            (chip_at * 2 + c, (chip_at + distance) * 2 + c)
            for chip_at in range(n_chips - distance)
            for c in range(2)
        ]

    blocks = [chip_pair] + [
        lax.ppermute(chip_pair, ("z_lo", "core"), behind(distance)) for distance in (2, 1)
    ][::-1]

    own = (columns, lax.ppermute(columns, "core", swap))
    chunks = split_columns(places_ref, *own, n_side, range(1, n_side))
    chunks, _ = lax.optimization_barrier((chunks, (q_other, do_other)))
    pieces = [cross(chunk, k, True) for k, chunk in enumerate(chunks, 1)]
    docs, _ = lax.optimization_barrier((segment_ids, chunks[0]))

    operands = (q_mine, do_mine, q_other, do_other, *blocks)
    near_grad, far_grad, score_grads, probs = attention(
        operands, make_bias(here_ref, docs, rows)
    )
    dq_mine, dq_other, own_grad = own_gradients(operands, score_grads, probs)
    far_back, near_back = (
        lax.ppermute(part, ("z_lo", "core"), [(b, a) for a, b in behind(distance)])
        for distance, part in ((2, far_grad), (1, near_grad))
    )

    (own_piece,) = split_columns(places_ref, *own, n_side, (0,))
    far_back, own_piece = lax.optimization_barrier((far_back, own_piece))
    grad = combine(own_grad, near_back, far_back)
    late, pieces[0], dq_other = lax.optimization_barrier((grad, pieces[0], dq_other))
    grads = [grad] + [cross(late if k == 1 else grad, k, True) for k in range(1, n_side)]
    dq_back = lax.ppermute(dq_other, "core", swap)
    query_grad = assemble(here_ref, dq_mine, dq_back)[None]
    pieces, grads, query_grad = lax.optimization_barrier((pieces, grads, query_grad))
    pieces = [own_piece] + list(pieces)
    terms = project(places_ref, pieces, grads, (2, 1, 3), jnp.bfloat16)
    parts = [cross(term, k, False) for term, k in zip(terms, (2, 1, 3))]
    (own_term,) = project(places_ref, pieces, grads, (0,), jnp.float32)
    term = add_parts(own_term, parts)
    rest = ("z_hi", "z_lo", "core")
    n_rest = lax.axis_size(rest)
    spread = lax.all_to_all(
        term.reshape(n_rest, term.shape[0] // n_rest, term.shape[1]), rest, 0, 0, tiled=True
    )
    return (query_grad, final_sum(spread))


def solution(mesh):
    axes = ("y", "x", "z_hi", "z_lo", "core")
    fine = Mesh(mesh.devices.reshape(4, 4, 2, 4, 2), axes)
    dp, ctx = axes[:3], axes[3:]
    return jax.shard_map(
        per_device,
        mesh=fine,
        in_specs=(P(dp, ctx, None),) * 5 + (P(dp, None),),
        out_specs=(P(dp, ctx, None), P(axes, None)),
        check_vma=False,
    )
```

```python
import functools

import jax
import jax.numpy as jnp
from jax import lax
from jax.experimental import pallas as pl
from jax.experimental.pallas import tpu as pltpu
from jax.sharding import Mesh, PartitionSpec as P

H = 16
KV = 2
DH = 128
GROUP = H // KV
SCALE = 1.0 / DH**0.5
LOG2E = 1.4426950408889634
REACH = 2
MASKED = -1e30
MIB = 1024 * 1024
SMALL = pltpu.CompilerParams(vmem_limit_bytes=4 * MIB)


def dot_nt(left, right):
    return lax.dot_general(
        left, right, (((1,), (1,)), ((), ())), preferred_element_type=jnp.float32
    )


def dot_nn(left, right):
    return jnp.dot(left, right, preferred_element_type=jnp.float32)


def whole(shape, dtype=jnp.bfloat16):
    return jax.ShapeDtypeStruct(shape, dtype)


SCALAR = pl.BlockSpec(memory_space=pltpu.SMEM)


def pair_kernel(keys, values, swapped, out):
    rows = keys.shape[0]
    out[:rows, :DH] = keys[...]
    out[:rows, DH:] = values[...]
    out[rows:] = swapped[...]


def chip_pairs(keys, values, swapped):
    return pl.pallas_call(
        pair_kernel,
        out_shape=whole((2 * keys.shape[0], 2 * DH)),
        compiler_params=SMALL,
        cost_estimate=pl.CostEstimate(flops=0, bytes_accessed=256 * 1024, transcendentals=0),
    )(keys, values, swapped)


def block_of(places_ref, k, i, n):
    y, x, core = places_ref[0], places_ref[1], places_ref[2]
    return jnp.where(core == 0, (y ^ k) * n + i, i * n + (x ^ k))


def chunk_kernel(places_ref, mine, other, *outs, places):
    n = mine.shape[1] // outs[0].shape[1]
    rows, step = mine.shape[0], outs[0].shape[1] // n
    for k, out in zip(places, outs):
        for i in range(n):
            held = pl.ds(pl.multiple_of(block_of(places_ref, k, i, n) * step, step), step)
            out[:rows, i * step : (i + 1) * step] = mine[:, held]
            out[rows:, i * step : (i + 1) * step] = other[:, held]


def split_columns(places_ref, mine, other, chunks, places):
    rows, width = mine.shape
    return pl.pallas_call(
        functools.partial(chunk_kernel, places=places),
        out_shape=(whole((2 * rows, width // chunks)),) * len(places),
        in_specs=[SCALAR, pl.BlockSpec(), pl.BlockSpec()],
        compiler_params=pltpu.CompilerParams(vmem_limit_bytes=16 * MIB),
        cost_estimate=pl.CostEstimate(flops=0, bytes_accessed=6 * MIB, transcendentals=0),
    )(places_ref, mine, other)


def bias_kernel(here_ref, docs, out):
    z_lo, core = here_ref[0], here_ref[1]
    rows = out.shape[1] // 2
    chip = 2 * rows
    shape = (rows, rows)
    down = lax.broadcasted_iota(jnp.int32, shape, 0)
    along = lax.broadcasted_iota(jnp.int32, shape, 1)

    def place(distance, which):
        start = (z_lo - distance) * chip + (core ^ which) * rows
        held = pl.ds(pl.multiple_of(jnp.maximum(start, 0), rows), rows)
        return start, jnp.broadcast_to(docs[:, held].astype(jnp.float32), shape)

    queries = [place(0, which) for which in range(2)]
    for block in range(2 * (REACH + 1)):
        key_start, key_row = place(block // 2, block % 2)
        key_doc, key_pos = key_row.T, key_start + down
        for which, (query_start, query_doc) in enumerate(queries):
            allowed = (key_pos >= 0) & (key_pos <= query_start + along) & (key_doc == query_doc)
            out[block * rows : (block + 1) * rows, which * rows : (which + 1) * rows] = jnp.where(
                allowed, 0.0, MASKED
            )


def make_bias(here, docs, rows):
    return pl.pallas_call(
        bias_kernel,
        out_shape=whole((2 * rows * (REACH + 1), 2 * rows), jnp.float32),
        in_specs=[SCALAR, pl.BlockSpec()],
        compiler_params=SMALL,
        cost_estimate=pl.CostEstimate(flops=0, bytes_accessed=MIB, transcendentals=0),
    )(here, docs)


def attention_kernel(
    q_mine, do_mine, q_other, do_other, chip_pair, near_pair, far_pair, bias,
    near_grad, far_grad, score_grads, probs, dk_acc, dv_acc,
):
    pairs = jnp.concatenate([chip_pair[...], near_pair[...], far_pair[...]], axis=0)
    key, value = pairs[:, :DH], pairs[:, DH:]
    chip = chip_pair.shape[0]

    def load(head):
        cols = slice(head * DH, (head + 1) * DH)
        return (
            jnp.concatenate([q_mine[:, cols], q_other[:, cols]], axis=0),
            jnp.concatenate([do_mine[:, cols], do_other[:, cols]], axis=0),
        )

    def products(head):
        query, grad = load(head)
        return dot_nt(key, query), dot_nt(value, grad)

    ahead = products(0)
    for head in range(GROUP):
        raw, prob_grad = ahead
        if head + 1 < GROUP:
            ahead = products(head + 1)
        score = raw * (SCALE * LOG2E) + bias[...]
        top = jnp.max(score, axis=0, keepdims=True)
        weight = jnp.exp2(score - top)
        inverse = 1.0 / jnp.sum(weight, axis=0, keepdims=True)
        prob = weight * inverse
        prob_half = prob.astype(jnp.bfloat16)
        delta = jnp.sum(prob_half.astype(jnp.float32) * prob_grad, axis=0, keepdims=True)
        score_grad = (prob * (prob_grad - delta) * SCALE).astype(jnp.bfloat16)
        score_grads[head] = score_grad
        probs[head] = prob_half[:chip]
        query, grad = load(head)
        dk = dot_nn(score_grad[chip:], query)
        dv = dot_nn(prob_half[chip:], grad)
        if head == 0:
            dk_acc[...] = dk
            dv_acc[...] = dv
        else:
            dk_acc[...] += dk
            dv_acc[...] += dv
    for out, start in ((near_grad, 0), (far_grad, chip)):
        out[:, :DH] = dk_acc[start : start + chip].astype(jnp.bfloat16)
        out[:, DH:] = dv_acc[start : start + chip].astype(jnp.bfloat16)


def attention(operands, bias):
    rows = operands[0].shape[0]
    chip = 2 * rows
    keys = chip * (REACH + 1)
    return pl.pallas_call(
        attention_kernel,
        out_shape=(
            whole((chip, 2 * DH)),
            whole((chip, 2 * DH)),
            whole((GROUP, keys, chip)),
            whole((GROUP, chip, chip)),
        ),
        scratch_shapes=[
            pltpu.VMEM((keys - chip, DH), jnp.float32),
            pltpu.VMEM((keys - chip, DH), jnp.float32),
        ],
        compiler_params=pltpu.CompilerParams(vmem_limit_bytes=24 * MIB),
        cost_estimate=pl.CostEstimate(
            flops=150 * keys * chip * DH * GROUP,
            bytes_accessed=4 * MIB,
            transcendentals=keys * chip * GROUP,
        ),
    )(*operands, bias)


def own_kernel(
    q_mine, do_mine, q_other, do_other, chip_pair, near_pair, far_pair, score_grads, probs,
    dq_mine, dq_other, own_grad,
):
    key_t = jnp.concatenate([ref[:, :DH] for ref in (chip_pair, near_pair, far_pair)], axis=0).T
    rows, chip = q_mine.shape[0], chip_pair.shape[0]
    for head in range(GROUP):
        cols = slice(head * DH, (head + 1) * DH)
        query = jnp.concatenate([q_mine[:, cols], q_other[:, cols]], axis=0)
        grad = jnp.concatenate([do_mine[:, cols], do_other[:, cols]], axis=0)
        dq = dot_nn(key_t, score_grads[head]).T.astype(jnp.bfloat16)
        dq_mine[:, cols] = dq[:rows]
        dq_other[:, cols] = dq[rows:]
        dk = dot_nn(score_grads[head, :chip], query)
        dv = dot_nn(probs[head], grad)
        if head == 0:
            own_grad[:, :DH] = dk
            own_grad[:, DH:] = dv
        else:
            own_grad[:, :DH] += dk
            own_grad[:, DH:] += dv


def own_gradients(operands, score_grads, probs):
    rows = operands[0].shape[0]
    chip = 2 * rows
    return pl.pallas_call(
        own_kernel,
        out_shape=(
            whole((rows, GROUP * DH)),
            whole((rows, GROUP * DH)),
            whole((chip, 2 * DH), jnp.float32),
        ),
        compiler_params=pltpu.CompilerParams(vmem_limit_bytes=24 * MIB),
        cost_estimate=pl.CostEstimate(
            flops=6 * score_grads.size * DH, bytes_accessed=6 * MIB, transcendentals=0
        ),
    )(*operands, score_grads, probs)


def combine_kernel(own, near, far, out):
    total = own[...] + near[...].astype(jnp.float32) + far[...].astype(jnp.float32)
    out[...] = total.T.astype(jnp.bfloat16)


def combine(own, near, far):
    return pl.pallas_call(
        combine_kernel,
        out_shape=whole((own.shape[1], own.shape[0])),
        compiler_params=SMALL,
        cost_estimate=pl.CostEstimate(flops=0, bytes_accessed=MIB, transcendentals=0),
    )(own, near, far)


def assemble_kernel(here_ref, mine, other, out):
    width = mine.shape[1]
    core = here_ref[1]
    out[:, pl.ds(pl.multiple_of(core * width, width), width)] = mine[...]
    out[:, pl.ds(pl.multiple_of((1 - core) * width, width), width)] = other[...]


def assemble(here, mine, other):
    return pl.pallas_call(
        assemble_kernel,
        out_shape=whole((mine.shape[0], 2 * mine.shape[1])),
        in_specs=[SCALAR, pl.BlockSpec(), pl.BlockSpec()],
        compiler_params=SMALL,
        cost_estimate=pl.CostEstimate(flops=0, bytes_accessed=MIB, transcendentals=0),
    )(here, mine, other)


def project_kernel(places_ref, *refs, offsets):
    n = (len(refs) - len(offsets)) // 2
    pieces, grads, outs = refs[:n], refs[n : 2 * n], refs[2 * n :]
    step = outs[0].shape[0]
    place = jnp.where(places_ref[2] == 0, places_ref[1], places_ref[0])
    left = jnp.concatenate([ref[...] for ref in grads], axis=1)
    for offset, out in zip(offsets, outs):
        columns = pl.ds(pl.multiple_of((place ^ offset) * step, step), step)
        right = jnp.concatenate([ref[:, columns] for ref in pieces], axis=0)
        out[...] = dot_nn(left, right).T.astype(out.dtype)


def project(places, pieces, grads, offsets, dtype):
    rows, columns = pieces[0].shape
    width = grads[0].shape[0]
    step = columns // len(pieces)
    return pl.pallas_call(
        functools.partial(project_kernel, offsets=offsets),
        out_shape=(whole((step, width), dtype),) * len(offsets),
        in_specs=[SCALAR] + [pl.BlockSpec()] * (2 * len(pieces)),
        compiler_params=pltpu.CompilerParams(vmem_limit_bytes=16 * MIB),
        cost_estimate=pl.CostEstimate(
            flops=2 * len(offsets) * len(pieces) * rows * step * width,
            bytes_accessed=2 * MIB * len(offsets),
            transcendentals=0,
        ),
    )(places, *pieces, *grads)


def add_kernel(*refs):
    total = refs[0][...]
    for ref in refs[1:-1]:
        total = total + ref[...].astype(jnp.float32)
    refs[-1][...] = total.astype(jnp.bfloat16)


def add_parts(own, parts):
    return pl.pallas_call(
        add_kernel,
        out_shape=whole(own.shape),
        compiler_params=SMALL,
        cost_estimate=pl.CostEstimate(flops=0, bytes_accessed=2 * MIB, transcendentals=0),
    )(own, *parts)


def final_kernel(parts, out):
    for head in range(KV):
        total = parts[head].astype(jnp.float32)
        for i in range(1, parts.shape[0] // KV):
            total = total + parts[KV * i + head].astype(jnp.float32)
        out[:, head * DH : (head + 1) * DH] = total[:, :DH]
        out[:, (KV + head) * DH : (KV + head + 1) * DH] = total[:, DH:]


def final_sum(parts):
    return pl.pallas_call(
        final_kernel,
        out_shape=whole((parts.shape[1], 2 * KV * DH), jnp.float32),
        compiler_params=SMALL,
        cost_estimate=pl.CostEstimate(flops=0, bytes_accessed=512 * 1024, transcendentals=0),
    )(parts)


def per_device(queries, keys, values, out_grad, layer_input, segment_ids):
    rows = queries.shape[1]
    chip = 2 * rows
    z_lo = lax.axis_index("z_lo")
    core = lax.axis_index("core")
    n_chips = lax.axis_size("z_lo")
    swap = [(0, 1), (1, 0)]
    here_ref = jnp.stack([z_lo, core]).astype(jnp.int32)
    places_ref = jnp.stack([lax.axis_index("y"), lax.axis_index("x"), core]).astype(jnp.int32)
    n_side = lax.axis_size("y")

    def cross(part, k, first):
        def pair(y, x, c):
            along_y = (c == 0) == first
            there = (y ^ k, x) if along_y else (y, x ^ k)
            return ((y * n_side + x) * 2 + c, (there[0] * n_side + there[1]) * 2 + c)

        pairs = [pair(y, x, c) for y in range(n_side) for x in range(n_side) for c in range(2)]
        return lax.ppermute(part, ("y", "x", "core"), pairs)


    def half_of(array, which):
        width = array.shape[-1] // 2
        return lax.dynamic_slice_in_dim(array[0], which * width, width, 1)

    k_mine, v_mine = half_of(keys, core), half_of(values, core)
    swapped = lax.ppermute(
        jnp.concatenate([half_of(keys, 1 - core), half_of(values, 1 - core)], axis=1), "core", swap
    )
    q_mine, do_mine = half_of(queries, core), half_of(out_grad, core)
    q_out, do_out = half_of(queries, 1 - core), half_of(out_grad, 1 - core)
    swapped, q_out, do_out = lax.optimization_barrier((swapped, q_out, do_out))
    chip_pair = chip_pairs(k_mine, v_mine, swapped)
    columns, q_out, do_out, _ = lax.optimization_barrier((layer_input[0], q_out, do_out, chip_pair))
    q_other, do_other = (lax.ppermute(part, "core", swap) for part in (q_out, do_out))

    def behind(distance):
        return [
            (chip_at * 2 + c, (chip_at + distance) * 2 + c)
            for chip_at in range(n_chips - distance)
            for c in range(2)
        ]

    blocks = [chip_pair] + [
        lax.ppermute(chip_pair, ("z_lo", "core"), behind(distance)) for distance in (2, 1)
    ][::-1]

    own = (columns, lax.ppermute(columns, "core", swap))
    chunks = split_columns(places_ref, *own, n_side, range(1, n_side))
    chunks, _ = lax.optimization_barrier((chunks, (q_other, do_other)))
    pieces = [cross(chunk, k, True) for k, chunk in enumerate(chunks, 1)]
    docs, _ = lax.optimization_barrier((segment_ids, chunks[0]))

    operands = (q_mine, do_mine, q_other, do_other, *blocks)
    near_grad, far_grad, score_grads, probs = attention(
        operands, make_bias(here_ref, docs, rows)
    )
    dq_mine, dq_other, own_grad = own_gradients(operands, score_grads, probs)
    far_back, near_back = (
        lax.ppermute(part, ("z_lo", "core"), [(b, a) for a, b in behind(distance)])
        for distance, part in ((2, far_grad), (1, near_grad))
    )

    (own_piece,) = split_columns(places_ref, *own, n_side, (0,))
    grad = combine(own_grad, near_back, far_back)
    late, pieces[0], dq_other = lax.optimization_barrier((grad, pieces[0], dq_other))
    grads = [grad] + [cross(late if k == 1 else grad, k, True) for k in range(1, n_side)]
    dq_back = lax.ppermute(dq_other, "core", swap)
    query_grad = assemble(here_ref, dq_mine, dq_back)[None]
    pieces, grads, query_grad, own_piece = lax.optimization_barrier(
        (pieces, grads, query_grad, own_piece)
    )
    pieces = [own_piece] + list(pieces)
    terms = project(places_ref, pieces, grads, (2, 1, 3), jnp.bfloat16)
    parts = [cross(term, k, False) for term, k in zip(terms, (2, 1, 3))]
    (own_term,) = project(places_ref, pieces, grads, (0,), jnp.float32)
    term = add_parts(own_term, parts)
    rest = ("z_hi", "z_lo", "core")
    n_rest = lax.axis_size(rest)
    spread = lax.all_to_all(
        term.reshape(n_rest, term.shape[0] // n_rest, term.shape[1]), rest, 0, 0, tiled=True
    )
    return (query_grad, final_sum(spread))


def solution(mesh):
    axes = ("y", "x", "z_hi", "z_lo", "core")
    fine = Mesh(mesh.devices.reshape(4, 4, 2, 4, 2), axes)
    dp, ctx = axes[:3], axes[3:]
    return jax.shard_map(
        per_device,
        mesh=fine,
        in_specs=(P(dp, ctx, None),) * 5 + (P(dp, None),),
        out_specs=(P(dp, ctx, None), P(axes, None)),
        check_vma=False,
    )
```

```python
import functools

import jax
import jax.numpy as jnp
from jax import lax
from jax.experimental import pallas as pl
from jax.experimental.pallas import tpu as pltpu
from jax.sharding import Mesh, PartitionSpec as P

H = 16
KV = 2
DH = 128
GROUP = H // KV
SCALE = 1.0 / DH**0.5
LOG2E = 1.4426950408889634
REACH = 2
MASKED = -1e30
MIB = 1024 * 1024
SMALL = pltpu.CompilerParams(vmem_limit_bytes=4 * MIB)


def dot_nt(left, right):
    return lax.dot_general(
        left, right, (((1,), (1,)), ((), ())), preferred_element_type=jnp.float32
    )


def dot_nn(left, right):
    return jnp.dot(left, right, preferred_element_type=jnp.float32)


def whole(shape, dtype=jnp.bfloat16):
    return jax.ShapeDtypeStruct(shape, dtype)


SCALAR = pl.BlockSpec(memory_space=pltpu.SMEM)


def pair_kernel(keys, values, swapped, out):
    rows = keys.shape[0]
    out[:rows, :DH] = keys[...]
    out[:rows, DH:] = values[...]
    out[rows:] = swapped[...]


def chip_pairs(keys, values, swapped):
    return pl.pallas_call(
        pair_kernel,
        out_shape=whole((2 * keys.shape[0], 2 * DH)),
        compiler_params=SMALL,
        cost_estimate=pl.CostEstimate(flops=0, bytes_accessed=256 * 1024, transcendentals=0),
    )(keys, values, swapped)


def block_of(places_ref, k, i, n):
    y, x, core = places_ref[0], places_ref[1], places_ref[2]
    return jnp.where(core == 0, (y ^ k) * n + i, i * n + (x ^ k))


def chunk_kernel(places_ref, mine, other, *outs, places):
    n = mine.shape[1] // outs[0].shape[1]
    rows, step = mine.shape[0], outs[0].shape[1] // n
    for k, out in zip(places, outs):
        for i in range(n):
            held = pl.ds(pl.multiple_of(block_of(places_ref, k, i, n) * step, step), step)
            out[:rows, i * step : (i + 1) * step] = mine[:, held]
            out[rows:, i * step : (i + 1) * step] = other[:, held]


def split_columns(places_ref, mine, other, chunks, places):
    rows, width = mine.shape
    return pl.pallas_call(
        functools.partial(chunk_kernel, places=places),
        out_shape=(whole((2 * rows, width // chunks)),) * len(places),
        in_specs=[SCALAR, pl.BlockSpec(), pl.BlockSpec()],
        compiler_params=pltpu.CompilerParams(vmem_limit_bytes=16 * MIB),
        cost_estimate=pl.CostEstimate(flops=0, bytes_accessed=6 * MIB, transcendentals=0),
    )(places_ref, mine, other)


def bias_kernel(here_ref, docs, out):
    z_lo, core = here_ref[0], here_ref[1]
    rows = out.shape[1] // 2
    chip = 2 * rows
    shape = (rows, rows)
    down = lax.broadcasted_iota(jnp.int32, shape, 0)
    along = lax.broadcasted_iota(jnp.int32, shape, 1)

    def place(distance, which):
        start = (z_lo - distance) * chip + (core ^ which) * rows
        held = pl.ds(pl.multiple_of(jnp.maximum(start, 0), rows), rows)
        return start, jnp.broadcast_to(docs[:, held].astype(jnp.float32), shape)

    queries = [place(0, which) for which in range(2)]
    for block in range(2 * (REACH + 1)):
        key_start, key_row = place(block // 2, block % 2)
        key_doc, key_pos = key_row.T, key_start + down
        for which, (query_start, query_doc) in enumerate(queries):
            allowed = (key_pos >= 0) & (key_pos <= query_start + along) & (key_doc == query_doc)
            out[block * rows : (block + 1) * rows, which * rows : (which + 1) * rows] = jnp.where(
                allowed, 0.0, MASKED
            )


def make_bias(here, docs, rows):
    return pl.pallas_call(
        bias_kernel,
        out_shape=whole((2 * rows * (REACH + 1), 2 * rows), jnp.float32),
        in_specs=[SCALAR, pl.BlockSpec()],
        compiler_params=SMALL,
        cost_estimate=pl.CostEstimate(flops=0, bytes_accessed=MIB, transcendentals=0),
    )(here, docs)


def attention_kernel(
    q_mine, do_mine, q_other, do_other, chip_pair, near_pair, far_pair, bias,
    near_grad, far_grad, score_grads, probs, dk_acc, dv_acc,
):
    pairs = jnp.concatenate([chip_pair[...], near_pair[...], far_pair[...]], axis=0)
    key, value = pairs[:, :DH], pairs[:, DH:]
    chip = chip_pair.shape[0]

    def load(head):
        cols = slice(head * DH, (head + 1) * DH)
        return (
            jnp.concatenate([q_mine[:, cols], q_other[:, cols]], axis=0),
            jnp.concatenate([do_mine[:, cols], do_other[:, cols]], axis=0),
        )

    def products(head):
        query, grad = load(head)
        return dot_nt(key, query), dot_nt(value, grad)

    ahead = products(0)
    for head in range(GROUP):
        raw, prob_grad = ahead
        if head + 1 < GROUP:
            ahead = products(head + 1)
        score = raw * (SCALE * LOG2E) + bias[...]
        top = jnp.max(score, axis=0, keepdims=True)
        weight = jnp.exp2(score - top)
        inverse = 1.0 / jnp.sum(weight, axis=0, keepdims=True)
        prob = weight * inverse
        prob_half = prob.astype(jnp.bfloat16)
        delta = jnp.sum(prob_half.astype(jnp.float32) * prob_grad, axis=0, keepdims=True)
        score_grad = (prob * (prob_grad - delta) * SCALE).astype(jnp.bfloat16)
        score_grads[head] = score_grad
        probs[head] = prob_half[:chip]
        query, grad = load(head)
        dk = dot_nn(score_grad[chip:], query)
        dv = dot_nn(prob_half[chip:], grad)
        if head == 0:
            dk_acc[...] = dk
            dv_acc[...] = dv
        else:
            dk_acc[...] += dk
            dv_acc[...] += dv
    for out, start in ((near_grad, 0), (far_grad, chip)):
        out[:, :DH] = dk_acc[start : start + chip].astype(jnp.bfloat16)
        out[:, DH:] = dv_acc[start : start + chip].astype(jnp.bfloat16)


def attention(operands, bias):
    rows = operands[0].shape[0]
    chip = 2 * rows
    keys = chip * (REACH + 1)
    return pl.pallas_call(
        attention_kernel,
        out_shape=(
            whole((chip, 2 * DH)),
            whole((chip, 2 * DH)),
            whole((GROUP, keys, chip)),
            whole((GROUP, chip, chip)),
        ),
        scratch_shapes=[
            pltpu.VMEM((keys - chip, DH), jnp.float32),
            pltpu.VMEM((keys - chip, DH), jnp.float32),
        ],
        compiler_params=pltpu.CompilerParams(vmem_limit_bytes=24 * MIB),
        cost_estimate=pl.CostEstimate(
            flops=150 * keys * chip * DH * GROUP,
            bytes_accessed=4 * MIB,
            transcendentals=keys * chip * GROUP,
        ),
    )(*operands, bias)


def own_kernel(
    q_mine, do_mine, q_other, do_other, chip_pair, near_pair, far_pair, score_grads, probs,
    dq_mine, dq_other, own_grad,
):
    key_t = jnp.concatenate([ref[:, :DH] for ref in (chip_pair, near_pair, far_pair)], axis=0).T
    rows, chip = q_mine.shape[0], chip_pair.shape[0]
    for head in range(GROUP):
        cols = slice(head * DH, (head + 1) * DH)
        query = jnp.concatenate([q_mine[:, cols], q_other[:, cols]], axis=0)
        grad = jnp.concatenate([do_mine[:, cols], do_other[:, cols]], axis=0)
        dq = dot_nn(key_t, score_grads[head]).T.astype(jnp.bfloat16)
        dq_mine[:, cols] = dq[:rows]
        dq_other[:, cols] = dq[rows:]
        dk = dot_nn(score_grads[head, :chip], query)
        dv = dot_nn(probs[head], grad)
        if head == 0:
            own_grad[:, :DH] = dk
            own_grad[:, DH:] = dv
        else:
            own_grad[:, :DH] += dk
            own_grad[:, DH:] += dv


def own_gradients(operands, score_grads, probs):
    rows = operands[0].shape[0]
    chip = 2 * rows
    return pl.pallas_call(
        own_kernel,
        out_shape=(
            whole((rows, GROUP * DH)),
            whole((rows, GROUP * DH)),
            whole((chip, 2 * DH), jnp.float32),
        ),
        compiler_params=pltpu.CompilerParams(vmem_limit_bytes=24 * MIB),
        cost_estimate=pl.CostEstimate(
            flops=6 * score_grads.size * DH, bytes_accessed=6 * MIB, transcendentals=0
        ),
    )(*operands, score_grads, probs)


def combine_kernel(own, far, near, out):
    total = own[...] + near[...].astype(jnp.float32) + far[...].astype(jnp.float32)
    out[...] = total.T.astype(jnp.bfloat16)


def combine(own, far, near):
    return pl.pallas_call(
        combine_kernel,
        out_shape=whole((own.shape[1], own.shape[0])),
        compiler_params=SMALL,
        cost_estimate=pl.CostEstimate(flops=0, bytes_accessed=MIB, transcendentals=0),
    )(own, far, near)


def assemble_kernel(here_ref, mine, other, out):
    width = mine.shape[1]
    core = here_ref[1]
    out[:, pl.ds(pl.multiple_of(core * width, width), width)] = mine[...]
    out[:, pl.ds(pl.multiple_of((1 - core) * width, width), width)] = other[...]


def assemble(here, mine, other):
    return pl.pallas_call(
        assemble_kernel,
        out_shape=whole((mine.shape[0], 2 * mine.shape[1])),
        in_specs=[SCALAR, pl.BlockSpec(), pl.BlockSpec()],
        compiler_params=SMALL,
        cost_estimate=pl.CostEstimate(flops=0, bytes_accessed=MIB, transcendentals=0),
    )(here, mine, other)


def project_kernel(places_ref, *refs, offsets):
    n = (len(refs) - len(offsets)) // 2
    pieces, grads, outs = refs[:n], refs[n : 2 * n], refs[2 * n :]
    step = outs[0].shape[0]
    place = jnp.where(places_ref[2] == 0, places_ref[1], places_ref[0])
    left = jnp.concatenate([ref[...] for ref in grads], axis=1)
    for offset, out in zip(offsets, outs):
        columns = pl.ds(pl.multiple_of((place ^ offset) * step, step), step)
        right = jnp.concatenate([ref[:, columns] for ref in pieces], axis=0)
        out[...] = dot_nn(left, right).T.astype(out.dtype)


def project(places, pieces, grads, offsets, dtype):
    rows, columns = pieces[0].shape
    width = grads[0].shape[0]
    step = columns // len(pieces)
    return pl.pallas_call(
        functools.partial(project_kernel, offsets=offsets),
        out_shape=(whole((step, width), dtype),) * len(offsets),
        in_specs=[SCALAR] + [pl.BlockSpec()] * (2 * len(pieces)),
        compiler_params=pltpu.CompilerParams(vmem_limit_bytes=16 * MIB),
        cost_estimate=pl.CostEstimate(
            flops=2 * len(offsets) * len(pieces) * rows * step * width,
            bytes_accessed=2 * MIB * len(offsets),
            transcendentals=0,
        ),
    )(places, *pieces, *grads)


def add_kernel(*refs):
    total = refs[0][...]
    for ref in refs[1:-1]:
        total = total + ref[...].astype(jnp.float32)
    refs[-1][...] = total.astype(jnp.bfloat16)


def add_parts(own, parts):
    return pl.pallas_call(
        add_kernel,
        out_shape=whole(own.shape),
        compiler_params=SMALL,
        cost_estimate=pl.CostEstimate(flops=0, bytes_accessed=2 * MIB, transcendentals=0),
    )(own, *parts)


def final_kernel(parts, out):
    for head in range(KV):
        total = parts[head].astype(jnp.float32)
        for i in range(1, parts.shape[0] // KV):
            total = total + parts[KV * i + head].astype(jnp.float32)
        out[:, head * DH : (head + 1) * DH] = total[:, :DH]
        out[:, (KV + head) * DH : (KV + head + 1) * DH] = total[:, DH:]


def final_sum(parts):
    return pl.pallas_call(
        final_kernel,
        out_shape=whole((parts.shape[1], 2 * KV * DH), jnp.float32),
        compiler_params=SMALL,
        cost_estimate=pl.CostEstimate(flops=0, bytes_accessed=512 * 1024, transcendentals=0),
    )(parts)


def per_device(queries, keys, values, out_grad, layer_input, segment_ids):
    rows = queries.shape[1]
    chip = 2 * rows
    z_lo = lax.axis_index("z_lo")
    core = lax.axis_index("core")
    n_chips = lax.axis_size("z_lo")
    swap = [(0, 1), (1, 0)]
    here_ref = jnp.stack([z_lo, core]).astype(jnp.int32)
    places_ref = jnp.stack([lax.axis_index("y"), lax.axis_index("x"), core]).astype(jnp.int32)
    n_side = lax.axis_size("y")

    def cross(part, k, first):
        def pair(y, x, c):
            along_y = (c == 0) == first
            there = (y ^ k, x) if along_y else (y, x ^ k)
            return ((y * n_side + x) * 2 + c, (there[0] * n_side + there[1]) * 2 + c)

        pairs = [pair(y, x, c) for y in range(n_side) for x in range(n_side) for c in range(2)]
        return lax.ppermute(part, ("y", "x", "core"), pairs)


    def half_of(array, which):
        width = array.shape[-1] // 2
        return lax.dynamic_slice_in_dim(array[0], which * width, width, 1)

    k_mine, v_mine = half_of(keys, core), half_of(values, core)
    swapped = lax.ppermute(
        jnp.concatenate([half_of(keys, 1 - core), half_of(values, 1 - core)], axis=1), "core", swap
    )
    q_mine, do_mine = half_of(queries, core), half_of(out_grad, core)
    q_out, do_out = half_of(queries, 1 - core), half_of(out_grad, 1 - core)
    swapped, q_out, do_out = lax.optimization_barrier((swapped, q_out, do_out))
    chip_pair = chip_pairs(k_mine, v_mine, swapped)
    columns, q_out, do_out, _ = lax.optimization_barrier((layer_input[0], q_out, do_out, chip_pair))
    q_other, do_other = (lax.ppermute(part, "core", swap) for part in (q_out, do_out))

    def behind(distance):
        return [
            (chip_at * 2 + c, (chip_at + distance) * 2 + c)
            for chip_at in range(n_chips - distance)
            for c in range(2)
        ]

    blocks = [chip_pair] + [
        lax.ppermute(chip_pair, ("z_lo", "core"), behind(distance)) for distance in (2, 1)
    ][::-1]

    own = (columns, lax.ppermute(columns, "core", swap))
    chunks = split_columns(places_ref, *own, n_side, range(1, n_side))
    chunks, _ = lax.optimization_barrier((chunks, (q_other, do_other)))
    pieces = [cross(chunk, k, True) for k, chunk in enumerate(chunks, 1)]
    docs, _ = lax.optimization_barrier((segment_ids, chunks[0]))

    operands = (q_mine, do_mine, q_other, do_other, *blocks)
    near_grad, far_grad, score_grads, probs = attention(
        operands, make_bias(here_ref, docs, rows)
    )
    dq_mine, dq_other, own_grad = own_gradients(operands, score_grads, probs)
    near_back, far_back = (
        lax.ppermute(part, ("z_lo", "core"), [(b, a) for a, b in behind(distance)])
        for distance, part in ((1, near_grad), (2, far_grad))
    )

    (own_piece,) = split_columns(places_ref, *own, n_side, (0,))
    grad = combine(own_grad, far_back, near_back)
    late, pieces[0], dq_other = lax.optimization_barrier((grad, pieces[0], dq_other))
    grads = [grad] + [cross(late if k == 1 else grad, k, True) for k in range(1, n_side)]
    dq_back = lax.ppermute(dq_other, "core", swap)
    query_grad = assemble(here_ref, dq_mine, dq_back)[None]
    pieces, grads, query_grad, own_piece = lax.optimization_barrier(
        (pieces, grads, query_grad, own_piece)
    )
    pieces = [own_piece] + list(pieces)
    terms = project(places_ref, pieces, grads, (2, 1, 3), jnp.bfloat16)
    parts = [cross(term, k, False) for term, k in zip(terms, (2, 1, 3))]
    (own_term,) = project(places_ref, pieces, grads, (0,), jnp.float32)
    term = add_parts(own_term, parts)
    rest = ("z_hi", "z_lo", "core")
    n_rest = lax.axis_size(rest)
    spread = lax.all_to_all(
        term.reshape(n_rest, term.shape[0] // n_rest, term.shape[1]), rest, 0, 0, tiled=True
    )
    return (query_grad, final_sum(spread))


def solution(mesh):
    axes = ("y", "x", "z_hi", "z_lo", "core")
    fine = Mesh(mesh.devices.reshape(4, 4, 2, 4, 2), axes)
    dp, ctx = axes[:3], axes[3:]
    return jax.shard_map(
        per_device,
        mesh=fine,
        in_specs=(P(dp, ctx, None),) * 5 + (P(dp, None),),
        out_specs=(P(dp, ctx, None), P(axes, None)),
        check_vma=False,
    )
```
